128 devices in a mesh: tx: 4 (over x), ty: 16 (over y, z), mem: 2 (over core).
Axes of the slice: x: 4, y: 4, z: 4, core: 2. Of those that a mesh axis runs over, the one named last changes fastest.
Arguments:
- volume: bfloat16 [64, 40, 192, 128], P(('tx', 'ty'), 'mem'), may hold values from -15 to 15
- super_matrix: bfloat16 [64, 192, 128, 128], P(('tx', 'ty')), may hold values from -0.5 to 0.5
- observed: bfloat16 [64, 24576], P(('tx', 'ty')), may hold values from -16 to 16
- error_var: float32 [64, 24576], P(('tx', 'ty')), may hold values from 24 to 384
- obs_cells: int32 [64, 24576], P(('tx', 'ty')), may hold values from 0 to 2047, as said below
- counts: int32 [64, 64], P(('tx', 'ty')), may hold values from 1 to 768, 24576 in all within a row
- state: bfloat16 [40, 8, 64, 2048], P('mem', None, 'tx', 'ty'), may hold values from -8 to 8
Outputs:
- analysis: bfloat16 [40, 8, 64, 2048], P('mem', None, 'tx', 'ty')
The draws below stay inside these ranges and needn't reach their ends.
Inputs may be any that keep to these rules, and one draw needn't show every extreme that they name: Each radar's counts over the tiles sum to 24576, and each radar's largest count is exactly 768. `obs_cells`: the cell is row-major inside the destination tile, 128 cells a row.
All inputs are finite; a program needn't handle non-finite values.
Results may differ from the reference program's by a relative error of at most 0.015.
Values may be sent and summed in bfloat16 or wider, within the bound.
A program may use at most 128 MiB of HBM per device.

```python
import math
import jax
import jax.numpy as jnp
import numpy as np
from jax import lax

K = 40
L = 8
CX = 16
CY = 128
B = 8
LOC = 16
NS = 5
CAP = 768
GB = 128
SB = 128
NT = 64
QR = 24576
NB = 192
NX = 64
NY = 2048


def draw_volume(key, part):
    key = jax.random.fold_in(key, 37)
    key_noise, key_coef, key_modes = jax.random.split(key, 3)
    gate_noise = jnp.clip(jax.random.normal(key_noise, (NT, K, NB, GB), jnp.float32), -3.0, 3.0)
    member_coef = jnp.clip(jax.random.normal(key_coef, (K, 8), jnp.float32), -2.5, 2.5)
    gate_modes = jnp.clip(jax.random.normal(key_modes, (NT, 8, NB, GB), jnp.float32), -2.5, 2.5)
    mode_scale = 0.6 * 0.7 ** jnp.arange(8, dtype=jnp.float32)
    member_coef = member_coef * mode_scale[None, :]
    volume_field = gate_noise
    for mode_id in range(8):
        volume_field = volume_field + member_coef[None, :, mode_id, None, None] * gate_modes[:, mode_id][:, None]
    return volume_field.astype(jnp.bfloat16)


def draw_obs_cells(key, part):
    key = jax.random.fold_in(key, 11)
    key_cx, key_cy, key_dx, key_dy = jax.random.split(key, 4)
    centre_x = jax.random.randint(key_cx, (NT, NB, 1), 0, CX)
    centre_y = jax.random.randint(key_cy, (NT, NB, 1), 0, CY)
    shift_x = jax.random.randint(key_dx, (NT, NB, SB), -B, B + 1)
    shift_y = jax.random.randint(key_dy, (NT, NB, SB), -B, B + 1)
    pos_x = jnp.clip(centre_x + shift_x, 0, CX - 1)
    pos_y = jnp.clip(centre_y + shift_y, 0, CY - 1)
    cell_ids = (pos_x * CY + pos_y).reshape(NT, QR)
    cell_ids = cell_ids.at[:, 0].set(0).at[:, 1].set(CX * CY - 1)
    return cell_ids.astype(jnp.int32)


def draw_state(key, part):
    key = jax.random.fold_in(key, 23)
    key_base, key_spread = jax.random.split(key)
    base_field = jnp.clip(jax.random.normal(key_base, (1, L, NX, NY), jnp.float32), -4.0, 4.0)
    spread_field = jnp.clip(jax.random.normal(key_spread, (K, L, NX, NY), jnp.float32), -4.0, 4.0)
    return (base_field + spread_field).astype(jnp.bfloat16)


def block_levels(own_key, shape, shards, low, largest):
    level, own = 1.0, jax.random.fold_in(own_key, 6)
    for dim, shards_of in shards:
        steps = jnp.exp(jax.random.uniform(jax.random.fold_in(own, dim), (shards_of,), jnp.float32, low / len(shards), largest / len(shards)))
        level = level * jnp.repeat(steps, shape[dim] // shards_of).reshape([-1 if axis == dim else 1 for axis in range(len(shape))])
    return level


def profile(amount, total, reach, lean):
    loads = [(1 << 20) // math.isqrt(rank ** lean) + 1 for rank in range(2, amount + 1)]
    surplus, holding = total - reach - (amount - 1), [1] * (amount - 1)
    while surplus > 0:
        free = [i for i in range(amount - 1) if holding[i] < reach]
        pool, left = sum([loads[i] for i in free]), surplus
        for i in free:
            addition = min(reach - holding[i], max(1, left * loads[i] // pool), surplus)
            holding[i] = holding[i] + addition
            surplus = surplus - addition
    return np.array([reach] + holding)


def ragged_sizes(stream_key, amount, total, reach, slope):
    if amount == 2:
        one = jax.random.randint(stream_key, (), max(1, total - reach), min(reach, total - 1) + 1)
        return jnp.stack([one, total - one])
    lengths = jnp.asarray(profile(amount, total, reach, slope), jnp.int32)
    pairs = (amount - 1) // 2
    donor, sink = lengths[1:1 + 2 * pairs:2], lengths[2:2 + 2 * pairs:2]
    margin = jnp.minimum(donor - 1, reach - sink)
    shifted = jax.random.randint(jax.random.fold_in(stream_key, 1), (pairs,), 0, 1 << 20) % (margin + 1)
    lengths = lengths.at[1:1 + 2 * pairs:2].set(donor - shifted).at[2:2 + 2 * pairs:2].set(sink + shifted)
    return lengths[jax.random.permutation(jax.random.fold_in(stream_key, 2), amount)]


def gaussian(key, shape, scale, bound, shards=(), kind=jnp.bfloat16):
    values = scale * jax.random.normal(key, shape, jnp.float32)
    if shards:
        values = values * block_levels(key, shape, shards, -0.22, 0.18)
    return jnp.clip(values, -bound, bound).astype(kind)


def setup_inputs(seed: int = 0) -> dict:
    streams_of = jax.random.split(jax.random.key(seed), 8)
    volume = draw_volume(jax.random.fold_in(streams_of[7], 71), 0)
    super_matrix = gaussian(streams_of[1], (NT, NB, GB, SB), GB ** -0.5, 0.5, ((0, 64),))
    observed = gaussian(streams_of[2], (NT, QR), 4.0, 16.0, ((0, 64),))
    error_var = jnp.clip(jnp.exp(math.log(384.0) - 2.7725887 * jax.random.uniform(streams_of[3], (NT, QR), jnp.float32) ** block_levels(streams_of[3], (NT, QR), ((0, 64),), -0.2, 0.2)), 24.0, 384.0)
    obs_cells = draw_obs_cells(jax.random.fold_in(streams_of[7], 71), 0)
    counts = jax.vmap(lambda own: ragged_sizes(own, NT, QR, CAP, 2))(jax.random.split(streams_of[5], NT)).reshape((NT, NT)).astype(jnp.int32)
    state = draw_state(jax.random.fold_in(streams_of[7], 71), 0)
    return dict(volume=volume, super_matrix=super_matrix, observed=observed, error_var=error_var, obs_cells=obs_cells, counts=counts, state=state)


exact = lax.Precision.HIGHEST

def settle(value):
    return lax.optimization_barrier(value.astype(jnp.bfloat16)).astype(jnp.float32)

def taper_table(cell_ids, width_x, width_y, spacing):
    pos_x = (cell_ids // width_y).astype(jnp.float32)
    pos_y = (cell_ids % width_y).astype(jnp.float32)
    nodes_x = width_x // spacing
    nodes_y = width_y // spacing
    centre_x = jnp.repeat(jnp.arange(nodes_x, dtype=jnp.float32) * spacing + (spacing - 1) * 0.5, nodes_y)
    centre_y = jnp.tile(jnp.arange(nodes_y, dtype=jnp.float32) * spacing + (spacing - 1) * 0.5, nodes_x)
    square = (pos_x[None, :] - centre_x[:, None]) ** 2 + (pos_y[None, :] - centre_y[:, None]) ** 2
    return jnp.exp(-square / (2.0 * LOC * LOC))

def tent_table(length, nodes, spacing):
    position = jnp.arange(length, dtype=jnp.float32)[:, None]
    centre = (jnp.arange(nodes, dtype=jnp.float32)[None, :] - 1.0) * spacing + (spacing - 1) * 0.5
    return jnp.maximum(0.0, 1.0 - jnp.abs(position - centre) / spacing)

def coarse_weights(gram, inform):
    members = inform.shape[1]
    identity = jnp.eye(members, dtype=jnp.float32)
    amat = identity + gram.reshape(-1, members, members) / (members - 1)
    scale = jnp.sqrt(lax.optimization_barrier(jnp.sum(amat * amat, axis=(1, 2))))[:, None, None]
    upper = amat / scale
    lower = jnp.broadcast_to(identity, amat.shape)
    for sweep in range(NS):
        middle = 1.5 * identity - 0.5 * jnp.einsum('cij,cjk->cik', lower, upper, precision=exact)
        upper = jnp.einsum('cij,cjk->cik', upper, middle, precision=exact)
        lower = jnp.einsum('cij,cjk->cik', middle, lower, precision=exact)
    inv_half = lower / jnp.sqrt(scale)
    step_one = jnp.einsum('cij,cj->ci', inv_half, inform, precision=exact)
    mean_shift = jnp.einsum('cij,cj->ci', inv_half, step_one, precision=exact) / (members - 1)
    shift = mean_shift - lax.optimization_barrier(jnp.mean(mean_shift, axis=1, keepdims=True))
    spread = inv_half - lax.optimization_barrier(jnp.mean(inv_half, axis=1, keepdims=True))
    trans = 1.0 / members + shift[:, :, None] + spread
    return trans.reshape(trans.shape[0], members * members)

def reference(volume, super_matrix, observed, error_var, obs_cells, counts, state):
    project = jnp.einsum('rkbg,rbgs->rkbs', volume.astype(jnp.float32), super_matrix.astype(jnp.float32))
    radar_obs = project.reshape(NT, K, QR).astype(jnp.bfloat16)
    inverse = (1.0 / error_var).astype(jnp.bfloat16)
    offsets = jnp.cumsum(counts, axis=1) - counts
    slot_ids = jnp.arange(CAP, dtype=jnp.int32)
    nodes = CX // B * (CY // B)

    def one_tile(tile_id):
        begin_at = offsets[:, tile_id]
        amounts = counts[:, tile_id]
        used = slot_ids[None, :] < amounts[:, None]
        source_ids = jnp.where(used, begin_at[:, None] + slot_ids[None, :], 0).astype(jnp.int32)
        tile_obs = jnp.where(used[:, None, :], jnp.take_along_axis(radar_obs, source_ids[:, None, :], axis=2), 0.0).astype(jnp.bfloat16)
        tile_value = jnp.where(used, jnp.take_along_axis(observed, source_ids, axis=1), 0.0).astype(jnp.bfloat16)
        tile_inverse = jnp.where(used, jnp.take_along_axis(inverse, source_ids, axis=1), 0.0).astype(jnp.bfloat16)
        tile_cells = jnp.where(used, jnp.take_along_axis(obs_cells, source_ids, axis=1), 0).astype(jnp.int32)

        def accumulate(running, pieces):
            block_obs, block_value, block_inverse, block_cells = pieces
            gram, inform = running
            values = block_obs.astype(jnp.float32)
            ens_mean = lax.optimization_barrier(jnp.sum(values, axis=0)) / K
            anomaly = settle(values - ens_mean)
            innovation = block_value.astype(jnp.float32) - ens_mean
            taper = taper_table(block_cells, CX, CY, B)
            weight_in = block_inverse.astype(jnp.float32)
            weight = settle(taper * weight_in)
            weight_innov = settle(taper * weight_in * innovation)
            pairs = settle(anomaly[:, None, :] * anomaly[None, :, :]).reshape(K * K, -1)
            gram = gram + jnp.dot(weight, pairs.T, precision=exact, preferred_element_type=jnp.float32)
            inform = inform + jnp.dot(weight_innov, anomaly.T, precision=exact, preferred_element_type=jnp.float32)
            return ((gram, inform), None)
        start_sums = (jnp.zeros((nodes, K * K), jnp.float32), jnp.zeros((nodes, K), jnp.float32))
        sums = lax.scan(accumulate, start_sums, (tile_obs, tile_value, tile_inverse, tile_cells))[0]
        return coarse_weights(sums[0], sums[1])
    trans = lax.map(one_tile, jnp.arange(NT, dtype=jnp.int32))
    tiles_x = NX // CX
    tiles_y = NY // CY
    coarse = trans.reshape(tiles_x, tiles_y, CX // B, CY // B, K * K).transpose(0, 2, 1, 3, 4)
    coarse = coarse.reshape(tiles_x * (CX // B), tiles_y * (CY // B), K * K)
    padded = jnp.pad(coarse, ((1, 1), (1, 1), (0, 0)), mode='edge')
    flat = padded.reshape(padded.shape[0], -1)
    table_x = tent_table(NX, padded.shape[0], B)
    table_y = tent_table(NY, padded.shape[1], B)

    def one_band(band_id):
        rows = lax.dynamic_slice_in_dim(table_x, band_id * B, B, 0)
        along = jnp.dot(rows, flat, precision=exact, preferred_element_type=jnp.float32).reshape(B, padded.shape[1], K * K)
        fine_weights = jnp.einsum('yb,xbn->xyn', table_y, along, precision=exact)
        fine_weights = settle(fine_weights).reshape(B, NY, K, K)
        band = lax.dynamic_slice_in_dim(state, band_id * B, B, 2).astype(jnp.float32)
        return jnp.einsum('klxy,xykj->jlxy', band, fine_weights).astype(jnp.bfloat16)
    bands = lax.map(one_band, jnp.arange(NX // B, dtype=jnp.int32))
    return bands.transpose(1, 2, 0, 3, 4).reshape(K, L, NX, NY)
```

```python
import numpy as np
import jax
import jax.numpy as jnp
from jax import lax
from jax.experimental import pallas as pl
from jax.experimental.pallas import tpu as pltpu
from jax.sharding import PartitionSpec as P

B = 8
LOC = 16
NS = 5
STEP = 512
SUB = 128
CHUNKS = 16


def pair_list():
    pairs = []
    for low in range(5):
        for high in range(low, 5):
            for turn in range(5 if low == high else 8):
                pairs.append((low, high, turn))
    for low in range(5):
        pairs.append((low, -1, 0))
    return pairs


def gram_kernel(
    count_ref, volume_ref, matrix_hbm, value_ref, error_ref, cell_ref, out_ref,
    wide, matrix, lhs, rhs, total, offsets, sems,
):
    radar_blocks = matrix.shape[0]
    tiles = count_ref.shape[1]
    chunk = radar_blocks // CHUNKS
    steps = radar_blocks * SUB // STEP
    per_step = STEP // SUB
    rows = total.shape[1]

    def fetch(index):
        part = pl.ds(index * chunk, chunk)
        return pltpu.make_async_copy(matrix_hbm.at[part], matrix.at[part], sems.at[index])

    for index in range(CHUNKS):
        fetch(index).start()

    offsets[0] = 0

    def add_count(tile, running):
        running = running + count_ref[0, tile]
        offsets[tile + 1] = running
        return running

    everything = lax.fori_loop(0, tiles, add_count, jnp.int32(0))
    for extra in range(8):
        offsets[tiles + 1 + extra] = everything

    def widen(member, carry):
        start = pl.multiple_of(member * radar_blocks, 8)
        wide[pl.ds(start, radar_blocks), :] = volume_ref[member].astype(jnp.float32)
        return carry

    lax.fori_loop(0, volume_ref.shape[0], widen, 0)
    total[...] = jnp.zeros_like(total)
    lhs[...] = jnp.zeros_like(lhs)

    centre_y = lax.broadcasted_iota(jnp.int32, (16, STEP), 0).astype(jnp.float32) * B + (B - 1) / 2
    lane = lax.broadcasted_iota(jnp.int32, (1, STEP), 1)
    chosen = pair_list()
    half = len(chosen) // 2

    def one_step(step, group, products):
        base = pl.multiple_of(step * STEP, STEP)
        here = pl.ds(base, STEP)
        cells = cell_ref[:, here]
        pos_x = (cells >> 7).astype(jnp.float32)
        pos_y = (cells & 127).astype(jnp.float32)
        inverse = (1.0 / error_ref[:, here]).astype(jnp.bfloat16).astype(jnp.float32)
        near_y = jnp.exp((pos_y - centre_y) ** 2 * (-0.5 / LOC**2)) * inverse
        weight = []
        for i in range(2):
            near_x = jnp.exp((pos_x - (i * B + (B - 1) / 2)) ** 2 * (-0.5 / LOC**2))
            weight.append((near_x * near_y).astype(jnp.bfloat16).astype(jnp.float32))
        weight = jnp.concatenate(weight, axis=0)
        values = value_ref[:, here].astype(jnp.float32)
        for sub in range(per_step):
            block = step * per_step + sub
            gates = wide[pl.ds(block, 40, stride=radar_blocks), :].astype(jnp.bfloat16)
            obs = jnp.dot(gates, matrix[block], preferred_element_type=jnp.float32)
            obs = obs.astype(jnp.bfloat16).astype(jnp.float32)
            mean = jnp.sum(obs, axis=0, keepdims=True) * (1.0 / 40)
            anomaly = (obs - mean).astype(jnp.bfloat16).astype(jnp.float32)
            innovation = values[:, sub * SUB:(sub + 1) * SUB] - mean
            part = [anomaly[8 * i:8 * i + 8] for i in range(5)]
            turned = {}
            made = []
            for low, high, turn in products:
                if high < 0:
                    made.append(part[low] * innovation)
                    continue
                if (high, turn) not in turned:
                    turned[high, turn] = part[high] if turn == 0 else pltpu.roll(part[high], turn, 0)
                made.append(part[low] * turned[high, turn])
            lanes = slice(sub * SUB, (sub + 1) * SUB)
            for index in range(0, len(made), 2):
                both = jnp.concatenate(
                    [made[index], made[index + 1] if index + 1 < len(made) else jnp.zeros_like(made[0])], axis=0
                )
                lhs[index * 8:index * 8 + 16, lanes] = both.astype(jnp.bfloat16)

        slot = lane + base

        def window(group):
            for i in range(8):
                first = offsets[group * 4 + i]
                last = offsets[group * 4 + i + 1]
                inside = (slot >= first) & (slot < last)
                rhs[i * 32:i * 32 + 32, :] = jnp.where(inside, weight, 0.0).astype(jnp.bfloat16)
            added = lax.dot_general(
                lhs[...], rhs[...], (((1,), (1,)), ((), ())), preferred_element_type=jnp.float32
            )
            total[group] += added[:, :128]
            total[group + 1] += added[:, 128:]

        group = lax.while_loop(lambda g: offsets[g * 4 + 4] <= base, lambda g: g + 1, group)

        def more(g):
            return (g < tiles // 4) & (offsets[jnp.minimum(g, tiles // 4) * 4] < base + STEP)

        def do(g):
            window(g)
            return g + 2

        lax.while_loop(more, do, group)
        return group

    mem = lax.axis_index("mem")
    for core in range(2):
        products = chosen[core * half:core * half + half]

        @pl.when(mem == core)
        def _():
            def chunk_loop(index, group):
                fetch(index).wait()
                count = steps // CHUNKS
                for inner in range(count):
                    group = one_step(index * count + inner, group, products)
                return group

            lax.fori_loop(0, CHUNKS, chunk_loop, jnp.int32(0))

    for group in range(tiles // 4):
        out_ref[group] = total[group].astype(jnp.bfloat16)


def gram(counts, volume, matrix, values, errors, cells):
    blocks = matrix.shape[0]
    tiles = counts.shape[1]
    rows = 448
    return pl.pallas_call(
        gram_kernel,
        out_shape=jax.ShapeDtypeStruct((tiles // 4, rows, 128), jnp.bfloat16),
        in_specs=[
            pl.BlockSpec(memory_space=pltpu.SMEM),
            pl.BlockSpec(memory_space=pltpu.VMEM),
            pl.BlockSpec(memory_space=pl.ANY),
            pl.BlockSpec(memory_space=pltpu.VMEM),
            pl.BlockSpec(memory_space=pltpu.VMEM),
            pl.BlockSpec(memory_space=pltpu.VMEM),
        ],
        out_specs=pl.BlockSpec(memory_space=pltpu.VMEM),
        scratch_shapes=[
            pltpu.VMEM((40 * blocks, 128), jnp.float32),
            pltpu.VMEM((blocks, 128, 128), jnp.bfloat16),
            pltpu.VMEM((rows, STEP), jnp.bfloat16),
            pltpu.VMEM((256, STEP), jnp.bfloat16),
            pltpu.VMEM((tiles // 4 + 1, rows, 128), jnp.float32),
            pltpu.SMEM((tiles + 9,), jnp.int32),
            pltpu.SemaphoreType.DMA((CHUNKS,)),
        ],
        compiler_params=pltpu.CompilerParams(vmem_limit_bytes=56 * 1024 * 1024),
        name="gram",
    )(counts, volume, matrix, values, errors, cells)


def apply_kernel(points_ref, tent_x_ref, tent_y_ref, state_ref, out_ref, fine, flat, result):
    levels, width_x, width_y = state_ref.shape[1:]
    members = state_ref.shape[0]
    own = out_ref.shape[0]
    points = points_ref[...].astype(jnp.float32).T.astype(jnp.bfloat16)

    def widen(member, carry):
        start = pl.multiple_of(member * levels * width_x, 8)
        flat[pl.ds(start, levels * width_x), :] = (
            state_ref[member].astype(jnp.float32).reshape(levels * width_x, width_y)
        )
        return carry

    lax.fori_loop(0, members, widen, 0)
    for x in range(0, width_x, 2):
        tent = jnp.concatenate(
            [tent_x_ref[:, x + i:x + i + 1] * tent_y_ref[...] for i in range(2)], axis=1
        ).astype(jnp.bfloat16)
        made = jnp.dot(points, tent, preferred_element_type=jnp.float32)
        made = made.astype(jnp.bfloat16).astype(jnp.float32)
        fine[x] = made[:, :128]
        fine[x + 1] = made[:, 128:]

    def column(x, carry):
        def add(k4, sums):
            sums = list(sums)
            for i in range(4):
                k = k4 * 4 + i
                field = flat[pl.ds(k * (levels * width_x) + x, levels, stride=width_x), :]
                for j in range(own):
                    row = fine[x, pl.ds(k * 32 + j, 8, stride=0), :]
                    sums[j] = sums[j] + row * field
            return tuple(sums)

        zero = jnp.zeros((levels, width_y), jnp.float32)
        sums = lax.fori_loop(0, members // 4, add, (zero,) * own)
        for j in range(own):
            result[pl.ds(j * (levels * width_x) + x, levels, stride=width_x), :] = sums[j]
        return carry

    lax.fori_loop(0, width_x, column, 0)

    def narrow(j, carry):
        start = pl.multiple_of(j * levels * width_x, 8)
        out_ref[j] = (
            result[pl.ds(start, levels * width_x), :]
            .reshape(levels, width_x, width_y)
            .astype(jnp.bfloat16)
        )
        return carry

    lax.fori_loop(0, own, narrow, 0)


def apply(points, tent_x, tent_y, state):
    members, levels, width_x, width_y = state.shape
    own = members // 2
    return pl.pallas_call(
        apply_kernel,
        out_shape=jax.ShapeDtypeStruct((own, levels, width_x, width_y), jnp.bfloat16),
        in_specs=[pl.BlockSpec(memory_space=pltpu.VMEM)] * 4,
        out_specs=pl.BlockSpec(memory_space=pltpu.VMEM),
        scratch_shapes=[
            pltpu.VMEM((width_x, points.shape[1], width_y), jnp.float32),
            pltpu.VMEM((members * levels * width_x, width_y), jnp.float32),
            pltpu.VMEM((own * levels * width_x, width_y), jnp.float32),
        ],
        compiler_params=pltpu.CompilerParams(vmem_limit_bytes=48 * 1024 * 1024),
        name="apply",
    )(points, tent_x, tent_y, state)


exact = lax.Precision.HIGHEST


def padded_2(block, sides, width):
    for axis, dim in sides:
        count = lax.axis_size(axis)
        forward = [(i, i + 1) for i in range(count - 1)]
        backward = [(target, source) for source, target in forward]
        low = lax.ppermute(
            lax.slice_in_dim(block, block.shape[dim] - width, None, axis=dim), axis, forward
        )
        high = lax.ppermute(lax.slice_in_dim(block, 0, width, axis=dim), axis, backward)
        block = jnp.concatenate([low, block, high], axis=dim)
    return block


def tent_table(length, nodes, spacing):
    position = jnp.arange(length, dtype=jnp.float32)[:, None]
    centre = (jnp.arange(nodes, dtype=jnp.float32)[None, :] - 1.0) * spacing + (spacing - 1) * 0.5
    return jnp.maximum(0.0, 1.0 - jnp.abs(position - centre) / spacing)


def coarse_weights(gram, inform):
    members = inform.shape[1]
    identity = jnp.eye(members, dtype=jnp.float32)
    amat = identity + gram.reshape(-1, members, members) / (members - 1)
    scale = jnp.sqrt(jnp.sum(amat * amat, axis=(1, 2)))[:, None, None]
    upper = amat / scale
    lower = jnp.broadcast_to(identity, amat.shape)
    for sweep in range(NS):
        middle = 1.5 * identity - 0.5 * jnp.einsum("cij,cjk->cik", lower, upper, precision=exact)
        upper = jnp.einsum("cij,cjk->cik", upper, middle, precision=exact)
        lower = jnp.einsum("cij,cjk->cik", middle, lower, precision=exact)
    inv_half = lower / jnp.sqrt(scale)
    step_one = jnp.einsum("cij,cj->ci", inv_half, inform, precision=exact)
    mean_shift = jnp.einsum("cij,cj->ci", inv_half, step_one, precision=exact) / (members - 1)
    shift = mean_shift - jnp.mean(mean_shift, axis=1, keepdims=True)
    spread = inv_half - jnp.mean(inv_half, axis=1, keepdims=True)
    trans = 1.0 / members + shift[:, :, None] + spread
    return trans.reshape(trans.shape[0], members * members)


def pair_table():
    table = np.zeros((880, 40, 40), np.float32)
    for index, (low, high, turn) in enumerate(pair_list()):
        if high < 0:
            continue
        for s in range(8):
            k, j = 8 * low + s, 8 * high + (s - turn) % 8
            if low == high and turn == 4 and s >= 4:
                continue
            table[index * 8 + s, k, j] = 1
            table[index * 8 + s, j, k] = 1
    return table.reshape(880, 1600).astype(jnp.bfloat16)


def per_device(volume, super_matrix, observed, error_var, obs_cells, counts, state):
    all_volume = lax.all_gather(volume[0], "mem", axis=0, tiled=True)
    all_state = lax.all_gather(state, "mem", axis=0, tiled=True)
    partial = gram(counts, all_volume, super_matrix[0], observed, error_var, obs_cells)
    by_tile = partial[:, :440].reshape(16, 440, 4, 32).transpose(0, 2, 1, 3).reshape(64, 440, 32)
    mine = lax.psum_scatter(by_tile, ("tx", "ty"), scatter_dimension=0, tiled=True)[0]
    rows = lax.all_gather(mine, "mem", axis=0, tiled=True)
    full = jnp.einsum("rc,rn->cn", rows, jnp.asarray(pair_table()), preferred_element_type=jnp.float32)
    inform = rows[840:].astype(jnp.float32).T
    trans = coarse_weights(full, inform).reshape(2, 16, 1600)
    padded = padded_2(trans.astype(jnp.bfloat16), (("tx", 0), ("ty", 1)), 1)
    index_tx, index_ty = lax.axis_index("tx"), lax.axis_index("ty")
    count_tx, count_ty = lax.axis_size("tx"), lax.axis_size("ty")
    padded = padded.at[0].set(jnp.where(index_tx == 0, padded[1], padded[0]))
    padded = padded.at[-1].set(jnp.where(index_tx == count_tx - 1, padded[-2], padded[-1]))
    padded = padded.at[:, 0].set(jnp.where(index_ty == 0, padded[:, 1], padded[:, 0]))
    padded = padded.at[:, -1].set(jnp.where(index_ty == count_ty - 1, padded[:, -2], padded[:, -1]))
    own = lax.dynamic_slice_in_dim(padded.reshape(72, 40, 40), lax.axis_index("mem") * 20, 20, 2)
    points = jnp.pad(own, ((0, 56), (0, 0), (0, 12))).reshape(128, 1280)
    tent_x = jnp.pad(jnp.repeat(tent_table(16, 4, B), 18, axis=1).T, ((0, 56), (0, 0)))
    tent_y = jnp.pad(jnp.tile(tent_table(128, 18, B), (1, 4)).T, ((0, 56), (0, 0)))
    return apply(points, tent_x, tent_y, all_state)


def solution(mesh):
    placed = (
        P(("tx", "ty"), "mem", None, None),
        P(("tx", "ty"), None, None, None),
        P(("tx", "ty"), None),
        P(("tx", "ty"), None),
        P(("tx", "ty"), None),
        P(("tx", "ty"), None),
        P("mem", None, "tx", "ty"),
    )
    return jax.shard_map(
        per_device,
        mesh=mesh,
        in_specs=placed,
        out_specs=P("mem", None, "tx", "ty"),
        check_vma=False,
    )
```

```python
import numpy as np
import jax
import jax.numpy as jnp
from jax import lax
from jax.experimental import pallas as pl
from jax.experimental.pallas import tpu as pltpu
from jax.sharding import PartitionSpec as P

B = 8
LOC = 16
NS = 5
STEP = 512
SUB = 128
CHUNKS = 16


def pair_list():
    pairs = []
    for low in range(5):
        for high in range(low, 5):
            for turn in range(5 if low == high else 8):
                pairs.append((low, high, turn))
    for low in range(5):
        pairs.append((low, -1, 0))
    return pairs


def gram_kernel(
    count_ref, volume_ref, other_ref, matrix_hbm, value_ref, error_ref, cell_ref, ab_ref, c_ref,
    wide, matrix, lhs, rhs, total, offsets, sems,
):
    radar_blocks = matrix.shape[0]
    tiles = count_ref.shape[1]
    chunk = radar_blocks // CHUNKS
    steps = radar_blocks * SUB // STEP
    per_step = STEP // SUB
    rows = total.shape[1]

    def fetch(index):
        part = pl.ds(index * chunk, chunk)
        return pltpu.make_async_copy(matrix_hbm.at[part], matrix.at[part], sems.at[index])

    for index in range(CHUNKS):
        fetch(index).start()

    offsets[0] = 0

    def add_count(tile, running):
        running = running + count_ref[0, tile]
        offsets[tile + 1] = running
        return running

    everything = lax.fori_loop(0, tiles, add_count, jnp.int32(0))
    for extra in range(8):
        offsets[tiles + 1 + extra] = everything

    mem = lax.axis_index("mem")
    held = volume_ref.shape[0]

    def widen(member, carry):
        start = pl.multiple_of((mem * held + member) * radar_blocks, 8)
        wide[pl.ds(start, radar_blocks), :] = volume_ref[member].astype(jnp.float32)
        start = pl.multiple_of(((1 - mem) * held + member) * radar_blocks, 8)
        wide[pl.ds(start, radar_blocks), :] = other_ref[member].astype(jnp.float32)
        return carry

    lax.fori_loop(0, held, widen, 0)
    total[...] = jnp.zeros_like(total)
    lhs[...] = jnp.zeros_like(lhs)

    centre_y = lax.broadcasted_iota(jnp.int32, (16, STEP), 0).astype(jnp.float32) * B + (B - 1) / 2
    lane = lax.broadcasted_iota(jnp.int32, (1, STEP), 1)
    chosen = pair_list()
    half = len(chosen) // 2

    def one_step(step, group, products):
        base = pl.multiple_of(step * STEP, STEP)
        here = pl.ds(base, STEP)
        cells = cell_ref[:, here]
        pos_x = (cells >> 7).astype(jnp.float32)
        pos_y = (cells & 127).astype(jnp.float32)
        inverse = (1.0 / error_ref[:, here]).astype(jnp.bfloat16).astype(jnp.float32)
        near_y = jnp.exp((pos_y - centre_y) ** 2 * (-0.5 / LOC**2)) * inverse
        weight = []
        for i in range(2):
            near_x = jnp.exp((pos_x - (i * B + (B - 1) / 2)) ** 2 * (-0.5 / LOC**2))
            weight.append((near_x * near_y).astype(jnp.bfloat16).astype(jnp.float32))
        weight = jnp.concatenate(weight, axis=0)
        values = value_ref[:, here].astype(jnp.float32)
        for sub in range(per_step):
            block = step * per_step + sub
            gates = wide[pl.ds(block, 40, stride=radar_blocks), :].astype(jnp.bfloat16)
            obs = jnp.dot(gates, matrix[block], preferred_element_type=jnp.float32)
            obs = obs.astype(jnp.bfloat16).astype(jnp.float32)
            mean = jnp.sum(obs, axis=0, keepdims=True) * (1.0 / 40)
            anomaly = (obs - mean).astype(jnp.bfloat16).astype(jnp.float32)
            innovation = values[:, sub * SUB:(sub + 1) * SUB] - mean
            part = [anomaly[8 * i:8 * i + 8] for i in range(5)]
            turned = {}
            made = []
            for low, high, turn in products:
                if high < 0:
                    made.append(part[low] * innovation)
                    continue
                if (high, turn) not in turned:
                    turned[high, turn] = part[high] if turn == 0 else pltpu.roll(part[high], turn, 0)
                made.append(part[low] * turned[high, turn])
            lanes = slice(sub * SUB, (sub + 1) * SUB)
            for index in range(0, len(made), 2):
                both = jnp.concatenate(
                    [made[index], made[index + 1] if index + 1 < len(made) else jnp.zeros_like(made[0])], axis=0
                )
                lhs[index * 8:index * 8 + 16, lanes] = both.astype(jnp.bfloat16)

        slot = lane + base

        def window(group):
            for i in range(8):
                first = offsets[group * 4 + i]
                last = offsets[group * 4 + i + 1]
                inside = (slot >= first) & (slot < last)
                rhs[i * 32:i * 32 + 32, :] = jnp.where(inside, weight, 0.0).astype(jnp.bfloat16)
            added = lax.dot_general(
                lhs[...], rhs[...], (((1,), (1,)), ((), ())), preferred_element_type=jnp.float32
            )
            total[group] += added[:, :128]
            total[group + 1] += added[:, 128:]

        group = lax.while_loop(lambda g: offsets[g * 4 + 4] <= base, lambda g: g + 1, group)

        def more(g):
            return (g < tiles // 4) & (offsets[jnp.minimum(g, tiles // 4) * 4] < base + STEP)

        def do(g):
            window(g)
            return g + 2

        lax.while_loop(more, do, group)
        return group

    for core in range(2):
        products = chosen[core * half:core * half + half]

        @pl.when(mem == core)
        def _():
            def chunk_loop(index, group):
                fetch(index).wait()
                count = steps // CHUNKS
                for inner in range(count):
                    group = one_step(index * count + inner, group, products)
                return group

            lax.fori_loop(0, CHUNKS, chunk_loop, jnp.int32(0))

    for x in range(4):
        for y in range(4):
            ab_ref[x, y] = total[x * 4 + y, :PART_A + PART_B].astype(jnp.bfloat16)
        for z, value in enumerate(block_swap([total[x * 4 + y, PART_A + PART_B:] for y in range(4)])):
            c_ref[z, x] = value.astype(jnp.bfloat16)


def gram(counts, volume, other, matrix, values, errors, cells):
    blocks = matrix.shape[0]
    tiles = counts.shape[1]
    rows = 448
    return pl.pallas_call(
        gram_kernel,
        out_shape=(
            jax.ShapeDtypeStruct((4, 4, PART_A + PART_B, 128), jnp.bfloat16),
            jax.ShapeDtypeStruct((4, 4, PART_C, 128), jnp.bfloat16),
        ),
        in_specs=[
            pl.BlockSpec(memory_space=pltpu.SMEM),
            pl.BlockSpec(memory_space=pltpu.VMEM),
            pl.BlockSpec(memory_space=pltpu.VMEM),
            pl.BlockSpec(memory_space=pl.ANY),
            pl.BlockSpec(memory_space=pltpu.VMEM),
            pl.BlockSpec(memory_space=pltpu.VMEM),
            pl.BlockSpec(memory_space=pltpu.VMEM),
        ],
        out_specs=(pl.BlockSpec(memory_space=pltpu.VMEM), pl.BlockSpec(memory_space=pltpu.VMEM)),
        scratch_shapes=[
            pltpu.VMEM((40 * blocks, 128), jnp.float32),
            pltpu.VMEM((blocks, 128, 128), jnp.bfloat16),
            pltpu.VMEM((rows, STEP), jnp.bfloat16),
            pltpu.VMEM((256, STEP), jnp.bfloat16),
            pltpu.VMEM((tiles // 4 + 1, rows, 128), jnp.float32),
            pltpu.SMEM((tiles + 9,), jnp.int32),
            pltpu.SemaphoreType.DMA((CHUNKS,)),
        ],
        compiler_params=pltpu.CompilerParams(vmem_limit_bytes=56 * 1024 * 1024),
        name="gram",
    )(counts, volume, other, matrix, values, errors, cells)


def apply_kernel(points_ref, tent_x_ref, tent_y_ref, state_ref, other_ref, out_ref, fine, flat, result):
    levels, width_x, width_y = state_ref.shape[1:]
    own = out_ref.shape[0]
    members = 2 * own
    mem, tx, ty = lax.axis_index("mem"), lax.axis_index("tx"), lax.axis_index("ty")
    kind_x = jnp.where(tx == 0, 0, jnp.where(tx == lax.axis_size("tx") - 1, 2, 1))
    kind_y = jnp.where(ty == 0, 0, jnp.where(ty == lax.axis_size("ty") - 1, 2, 1))
    tent_x, tent_y = tent_x_ref[kind_x], tent_y_ref[kind_y]
    points = points_ref[...].astype(jnp.float32)
    points = jnp.concatenate([points, jnp.zeros((48, points.shape[1]), jnp.float32)], axis=0).T
    points = points[:, :80].astype(jnp.bfloat16)

    def widen(member, carry):
        for source, first in ((state_ref, mem * own), (other_ref, (1 - mem) * own)):
            start = pl.multiple_of((first + member) * levels * width_x, 8)
            flat[pl.ds(start, levels * width_x), :] = (
                source[member].astype(jnp.float32).reshape(levels * width_x, width_y)
            )
        return carry

    lax.fori_loop(0, own, widen, 0)
    for x in range(0, width_x, 2):
        tent = jnp.concatenate(
            [tent_x[:, x + i:x + i + 1] * tent_y for i in range(2)], axis=1
        ).astype(jnp.bfloat16)
        made = jnp.dot(points, tent, preferred_element_type=jnp.float32)
        made = made.astype(jnp.bfloat16).astype(jnp.float32)
        fine[x] = made[:, :128]
        fine[x + 1] = made[:, 128:]

    def column(x, carry):
        def add(k4, sums):
            sums = list(sums)
            for i in range(4):
                k = k4 * 4 + i
                field = flat[pl.ds(k * (levels * width_x) + x, levels, stride=width_x), :]
                for j in range(own):
                    row = fine[x, pl.ds(k * 32 + j, 8, stride=0), :]
                    sums[j] = sums[j] + row * field
            return tuple(sums)

        zero = jnp.zeros((levels, width_y), jnp.float32)
        sums = lax.fori_loop(0, members // 4, add, (zero,) * own)
        for j in range(own):
            result[pl.ds(j * (levels * width_x) + x, levels, stride=width_x), :] = sums[j]
        return carry

    lax.fori_loop(0, width_x, column, 0)

    def narrow(j, carry):
        start = pl.multiple_of(j * levels * width_x, 8)
        out_ref[j] = (
            result[pl.ds(start, levels * width_x), :]
            .reshape(levels, width_x, width_y)
            .astype(jnp.bfloat16)
        )
        return carry

    lax.fori_loop(0, own, narrow, 0)


def apply(points, tent_x, tent_y, state, other):
    own, levels, width_x, width_y = state.shape
    members = 2 * own
    return pl.pallas_call(
        apply_kernel,
        out_shape=jax.ShapeDtypeStruct((own, levels, width_x, width_y), jnp.bfloat16),
        in_specs=[pl.BlockSpec(memory_space=pltpu.VMEM)] * 5,
        out_specs=pl.BlockSpec(memory_space=pltpu.VMEM),
        scratch_shapes=[
            pltpu.VMEM((width_x, points.shape[1], width_y), jnp.float32),
            pltpu.VMEM((members * levels * width_x, width_y), jnp.float32),
            pltpu.VMEM((own * levels * width_x, width_y), jnp.float32),
        ],
        compiler_params=pltpu.CompilerParams(vmem_limit_bytes=48 * 1024 * 1024),
        name="apply",
    )(points, tent_x, tent_y, state, other)


MESH = pl.DeviceIdType.MESH
PART_A, PART_B, PART_C = 160, 160, 128
GROUPS = 6
WIDE = 256
LINK_LANES = 1280


def place_of(row):
    if row < PART_A:
        return row % (PART_A // 4), row // (PART_A // 4)
    row -= PART_A
    if row < PART_B:
        return PART_A // 4 + row % (PART_B // 4), row // (PART_B // 4)
    row -= PART_B
    return (PART_A + PART_B) // 4 + row % (PART_C // 4), row // (PART_C // 4)


def pick_tables():
    rows = np.zeros((1648, WIDE), np.float32)
    quarters = np.zeros((1648, 128), np.float32)

    def put(target, product, s):
        core, local = divmod(product * 8 + s, 440)
        row, quarter = place_of(local)
        rows[target] = 0
        quarters[target] = 0
        rows[target, core * 112 + row] = 1
        quarters[target, quarter * 32:quarter * 32 + 32] = 1

    for product, (low, high, turn) in enumerate(pair_list()):
        for s in range(8):
            if high < 0:
                put(1600 + 8 * low + s, product, s)
                continue
            k, j = 8 * low + s, 8 * high + (s - turn) % 8
            put(j * 40 + k, product, s)
            put(k * 40 + j, product, s)
    return rows.astype(jnp.bfloat16), quarters


def lane_table():
    lanes = np.arange(WIDE)
    table = np.full((8, WIDE), -1, np.int32)
    table[0] = np.where(lanes < 240, lanes // 40, 7)
    table[1] = np.where(lanes < 240, lanes % 40, -1)
    return table


def block_swap(arrays):
    lane = lax.broadcasted_iota(jnp.int32, arrays[0].shape, 1)
    for step, mask in ((2, lane < 64), (1, (lane & 32) == 0)):
        turned = list(arrays)
        for low in range(4):
            if low & step:
                continue
            first, second = arrays[low], arrays[low + step]
            turned[low] = jnp.where(mask, first, pltpu.roll(second, 32 * step, 1))
            turned[low + step] = jnp.where(mask, pltpu.roll(first, 128 - 32 * step, 1), second)
        arrays = turned
    return arrays


def split(value):
    high = value.astype(jnp.bfloat16)
    return high, (value - high.astype(jnp.float32)).astype(jnp.bfloat16)


def bdot(left, right):
    return jnp.dot(left, right, preferred_element_type=jnp.float32)


def coarse_points(summed, pick_ref, quarter_ref, lane_ref, picked, spread_rows, rows, mem):
    lane_i, lane_j = lane_ref[0:1], lane_ref[1:2]
    high, low = split(summed)
    both = jnp.concatenate(
        [jnp.concatenate([high, low], axis=1).astype(jnp.float32), jnp.zeros((32, WIDE), jnp.float32)], axis=0
    ).astype(jnp.bfloat16)
    quarters = quarter_ref[...]
    found = bdot(pick_ref[...], both)
    picked[...] = jnp.concatenate(
        [found[:, :128] * quarters, found[:, 128:] * quarters], axis=1
    ).astype(jnp.bfloat16)
    row_c = lax.broadcasted_iota(jnp.int32, (WIDE, WIDE), 0) & 31
    eye = (lax.broadcasted_iota(jnp.int32, (40, WIDE), 0) == lane_j).astype(jnp.float32)
    real = lane_j >= 0
    same = (
        (jnp.concatenate(
            [jnp.full((40, WIDE), i, jnp.int32) for i in range(6)] + [jnp.full((16, WIDE), 9, jnp.int32)], axis=0
        ) == lane_i)
        .astype(jnp.float32)
        .astype(jnp.bfloat16)
    )

    def blocks(value):
        parts = [jnp.where(lane_i == i, value, 0.0) for i in range(6)] + [jnp.zeros((16, WIDE), jnp.float32)]
        return split(jnp.concatenate(parts, axis=0))

    def times(values, right):
        right_high, right_low = right
        highs, lows = zip(*[split(value) for value in values])
        count = len(values) * 40
        stack = jnp.concatenate([part.astype(jnp.float32) for part in highs + lows], axis=0).astype(jnp.bfloat16)
        main = bdot(stack, right_high)
        rest = bdot(stack[:count], right_low)
        return [
            main[40 * i:40 * i + 40] + (main[count + 40 * i:count + 40 * i + 40] + rest[40 * i:40 * i + 40])
            for i in range(len(values))
        ]

    uppers, lowers, scales, informs = [], [], [], []
    for group in range(GROUPS):
        expand = (row_c == lane_i + 6 * group).astype(jnp.float32) * real.astype(jnp.float32)
        spread_rows[...] = bdot(picked[...], expand.astype(jnp.bfloat16))
        gram = jnp.zeros((40, WIDE), jnp.float32)
        for j in range(40):
            gram = jnp.where(lane_j == j, spread_rows[40 * j:40 * j + 40], gram)
        informs.append(spread_rows[1600:1640])
        amat = eye + gram * (1.0 / 39)
        square = jnp.sum(amat * amat, axis=0, keepdims=True)
        first = square.astype(jnp.bfloat16).astype(jnp.float32)
        second = (square - first).astype(jnp.bfloat16).astype(jnp.float32)
        third = square - first - second
        parts = jnp.concatenate(
            [jnp.broadcast_to(part, (8, WIDE)) for part in (first, second, third, jnp.zeros_like(third))], axis=0
        )
        norm = bdot(parts.astype(jnp.bfloat16), same)
        norm = norm[0:1] + norm[8:9] + norm[16:17]
        scale = jnp.sqrt(jnp.where(real, norm, 1.0))
        scales.append(scale)
        uppers.append(amat / scale)
    for group in range(GROUPS):
        middle = 1.5 * eye - 0.5 * uppers[group]
        lowers.append(middle)
        uppers[group] = times([uppers[group]], blocks(middle))[0]
    for sweep in range(1, NS):
        middles = []
        for group in range(GROUPS):
            product = times([lowers[group]], blocks(uppers[group]))[0]
            middles.append(blocks(1.5 * eye - 0.5 * product))
        for group in range(GROUPS):
            if sweep < NS - 1:
                uppers[group], lowers[group] = times([uppers[group], lowers[group]], middles[group])
            else:
                lowers[group] = times([lowers[group]], middles[group])[0]
    target = lax.broadcasted_iota(jnp.int32, (WIDE, 768), 1)
    source = lax.broadcasted_iota(jnp.int32, (WIDE, 768), 0)
    own = target & 31
    wanted = (target >> 7) * 40 + mem * 20 + own
    choose = ((source == wanted) & (own < 20)).astype(jnp.float32).astype(jnp.bfloat16)
    for group in range(GROUPS):
        inv_half = lowers[group] / jnp.sqrt(scales[group])
        step_one = jnp.sum(inv_half * informs[group], axis=0, keepdims=True)
        product = inv_half * step_one
        high, low = split(product)
        stack = jnp.concatenate([high.astype(jnp.float32), low.astype(jnp.float32)], axis=0).astype(jnp.bfloat16)
        moved = bdot(stack, same)
        shift = (moved[:40] + moved[40:]) * (1.0 / 39)
        shift = shift - jnp.sum(shift, axis=0, keepdims=True) * (1.0 / 40)
        spread = inv_half - jnp.sum(inv_half, axis=0, keepdims=True) * (1.0 / 40)
        trans = (1.0 / 40 + shift + spread).astype(jnp.bfloat16)
        chosen = bdot(trans, choose)
        for i in range(6):
            point = group * 6 + i
            if point < 32:
                rows[point * 40:point * 40 + 40, :] = chosen[:, i * 128:i * 128 + 128]


def gather_members(rows, lane):
    quarter = lane >> 5
    pieces = []
    for q in range(10):
        piece = rows[pl.ds(4 * q, 32, stride=40), :]
        for p in range(1, 4):
            piece = jnp.where(quarter == p, rows[pl.ds(4 * q + p, 32, stride=40), :], piece)
        pieces.append(piece)
    return jnp.concatenate(pieces, axis=1)


def swap_kernel(volume_ref, other_ref, send, recv):
    mem = lax.axis_index("mem")
    mate = (lax.axis_index("tx"), lax.axis_index("ty"), 1 - mem)
    barrier = pltpu.get_barrier_semaphore()
    pl.semaphore_signal(barrier, inc=1, device_id=mate, device_id_type=MESH)
    pl.semaphore_wait(barrier, 1)
    count = send.shape[0]
    share = volume_ref.shape[0] // count
    copies = []
    for index in range(count):
        part = pl.ds(index * share, share)
        copies.append(
            pltpu.make_async_remote_copy(
                src_ref=volume_ref.at[part], dst_ref=other_ref.at[part], send_sem=send.at[index],
                recv_sem=recv.at[index], device_id=mate, device_id_type=MESH,
            )
        )
    for copy in copies:
        copy.start()
    for copy in copies:
        copy.wait()


def swap(volume):
    return pl.pallas_call(
        swap_kernel,
        out_shape=jax.ShapeDtypeStruct(volume.shape, volume.dtype),
        in_specs=[pl.BlockSpec(memory_space=pl.ANY)],
        out_specs=pl.BlockSpec(memory_space=pl.ANY),
        scratch_shapes=[pltpu.SemaphoreType.DMA((4,)), pltpu.SemaphoreType.DMA((4,))],
        compiler_params=pltpu.CompilerParams(collective_id=0, has_side_effects=True),
        name="swap",
    )(volume)


def coarse_kernel(
    ab_ref, c_ref, pick_ref, quarter_ref, lane_ref, state_ref, points_ref, other_ref,
    own_a, own_b, own_c, got_a, got_b, got_c, next_a, next_b, next_c, got_a2, got_b2, got_c2,
    last_a, last_b, last_c, got_a3, got_b3, got_c3, summed, picked, spread_rows, rows, edges, columns, halo,
    send, recv, local,
):
    x, ty, mem = lax.axis_index("tx"), lax.axis_index("ty"), lax.axis_index("mem")
    y, z = ty // 4, ty % 4
    mate = (x, ty, 1 - mem)

    def along(axis, turn):
        if axis == 0:
            return ((x + turn) % 4, ty, mem)
        if axis == 1:
            return (x, ((y + turn) % 4) * 4 + z, mem)
        return (x, y * 4 + (z + turn) % 4, mem)

    around = []
    for side, step in ((0, 1), (1, 15)):
        for turn in range(3):
            around.append((side, turn, ((x + 5 - turn) % 4, (ty + step) % 16, mem)))
    peers = [along(axis, turn) for axis in range(3) for turn in range(1, 4)] + [mate]
    peers += [along(0, 1), along(0, 3)] + [device for _, _, device in around]
    barrier = pltpu.get_barrier_semaphore()
    for device in peers:
        pl.semaphore_signal(barrier, inc=1, device_id=device, device_id_type=MESH)

    mine = [
        pltpu.make_async_copy(ab_ref.at[x, :, pl.ds(0, PART_A)], own_a, local.at[0]),
        pltpu.make_async_copy(ab_ref.at[:, y, pl.ds(PART_A, PART_B)], own_b, local.at[1]),
        pltpu.make_async_copy(c_ref.at[z], own_c, local.at[2]),
    ]
    for copy in mine:
        copy.start()
    pl.semaphore_wait(barrier, len(peers))

    def link(source, target, index, device):
        copy = pltpu.make_async_remote_copy(
            src_ref=source, dst_ref=target, send_sem=send.at[index], recv_sem=recv.at[index],
            device_id=device, device_id_type=MESH,
        )
        copy.start()
        return copy

    started = []

    def stage(number, axis, source, target):
        copies = []
        for turn in (2, 1, 3):
            place = ((x, y, z)[axis] + turn) % 4
            copies.append(link(source(place), target.at[turn - 1], number * 3 + turn - 1, along(axis, turn)))
        started.extend(copies)
        return copies

    first = [
        stage(0, 0, lambda place: ab_ref.at[place, :, pl.ds(0, PART_A)], got_a),
        stage(1, 1, lambda place: ab_ref.at[:, place, pl.ds(PART_A, PART_B)], got_b),
        stage(2, 2, lambda place: c_ref.at[place], got_c),
    ]
    state_copy = link(state_ref, other_ref, 27, mate)

    def wait_all(copies):
        for copy in copies:
            copy.wait_recv()

    def add_up(own, got, index):
        value = own[index].astype(jnp.float32)
        for turn in range(3):
            value = value + got[turn, index].astype(jnp.float32)
        return value

    def add_last(own, got):
        value = own.astype(jnp.float32)
        for turn in range(3):
            value = value + got[turn].astype(jnp.float32)
        return value

    mine[0].wait()
    wait_all(first[0])
    for index in range(4):
        next_a[index] = add_up(own_a, got_a, index).astype(jnp.bfloat16)
    second_a = stage(3, 1, lambda place: next_a.at[place], got_a2)
    mine[1].wait()
    wait_all(first[1])
    for index, value in enumerate(block_swap([add_up(own_b, got_b, index) for index in range(4)])):
        next_b[index] = value.astype(jnp.bfloat16)
    second_b = stage(4, 2, lambda place: next_b.at[place], got_b2)
    mine[2].wait()
    wait_all(first[2])
    for index in range(4):
        next_c[index] = add_up(own_c, got_c, index).astype(jnp.bfloat16)
    second_c = stage(5, 0, lambda place: next_c.at[place], got_c2)

    def quarter_rows(value, target):
        size = value.shape[0] // 4
        for index, part in enumerate(block_swap([value[i * size:(i + 1) * size] for i in range(4)])):
            target[index] = part

    wait_all(second_a)
    quarter_rows(add_last(next_a[y], got_a2), last_a)
    third_a = stage(6, 2, lambda place: last_a.at[place], got_a3)
    wait_all(second_b)
    quarter_rows(add_last(next_b[z], got_b2), last_b)
    third_b = stage(7, 0, lambda place: last_b.at[place], got_b3)
    wait_all(second_c)
    quarter_rows(add_last(next_c[x], got_c2), last_c)
    third_c = stage(8, 1, lambda place: last_c.at[place], got_c3)

    wait_all(third_a)
    summed[mem, 0:40] = add_last(last_a[z], got_a3)
    wait_all(third_b)
    summed[mem, 40:80] = add_last(last_b[x], got_b3)
    wait_all(third_c)
    summed[mem, 80:112] = add_last(last_c[y], got_c3)
    halves = link(summed.at[mem], summed.at[mem], 28, mate)
    halves.wait_recv()

    coarse_points(
        summed[...].reshape(224, 128), pick_ref, quarter_ref, lane_ref, picked, spread_rows, rows, mem
    )
    lane = lax.broadcasted_iota(jnp.int32, (32, 128), 1)
    points = gather_members(rows, lane)
    edges[...] = points.astype(jnp.bfloat16)
    line = lax.broadcasted_iota(jnp.int32, (16, LINK_LANES), 0)
    copies = [
        link(edges.at[pl.ds(16, 16)], halo.at[0], 29, along(0, 1)),
        link(edges.at[pl.ds(0, 16)], halo.at[1], 30, along(0, 3)),
    ]
    for side, turn, device in around:
        index = side * 3 + turn
        column = 15 if side == 0 else 0
        value = jnp.where(
            line == 2 * index, points[column:column + 1],
            jnp.where(line == 2 * index + 1, points[16 + column:17 + column], 0.0),
        )
        columns[index] = value.astype(jnp.bfloat16)
        copies.append(link(columns.at[index], halo.at[2 + index], 31 + index, device))
    points_ref[0:32, :] = edges[...]
    wait_all(copies)
    points_ref[32:48, :] = halo[0]
    points_ref[48:64, :] = halo[1]
    total = halo[2].astype(jnp.float32)
    for index in range(1, 6):
        total = total + halo[2 + index].astype(jnp.float32)
    points_ref[64:80, :] = total.astype(jnp.bfloat16)
    for copy in started + copies + [halves]:
        copy.wait_send()
    state_copy.wait()


def coarse(partial_ab, partial_c, state):
    pick, quarter = pick_tables()
    bf16, f32 = jnp.bfloat16, jnp.float32
    part = ((PART_A, bf16), (PART_B, bf16), (PART_C, bf16))
    return pl.pallas_call(
        coarse_kernel,
        out_shape=(
            jax.ShapeDtypeStruct((80, LINK_LANES), bf16),
            jax.ShapeDtypeStruct(state.shape, state.dtype),
        ),
        in_specs=[
            pl.BlockSpec(memory_space=pl.ANY),
            pl.BlockSpec(memory_space=pl.ANY),
            pl.BlockSpec(memory_space=pltpu.VMEM),
            pl.BlockSpec(memory_space=pltpu.VMEM),
            pl.BlockSpec(memory_space=pltpu.VMEM),
            pl.BlockSpec(memory_space=pl.ANY),
        ],
        out_specs=(pl.BlockSpec(memory_space=pltpu.VMEM), pl.BlockSpec(memory_space=pl.ANY)),
        scratch_shapes=[pltpu.VMEM((4, size, 128), kind) for size, kind in part]
        + [pltpu.VMEM((3, 4, size, 128), kind) for size, kind in part]
        + [pltpu.VMEM((4, size, 128), kind) for size, kind in part]
        + [pltpu.VMEM((3, size, 128), kind) for size, kind in part]
        + [pltpu.VMEM((4, size // 4, 128), f32) for size, kind in part]
        + [pltpu.VMEM((3, size // 4, 128), f32) for size, kind in part]
        + [
            pltpu.VMEM((2, 112, 128), f32),
            pltpu.VMEM((1648, WIDE), bf16),
            pltpu.VMEM((1648, WIDE), f32),
            pltpu.VMEM((1280, 128), f32),
            pltpu.VMEM((32, LINK_LANES), bf16),
            pltpu.VMEM((6, 16, LINK_LANES), bf16),
            pltpu.VMEM((8, 16, LINK_LANES), bf16),
            pltpu.SemaphoreType.DMA((37,)),
            pltpu.SemaphoreType.DMA((37,)),
            pltpu.SemaphoreType.DMA((3,)),
        ],
        compiler_params=pltpu.CompilerParams(
            collective_id=1, has_side_effects=True, vmem_limit_bytes=48 * 1024 * 1024
        ),
        name="coarse",
    )(partial_ab, partial_c, jnp.asarray(pick), jnp.asarray(quarter), jnp.asarray(lane_table()), state)


def tent(length, nodes):
    position = np.arange(length, dtype=np.float32)[:, None]
    centre = (np.arange(nodes, dtype=np.float32)[None, :] - 1.0) * B + (B - 1) * 0.5
    return np.maximum(0.0, 1.0 - np.abs(position - centre) / B)


def tent_tables():
    place_x, place_y = np.full(80, -1), np.full(80, -1)
    for i in range(2):
        for j in range(16):
            place_x[i * 16 + j], place_y[i * 16 + j] = i + 1, j + 1
            place_x[32 + i * 16 + j], place_y[32 + i * 16 + j] = 3 * i, j + 1
    for side in range(2):
        for turn in range(3):
            for i in range(2):
                row = 64 + (side * 3 + turn) * 2 + i
                place_y[row] = 17 * side
                place_x[row] = {1: i + 1, 0: 0 if i == 1 else -1, 2: 3 if i == 0 else -1}[turn]
    tables = []
    for length, nodes, place in ((16, 4, place_x), (128, 18, place_y)):
        table = np.zeros((3, 80, length), np.float32)
        for kind in range(3):
            weights = tent(length, nodes)
            if kind == 0:
                weights[:, 1] += weights[:, 0]
                weights[:, 0] = 0
            if kind == 2:
                weights[:, -2] += weights[:, -1]
                weights[:, -1] = 0
            for row in range(80):
                if place[row] >= 0:
                    table[kind, row] = weights[:, place[row]]
        tables.append(table)
    return tables


def per_device(volume, super_matrix, observed, error_var, obs_cells, counts, state):
    other_volume = swap(volume[0])
    partial_ab, partial_c = gram(counts, volume[0], other_volume, super_matrix[0], observed, error_var, obs_cells)
    points, other_state = coarse(partial_ab, partial_c, state)
    tent_x, tent_y = tent_tables()
    return apply(points, jnp.asarray(tent_x), jnp.asarray(tent_y), state, other_state)


def solution(mesh):
    placed = (
        P(("tx", "ty"), "mem", None, None),
        P(("tx", "ty"), None, None, None),
        P(("tx", "ty"), None),
        P(("tx", "ty"), None),
        P(("tx", "ty"), None),
        P(("tx", "ty"), None),
        P("mem", None, "tx", "ty"),
    )
    return jax.shard_map(
        per_device,
        mesh=mesh,
        in_specs=placed,
        out_specs=P("mem", None, "tx", "ty"),
        check_vma=False,
    )
```

```python
import numpy as np
import jax
import jax.numpy as jnp
from jax import lax
from jax.experimental import pallas as pl
from jax.experimental.pallas import tpu as pltpu
from jax.sharding import PartitionSpec as P

B = 8
LOC = 16
NS = 5
STEP = 512
SUB = 128
CHUNKS = 12


MESH = pl.DeviceIdType.MESH
PART_A, PART_B, PART_C = 160, 160, 128
GROUPS = 3
WIDE = 256
LINK_LANES = 1280


def place_of(row):
    if row < PART_A:
        return row % (PART_A // 8), row // (PART_A // 8)
    row -= PART_A
    if row < PART_B:
        return PART_A // 8 + row % (PART_B // 8), row // (PART_B // 8)
    row -= PART_B
    return (PART_A + PART_B) // 8 + row % (PART_C // 8), row // (PART_C // 8)


def pick_tables():
    rows = np.zeros((1648, 128), np.float32)
    eighths = np.zeros((1648, 128), np.float32)

    def put(target, core, local):
        row, eighth = place_of(local)
        rows[target] = 0
        eighths[target] = 0
        rows[target, core * 56 + row] = 1
        eighths[target, eighth * 16:eighth * 16 + 16] = 1

    for core, products in enumerate(core_products()):
        for index, entry in enumerate([entry for both in products for entry in both]):
            if entry is None:
                continue
            low, high, turn = entry
            for s in range(8):
                if high < 0:
                    put(1600 + 8 * low + s, core, index * 8 + s)
                    continue
                k, j = 8 * low + s, 8 * high + (s - turn) % 8
                put(j * 40 + k, core, index * 8 + s)
                put(k * 40 + j, core, index * 8 + s)
    return rows.astype(jnp.bfloat16), eighths.astype(jnp.bfloat16)


def lane_table():
    lanes = np.arange(WIDE)
    table = np.full((8, WIDE), -1, np.int32)
    table[0] = np.where(lanes < 240, lanes // 40, 7)
    table[1] = np.where(lanes < 240, lanes % 40, -1)
    return table


def block_swap(arrays):
    lane = lax.broadcasted_iota(jnp.int32, arrays[0].shape, 1)
    count = len(arrays)
    step = count // 2
    while step:
        width = step * (128 // count)
        mask = (lane & width) == 0
        turned = list(arrays)
        for low in range(count):
            if low & step:
                continue
            first, second = arrays[low], arrays[low + step]
            turned[low] = jnp.where(mask, first, pltpu.roll(second, width, 1))
            turned[low + step] = jnp.where(mask, pltpu.roll(first, 128 - width, 1), second)
        arrays = turned
        step //= 2
    return arrays


def split(value):
    high = value.astype(jnp.bfloat16)
    return high, (value - high.astype(jnp.float32)).astype(jnp.bfloat16)


def bdot(left, right):
    return jnp.dot(left, right, preferred_element_type=jnp.float32)


def coarse_points(summed, pick_ref, eighth_ref, lane_ref, picked, spread_rows, rows):
    lane_i, lane_j = lane_ref[0:1], lane_ref[1:2]
    high, low = split(summed)
    both = jnp.concatenate([high, low], axis=1)
    both = jnp.concatenate([both, jnp.zeros((16, WIDE), jnp.bfloat16)], axis=0)
    eighths = eighth_ref[...].astype(jnp.float32)
    found = bdot(pick_ref[...], both)
    picked[...] = jnp.concatenate(
        [found[:, :128] * eighths, found[:, 128:] * eighths], axis=1
    ).astype(jnp.bfloat16)
    row_c = lax.broadcasted_iota(jnp.int32, (WIDE, WIDE), 0) & 15
    eye = (lax.broadcasted_iota(jnp.int32, (40, WIDE), 0) == lane_j).astype(jnp.float32)
    real = lane_j >= 0
    same = (
        (jnp.concatenate(
            [jnp.full((40, WIDE), i, jnp.int32) for i in range(6)] + [jnp.full((16, WIDE), 9, jnp.int32)], axis=0
        ) == lane_i)
        .astype(jnp.float32)
        .astype(jnp.bfloat16)
    )

    def blocks(value):
        parts = [jnp.where(lane_i == i, value, 0.0) for i in range(6)] + [jnp.zeros((16, WIDE), jnp.float32)]
        return split(jnp.concatenate(parts, axis=0))

    def times(values, right):
        right_high, right_low = right
        highs, lows = zip(*[split(value) for value in values])
        count = len(values) * 40
        stack = jnp.concatenate([part.astype(jnp.float32) for part in highs + lows], axis=0).astype(jnp.bfloat16)
        main = bdot(stack, right_high)
        rest = bdot(stack[:count], right_low)
        return [
            main[40 * i:40 * i + 40] + (main[count + 40 * i:count + 40 * i + 40] + rest[40 * i:40 * i + 40])
            for i in range(len(values))
        ]

    uppers, lowers, scales, informs = [], [], [], []
    for group in range(GROUPS):
        expand = (row_c == lane_i + 6 * group).astype(jnp.float32) * real.astype(jnp.float32)
        spread_rows[...] = bdot(picked[...], expand.astype(jnp.bfloat16))
        gram = jnp.zeros((40, WIDE), jnp.float32)
        for j in range(40):
            gram = jnp.where(lane_j == j, spread_rows[40 * j:40 * j + 40], gram)
        informs.append(spread_rows[1600:1640])
        amat = eye + gram * (1.0 / 39)
        square = jnp.sum(amat * amat, axis=0, keepdims=True)
        first = square.astype(jnp.bfloat16).astype(jnp.float32)
        second = (square - first).astype(jnp.bfloat16).astype(jnp.float32)
        third = square - first - second
        parts = jnp.concatenate(
            [jnp.broadcast_to(part, (8, WIDE)) for part in (first, second, third, jnp.zeros_like(third))], axis=0
        )
        norm = bdot(parts.astype(jnp.bfloat16), same)
        norm = norm[0:1] + norm[8:9] + norm[16:17]
        scale = jnp.sqrt(jnp.where(real, norm, 1.0))
        scales.append(scale)
        uppers.append(amat / scale)
    for group in range(GROUPS):
        middle = 1.5 * eye - 0.5 * uppers[group]
        lowers.append(middle)
        uppers[group] = times([uppers[group]], blocks(middle))[0]
    for sweep in range(1, NS):
        middles = []
        for group in range(GROUPS):
            product = times([lowers[group]], blocks(uppers[group]))[0]
            middles.append(blocks(1.5 * eye - 0.5 * product))
        for group in range(GROUPS):
            if sweep < NS - 1:
                uppers[group], lowers[group] = times([uppers[group], lowers[group]], middles[group])
            else:
                lowers[group] = times([lowers[group]], middles[group])[0]
    target = lax.broadcasted_iota(jnp.int32, (WIDE, 768), 1)
    source = lax.broadcasted_iota(jnp.int32, (WIDE, 768), 0)
    own = target & 31
    chooses = []
    for core in range(2):
        wanted = (target >> 7) * 40 + core * 20 + own
        chooses.append(((source == wanted) & (own < 20)).astype(jnp.float32).astype(jnp.bfloat16))
    for group in range(GROUPS):
        inv_half = lowers[group] / jnp.sqrt(scales[group])
        step_one = jnp.sum(inv_half * informs[group], axis=0, keepdims=True)
        product = inv_half * step_one
        high, low = split(product)
        stack = jnp.concatenate([high.astype(jnp.float32), low.astype(jnp.float32)], axis=0).astype(jnp.bfloat16)
        moved = bdot(stack, same)
        shift = (moved[:40] + moved[40:]) * (1.0 / 39)
        shift = shift - jnp.sum(shift, axis=0, keepdims=True) * (1.0 / 40)
        spread = inv_half - jnp.sum(inv_half, axis=0, keepdims=True) * (1.0 / 40)
        trans = (1.0 / 40 + shift + spread).astype(jnp.bfloat16)
        for core in range(2):
            chosen = bdot(trans, chooses[core])
            for i in range(6):
                point = group * 6 + i
                if point < 16:
                    rows[core, point * 40:point * 40 + 40, :] = chosen[:, i * 128:i * 128 + 128]


def gather_members(rows, lane):
    quarter = lane >> 5
    pieces = []
    for q in range(10):
        piece = rows[pl.ds(4 * q, 16, stride=40), :]
        for p in range(1, 4):
            piece = jnp.where(quarter == p, rows[pl.ds(4 * q + p, 16, stride=40), :], piece)
        pieces.append(piece)
    return jnp.concatenate(pieces, axis=1)


UNROLL = 4


def core_products():
    first, second = [], []
    for high in (4, 3, 2, 1):
        for low in range(high):
            for turn in range(0, 8, 2):
                both = ((low, high, turn), (low, high, turn + 1))
                (first if high > 2 else second).append(both)
    for low in range(5):
        second.append(((low, low, 0), (low, low, 1)))
        second.append(((low, low, 2), (low, low, 3)))
    second.append(((0, 0, 4), (1, 1, 4)))
    second.append(((2, 2, 4), (3, 3, 4)))
    second.append(((0, -1, 0), (1, -1, 0)))
    second.append(((2, -1, 0), (3, -1, 0)))
    second.append(((4, 4, 4), (4, -1, 0)))
    second.append((None, None))
    return first, second


def gram_kernel(
    count_ref, volume_hbm, other_hbm, matrix_hbm, value_ref, error_ref, cell_ref, ab_ref, c_ref,
    volume, matrix, wide, anomalies, surprises, weights, lhs0, lhs1, rhs0, rhs1, total, offsets, sems,
):
    mem = lax.axis_index("mem")
    chunks = sems.shape[0]
    radar_blocks = matrix.shape[0]
    held = volume_hbm.shape[0]
    tiles = count_ref.shape[1]
    chunk = radar_blocks // chunks
    steps = radar_blocks * SUB // STEP
    per_step = STEP // SUB

    def fetch(index):
        part = pl.ds(index * chunk, chunk)
        return (
            pltpu.make_async_copy(volume_hbm.at[:, part], volume.at[pl.ds(mem * held, held), part], sems.at[index, 0]),
            pltpu.make_async_copy(
                other_hbm.at[:, part], volume.at[pl.ds((1 - mem) * held, held), part], sems.at[index, 1]
            ),
            pltpu.make_async_copy(matrix_hbm.at[part], matrix.at[part], sems.at[index, 2]),
        )

    for index in range(chunks):
        for copy in fetch(index):
            copy.start()

    offsets[0] = 0
    running = jnp.int32(0)
    for tile in range(tiles):
        running = running + count_ref[0, tile]
        offsets[tile + 1] = running
    for extra in range(12):
        offsets[tiles + 1 + extra] = running
    total[...] = jnp.zeros_like(total)
    centre_y = lax.broadcasted_iota(jnp.int32, (16, STEP), 0).astype(jnp.float32) * B + (B - 1) / 2

    def project(index, carry):
        for copy in fetch(index):
            copy.wait()
        part = pl.ds(pl.multiple_of(index * chunk, chunk), chunk)
        for member in range(2 * held):
            wide[member * chunk:member * chunk + chunk, :] = volume[member, part].astype(jnp.float32)
        for inner in range(chunk // per_step):
            step = index * (chunk // per_step) + inner
            here = pl.ds(pl.multiple_of(step * STEP, STEP), STEP)
            cells = cell_ref[:, here]
            pos_x = (cells >> 7).astype(jnp.float32)
            pos_y = (cells & 127).astype(jnp.float32)
            inverse = (1.0 / error_ref[:, here]).astype(jnp.bfloat16).astype(jnp.float32)
            near_y = jnp.exp((pos_y - centre_y) ** 2 * (-0.5 / LOC**2)) * inverse
            for i in range(2):
                near_x = jnp.exp((pos_x - (i * B + (B - 1) / 2)) ** 2 * (-0.5 / LOC**2))
                weights[step, i * 16:i * 16 + 16, :] = (near_x * near_y).astype(jnp.bfloat16)
            values = value_ref[:, here].astype(jnp.float32)
            for sub in range(per_step):
                local = inner * per_step + sub
                block = index * chunk + local
                gates = wide[pl.ds(local, 2 * held, stride=chunk), :].astype(jnp.bfloat16)
                obs = jnp.dot(gates, matrix[block], preferred_element_type=jnp.float32)
                obs = obs.astype(jnp.bfloat16).astype(jnp.float32)
                mean = jnp.sum(obs, axis=0, keepdims=True) * (1.0 / 40)
                anomalies[block] = obs - mean
                surprises[block] = jnp.broadcast_to(values[:, sub * SUB:(sub + 1) * SUB] - mean, (8, SUB))
        return carry

    lax.fori_loop(0, chunks, project, 0)

    lane = lax.broadcasted_iota(jnp.int32, (8, STEP), 1)

    def build(item, lhs, rhs, products):
        step, group = item
        step = jnp.minimum(step, steps - 1)
        for sub in range(per_step):
            block = step * per_step + sub
            lanes = slice(sub * SUB, (sub + 1) * SUB)
            part = [
                anomalies[block, 8 * i:8 * i + 8, :].astype(jnp.bfloat16).astype(jnp.float32) for i in range(5)
            ]
            made = {}

            def operand(kind, entry):
                low, high, turn = entry
                if kind == 0:
                    return part[low]
                if high < 0:
                    return surprises[block]
                if (high, turn) not in made:
                    made[high, turn] = part[high] if turn == 0 else pltpu.roll(part[high], turn, 0)
                return made[high, turn]

            packed = {}

            def pack(kind, both):
                key = tuple((kind, entry[0]) if kind == 0 else (kind, entry[1:]) for entry in both)
                if key not in packed:
                    packed[key] = jnp.concatenate([operand(kind, entry) for entry in both], axis=0).astype(jnp.bfloat16)
                return packed[key]

            for index, both in enumerate(products):
                if both[0] is None:
                    continue
                lhs[index * 16:index * 16 + 16, lanes] = pack(0, both) * pack(1, both)
        slot = lane + step * STEP
        reached = [jnp.where(slot >= offsets[group * 4 + i], 1.0, 0.0) for i in range(9)]
        weight = weights[step]
        for i in range(8):
            inside = reached[i] - reached[i + 1]
            inside = jnp.concatenate([inside, inside], axis=0).astype(jnp.bfloat16)
            for half in range(2):
                rhs[i * 32 + half * 16:i * 32 + half * 16 + 16, :] = weight[half * 16:half * 16 + 16] * inside

    def use(group, lhs, rhs):
        added = lax.dot_general(
            lhs[...], rhs[...], (((1,), (1,)), ((), ())), preferred_element_type=jnp.float32
        )
        total[group] += added[:, :128]
        total[group + 1] += added[:, 128:]

    def follow(item):
        step, group = item
        end = (step + 1) * STEP
        again = (group + 2 < tiles // 4) & (offsets[group * 4 + 8] < end)
        ahead = (offsets[group * 4 + 4] <= end).astype(jnp.int32) + (offsets[group * 4 + 8] <= end).astype(jnp.int32)
        next_step = jnp.where(again, step, step + 1)
        next_group = jnp.where(again, group + 2, group + ahead)
        return next_step, jnp.where(next_step >= steps, tiles // 4, next_group)

    for core, products in enumerate(core_products()):

        @pl.when(mem == core)
        def _():
            if products[-1][0] is None:
                lhs0[len(products) * 16 - 16:, :] = jnp.zeros((16, STEP), jnp.bfloat16)
                lhs1[len(products) * 16 - 16:, :] = jnp.zeros((16, STEP), jnp.bfloat16)
            start = (jnp.int32(0), jnp.int32(0))
            build(start, lhs0, rhs0, products)

            def body(item):
                for turn in range(UNROLL):
                    lhs, rhs = (lhs0, rhs0) if turn % 2 == 0 else (lhs1, rhs1)
                    other_lhs, other_rhs = (lhs1, rhs1) if turn % 2 == 0 else (lhs0, rhs0)
                    following = follow(item)
                    use(item[1], lhs, rhs)
                    build(following, other_lhs, other_rhs, products)
                    item = following
                return item

            lax.while_loop(lambda item: item[0] < steps, body, start)

    for x in range(4):
        for y in range(4):
            ab_ref[x, y] = total[x * 4 + y, :PART_A + PART_B].astype(jnp.bfloat16)
        for z, value in enumerate(block_swap([total[x * 4 + y, PART_A + PART_B:] for y in range(4)])):
            c_ref[z, x] = value.astype(jnp.bfloat16)


def gram(counts, volume, other, matrix, values, errors, cells):
    blocks = matrix.shape[0]
    tiles = counts.shape[1]
    members = 2 * volume.shape[0]
    rows = PART_A + PART_B + PART_C
    steps = blocks * SUB // STEP
    vmem = pl.BlockSpec(memory_space=pltpu.VMEM)
    hbm = pl.BlockSpec(memory_space=pl.ANY)
    return pl.pallas_call(
        gram_kernel,
        out_shape=(
            jax.ShapeDtypeStruct((4, 4, PART_A + PART_B, 128), jnp.bfloat16),
            jax.ShapeDtypeStruct((4, 4, PART_C, 128), jnp.bfloat16),
        ),
        in_specs=[pl.BlockSpec(memory_space=pltpu.SMEM), hbm, hbm, hbm, vmem, vmem, vmem],
        out_specs=(vmem, vmem),
        scratch_shapes=[
            pltpu.VMEM((members, blocks, 128), jnp.bfloat16),
            pltpu.VMEM((blocks, 128, 128), jnp.bfloat16),
            pltpu.VMEM((members * (blocks // CHUNKS), 128), jnp.float32),
            pltpu.VMEM((blocks, members, 128), jnp.float32),
            pltpu.VMEM((blocks, 8, 128), jnp.float32),
            pltpu.VMEM((steps, 32, STEP), jnp.bfloat16),
            pltpu.VMEM((rows, STEP), jnp.bfloat16),
            pltpu.VMEM((rows, STEP), jnp.bfloat16),
            pltpu.VMEM((256, STEP), jnp.bfloat16),
            pltpu.VMEM((256, STEP), jnp.bfloat16),
            pltpu.VMEM((tiles // 4 + 2, rows, 128), jnp.float32),
            pltpu.SMEM((tiles + 13,), jnp.int32),
            pltpu.SemaphoreType.DMA((CHUNKS, 3)),
        ],
        compiler_params=pltpu.CompilerParams(vmem_limit_bytes=56 * 1024 * 1024),
        name="gram",
    )(counts, volume, other, matrix, values, errors, cells)


def apply_kernel(points_ref, tent_x_ref, tent_y_ref, state_ref, other_ref, out_ref, fine, flat, result):
    levels, width_x, width_y = state_ref.shape[1:]
    own = out_ref.shape[0]
    members = 2 * own
    mem, tx, ty = lax.axis_index("mem"), lax.axis_index("tx"), lax.axis_index("ty")
    kind_x = jnp.where(tx == 0, 0, jnp.where(tx == lax.axis_size("tx") - 1, 2, 1))
    kind_y = jnp.where(ty == 0, 0, jnp.where(ty == lax.axis_size("ty") - 1, 2, 1))
    tent_x, tent_y = tent_x_ref[kind_x], tent_y_ref[kind_y]
    points = points_ref[...].astype(jnp.float32)
    points = jnp.concatenate([points, jnp.zeros((48, points.shape[1]), jnp.float32)], axis=0).T
    points = points[:, :80].astype(jnp.bfloat16)

    def widen(member, carry):
        for source, first in ((state_ref, mem * own), (other_ref, (1 - mem) * own)):
            start = pl.multiple_of((first + member) * levels * width_x, 8)
            flat[pl.ds(start, levels * width_x), :] = (
                source[member].astype(jnp.float32).reshape(levels * width_x, width_y)
            )
        return carry

    lax.fori_loop(0, own, widen, 0)
    for x in range(0, width_x, 2):
        tent = jnp.concatenate(
            [tent_x[:, x + i:x + i + 1] * tent_y for i in range(2)], axis=1
        ).astype(jnp.bfloat16)
        made = jnp.dot(points, tent, preferred_element_type=jnp.float32)
        made = made.astype(jnp.bfloat16).astype(jnp.float32)
        fine[x] = made[:, :128]
        fine[x + 1] = made[:, 128:]

    def column(x, carry):
        def add(k4, sums):
            sums = list(sums)
            for i in range(4):
                k = k4 * 4 + i
                field = flat[pl.ds(k * (levels * width_x) + x, levels, stride=width_x), :]
                for j in range(own):
                    row = fine[x, pl.ds(k * 32 + j, 8, stride=0), :]
                    sums[j] = sums[j] + row * field
            return tuple(sums)

        zero = jnp.zeros((levels, width_y), jnp.float32)
        sums = lax.fori_loop(0, members // 4, add, (zero,) * own)
        for j in range(own):
            result[pl.ds(j * (levels * width_x) + x, levels, stride=width_x), :] = sums[j]
        return carry

    lax.fori_loop(0, width_x, column, 0)

    def narrow(j, carry):
        start = pl.multiple_of(j * levels * width_x, 8)
        out_ref[j] = (
            result[pl.ds(start, levels * width_x), :]
            .reshape(levels, width_x, width_y)
            .astype(jnp.bfloat16)
        )
        return carry

    lax.fori_loop(0, own, narrow, 0)


def apply(points, tent_x, tent_y, state, other):
    own, levels, width_x, width_y = state.shape
    members = 2 * own
    return pl.pallas_call(
        apply_kernel,
        out_shape=jax.ShapeDtypeStruct((own, levels, width_x, width_y), jnp.bfloat16),
        in_specs=[pl.BlockSpec(memory_space=pltpu.VMEM)] * 5,
        out_specs=pl.BlockSpec(memory_space=pltpu.VMEM),
        scratch_shapes=[
            pltpu.VMEM((width_x, points.shape[1], width_y), jnp.float32),
            pltpu.VMEM((members * levels * width_x, width_y), jnp.float32),
            pltpu.VMEM((own * levels * width_x, width_y), jnp.float32),
        ],
        compiler_params=pltpu.CompilerParams(vmem_limit_bytes=48 * 1024 * 1024),
        name="apply",
    )(points, tent_x, tent_y, state, other)


def swap_kernel(volume_ref, other_ref, send, recv):
    mem = lax.axis_index("mem")
    mate = (lax.axis_index("tx"), lax.axis_index("ty"), 1 - mem)
    barrier = pltpu.get_barrier_semaphore()
    pl.semaphore_signal(barrier, inc=1, device_id=mate, device_id_type=MESH)
    pl.semaphore_wait(barrier, 1)
    count = send.shape[0]
    share = volume_ref.shape[0] // count
    copies = []
    for index in range(count):
        part = pl.ds(index * share, share)
        copies.append(
            pltpu.make_async_remote_copy(
                src_ref=volume_ref.at[part], dst_ref=other_ref.at[part], send_sem=send.at[index],
                recv_sem=recv.at[index], device_id=mate, device_id_type=MESH,
            )
        )
    for copy in copies:
        copy.start()
    for copy in copies:
        copy.wait()


def swap(volume):
    return pl.pallas_call(
        swap_kernel,
        out_shape=jax.ShapeDtypeStruct(volume.shape, volume.dtype),
        in_specs=[pl.BlockSpec(memory_space=pl.ANY)],
        out_specs=pl.BlockSpec(memory_space=pl.ANY),
        scratch_shapes=[pltpu.SemaphoreType.DMA((4,)), pltpu.SemaphoreType.DMA((4,))],
        compiler_params=pltpu.CompilerParams(collective_id=0, has_side_effects=True),
        name="swap",
    )(volume)


def coarse_kernel(
    ab_ref, c_ref, pick_ref, eighth_ref, lane_ref, state_ref, points_ref, other_ref,
    own_a, own_b, own_c, pass_a, pass_b, pass_c, via_a, via_b, via_c, got_a, got_b, got_c,
    next_a, next_b, next_c, got_a2, got_b2, got_c2, last_a, last_b, last_c, got_a3, got_b3, got_c3,
    folded, summed, pick, eighth, picked, spread_rows, rows, edges, columns, halo, corners,
    send, recv, local,
):
    x, ty, mem = lax.axis_index("tx"), lax.axis_index("ty"), lax.axis_index("mem")
    y, z = ty // 4, ty % 4
    spot = (x, y, z)

    def along(axis, turn, core=None):
        core = mem if core is None else core
        if axis == 0:
            return ((x + turn) % 4, ty, core)
        if axis == 1:
            return (x, ((y + turn) % 4) * 4 + z, core)
        return (x, y * 4 + (z + turn) % 4, core)

    mate = (x, ty, 1 - mem)
    ahead = 2 * mem - 1
    around = []
    for step in (1, 15):
        for core in range(2):
            around.append(((x, (ty + step) % 16, core), (((x + ahead) + 4) % 4, (ty + step) % 16, core)))
    peers = [along(axis, turn, core) for axis in range(3) for turn in range(1, 4) for core in (mem, 1 - mem)]
    peers += [mate] + [device for pair in around for device in pair]
    peers += [(((x - ahead) + 4) % 4, (ty + step) % 16, mem) for step in (1, 15)]
    barrier = pltpu.get_barrier_semaphore()
    for device in peers:
        pl.semaphore_signal(barrier, inc=1, device_id=device, device_id_type=MESH)

    parts = (
        (0, lambda place, first, size: ab_ref.at[place, :, pl.ds(first, size)], PART_A),
        (1, lambda place, first, size: ab_ref.at[:, place, pl.ds(PART_A + first, size)], PART_B),
        (2, lambda place, first, size: c_ref.at[place, :, pl.ds(first, size)], PART_C),
    )
    owns, passes, vias, gots = (own_a, own_b, own_c), (pass_a, pass_b, pass_c), (via_a, via_b, via_c), (got_a, got_b, got_c)
    fetched = []
    for index, (axis, piece, size) in enumerate(parts):
        half = size // 2
        up, down = (spot[axis] + 1) % 4, (spot[axis] + 3) % 4
        fetched.append(
            [
                pltpu.make_async_copy(piece(up, 0, half), passes[index].at[0], local.at[3 * index]),
                pltpu.make_async_copy(piece(down, half, half), passes[index].at[1], local.at[3 * index + 1]),
                pltpu.make_async_copy(piece(spot[axis], 0, size), owns[index], local.at[3 * index + 2]),
            ]
        )
        for copy in fetched[index]:
            copy.start()
    tables = [
        pltpu.make_async_copy(pick_ref, pick, local.at[9]),
        pltpu.make_async_copy(eighth_ref, eighth, local.at[10]),
    ]
    for copy in tables:
        copy.start()
    for index in (0, 5, 6, 11):
        corners[index * 16:index * 16 + 16, :] = jnp.zeros((16, 128), jnp.float32)
    corners[192:256, :] = jnp.zeros((64, 128), jnp.float32)
    for core in range(2):
        rows[core, 640:, :] = jnp.zeros((rows.shape[1] - 640, 128), jnp.float32)
    pl.semaphore_wait(barrier, len(peers))

    started = []

    def link(source, target, index, device, landing=None):
        copy = pltpu.make_async_remote_copy(
            src_ref=source, dst_ref=target, send_sem=send.at[index],
            recv_sem=recv.at[index if landing is None else landing], device_id=device, device_id_type=MESH,
        )
        copy.start()
        started.append(copy)
        return copy

    relays, plains, finals = [], [], []
    for index, (axis, piece, size) in enumerate(parts):
        half = size // 2
        opposite = (spot[axis] + 2) % 4
        relays.append(
            [
                link(piece(opposite, 0, half), vias[index].at[0], 6 * index, along(axis, 1)),
                link(piece(opposite, half, half), vias[index].at[1], 6 * index + 1, along(axis, 3)),
            ]
        )
    for index, (axis, piece, size) in enumerate(parts):
        half = size // 2
        up, down = (spot[axis] + 1) % 4, (spot[axis] + 3) % 4
        plains.append(
            [
                link(piece(up, half, half), gots[index].at[0, :, pl.ds(half, half)], 6 * index + 2, along(axis, 1)),
                link(piece(down, 0, half), gots[index].at[1, :, pl.ds(0, half)], 6 * index + 3, along(axis, 3)),
            ]
        )
    state_copy = link(state_ref, other_ref, 18, mate)
    for index, (axis, piece, size) in enumerate(parts):
        half = size // 2
        finals.append([])
        for way in range(2):
            fetched[index][way].wait()
            relays[index][way].wait_recv()
            for block in range(4):
                passes[index][way, block] = (
                    passes[index][way, block].astype(jnp.float32) + vias[index][way, block].astype(jnp.float32)
                ).astype(jnp.bfloat16)
            target = gots[index].at[way, :, pl.ds(way * half, half)]
            finals[index].append(
                link(passes[index].at[way], target, 6 * index + 4 + way, along(axis, 1 + 2 * way))
            )

    def arrive(index):
        fetched[index][2].wait()
        for copy in plains[index] + finals[index]:
            copy.wait_recv()

    def add_up(index, block):
        value = owns[index][block].astype(jnp.float32)
        for way in range(2):
            value = value + gots[index][way, block].astype(jnp.float32)
        return value

    def stage(first, axis, source, target):
        copies = []
        for turn in (2, 1, 3):
            place = (spot[axis] + turn) % 4
            copies.append(link(source.at[place], target.at[turn - 1], first + turn - 1, along(axis, turn)))
        return copies

    def wait_all(copies):
        for copy in copies:
            copy.wait_recv()

    def add_last(own, got):
        value = own.astype(jnp.float32)
        for turn in range(3):
            value = value + got[turn].astype(jnp.float32)
        return value

    arrive(0)
    for block in range(4):
        next_a[block] = add_up(0, block).astype(jnp.bfloat16)
    second_a = stage(19, 1, next_a, got_a2)
    arrive(1)
    for block, value in enumerate(block_swap([add_up(1, block) for block in range(4)])):
        next_b[block] = value.astype(jnp.bfloat16)
    second_b = stage(22, 2, next_b, got_b2)
    arrive(2)
    for block in range(4):
        next_c[block] = add_up(2, block).astype(jnp.bfloat16)
    second_c = stage(25, 0, next_c, got_c2)

    def fold(value, target):
        size = value.shape[0] // 8
        folded[0:value.shape[0], :] = value
        pieces = [folded[i * size:(i + 1) * size, :] for i in range(8)]
        for index, part in enumerate(block_swap(pieces)):
            target[index] = part

    def third(number, axis, source, target):
        first = 28 + 8 * number
        for turn in (2, 1, 3, 0):
            place = (spot[axis] + turn) % 4
            for other in range(2):
                if turn == 0 and other == 0:
                    continue
                core = 1 - mem if other else mem
                link(
                    source.at[place * 2 + core], target.at[mem * 4 + turn], first + 2 * turn + other,
                    along(axis, turn, core), first + 2 * turn + mem,
                )
        target[mem * 4] = source[spot[axis] * 2 + mem]

    def sum_third(number, source, target, row):
        first = 28 + 8 * number

        def landed(core, turn):
            pltpu.make_async_remote_copy(
                src_ref=source.at[0], dst_ref=target.at[core * 4 + turn], send_sem=send.at[first],
                recv_sem=recv.at[first + 2 * turn + core], device_id=mate, device_id_type=MESH,
            ).wait_recv()

        landed(1 - mem, 0)
        for turn in range(1, 4):
            for core in range(2):
                landed(core, turn)
        size = source.shape[1]
        for core in range(2):
            value = target[core * 4]
            for turn in range(1, 4):
                value = value + target[core * 4 + turn]
            summed[core * 56 + row:core * 56 + row + size, :] = value

    wait_all(second_a)
    fold(add_last(next_a[y], got_a2), last_a)
    third(0, 2, last_a, got_a3)
    wait_all(second_b)
    fold(add_last(next_b[z], got_b2), last_b)
    third(1, 0, last_b, got_b3)
    wait_all(second_c)
    fold(add_last(next_c[x], got_c2), last_c)
    third(2, 1, last_c, got_c3)
    sum_third(0, last_a, got_a3, 0)
    sum_third(1, last_b, got_b3, 20)
    sum_third(2, last_c, got_c3, 40)

    for copy in tables:
        copy.wait()
    coarse_points(summed[...], pick, eighth, lane_ref, picked, spread_rows, rows)

    quarter_of = lax.broadcasted_iota(jnp.int32, (16, 128), 1) >> 5
    for core in range(2):
        for side in range(2):
            point = 15 * (1 - side)
            value = rows[core, pl.ds(point * 40, 16, stride=4), :]
            for p in range(1, 4):
                value = jnp.where(quarter_of == p, rows[core, pl.ds(point * 40 + p, 16, stride=4), :], value)
            columns[core, side] = value
    outer = jnp.where(mem == 1, 0, 2)
    for index, (straight, slanted) in enumerate(around):
        side, core = index // 2, index % 2
        for device, turn in ((straight, 1), (slanted, outer)):
            slot = (side * 3 + turn) * 2 + mem
            link(
                columns.at[core, side], corners.at[pl.ds(slot * 16, 16)],
                52 + 2 * index + (1 if device is slanted else 0), device, 52 + slot,
            )
    lane = lax.broadcasted_iota(jnp.int32, (16, 128), 1)
    for core in range(2):
        edges[core] = gather_members(rows.at[core], lane).astype(jnp.bfloat16)
    link(edges.at[1 - mem], halo.at[mem], 60, mate, 64 + mem)
    for other in range(2):
        core = 1 - mem if other else mem
        link(edges.at[core], halo.at[3 - mem], 61 + other, ((x + ahead + 4) % 4, ty, core), 64 + 3 - mem)
    points_ref[pl.ds(pl.multiple_of(mem * 16, 16), 16), :] = edges[mem]

    def landed(source, target, index):
        pltpu.make_async_remote_copy(
            src_ref=source, dst_ref=target, send_sem=send.at[0], recv_sem=recv.at[index],
            device_id=mate, device_id_type=MESH,
        ).wait_recv()

    for slot in (1, 2, 3, 4, 7, 8, 9, 10):
        landed(columns.at[0, 0], corners.at[pl.ds(slot * 16, 16)], 52 + slot)
    for q in range(10):
        points_ref[64:80, q * 128:q * 128 + 128] = corners[pl.ds(q, 16, stride=16), :].astype(jnp.bfloat16)
    landed(edges.at[0], halo.at[1 - mem], 64 + 1 - mem)
    points_ref[pl.ds(pl.multiple_of((1 - mem) * 16, 16), 16), :] = halo[1 - mem]
    for slot in (2, 3):
        landed(edges.at[0], halo.at[slot], 64 + slot)
        points_ref[slot * 16:slot * 16 + 16, :] = halo[slot]
    state_copy.wait_recv()
    for copy in started:
        copy.wait_send()


def coarse(partial_ab, partial_c, state):
    pick, eighth = pick_tables()
    bf16, f32 = jnp.bfloat16, jnp.float32
    sizes = (PART_A, PART_B, PART_C)
    hbm, vmem = pl.BlockSpec(memory_space=pl.ANY), pl.BlockSpec(memory_space=pltpu.VMEM)
    return pl.pallas_call(
        coarse_kernel,
        out_shape=(
            jax.ShapeDtypeStruct((80, LINK_LANES), bf16),
            jax.ShapeDtypeStruct(state.shape, state.dtype),
        ),
        in_specs=[hbm, hbm, hbm, hbm, vmem, hbm],
        out_specs=(vmem, hbm),
        scratch_shapes=[pltpu.VMEM((4, size, 128), bf16) for size in sizes]
        + [pltpu.VMEM((2, 4, size // 2, 128), bf16) for size in sizes]
        + [pltpu.VMEM((2, 4, size // 2, 128), bf16) for size in sizes]
        + [pltpu.VMEM((2, 4, size, 128), bf16) for size in sizes]
        + [pltpu.VMEM((4, size, 128), bf16) for size in sizes]
        + [pltpu.VMEM((3, size, 128), bf16) for size in sizes]
        + [pltpu.VMEM((8, size // 8, 128), f32) for size in sizes]
        + [pltpu.VMEM((8, size // 8, 128), f32) for size in sizes]
        + [
            pltpu.VMEM((PART_A, 128), f32),
            pltpu.VMEM((112, 128), f32),
            pltpu.VMEM((1648, 128), bf16),
            pltpu.VMEM((1648, 128), bf16),
            pltpu.VMEM((1648, WIDE), bf16),
            pltpu.VMEM((1648, WIDE), f32),
            pltpu.VMEM((2, 672, 128), f32),
            pltpu.VMEM((2, 16, LINK_LANES), bf16),
            pltpu.VMEM((2, 2, 16, 128), f32),
            pltpu.VMEM((4, 16, LINK_LANES), bf16),
            pltpu.VMEM((256, 128), f32),
            pltpu.SemaphoreType.DMA((68,)),
            pltpu.SemaphoreType.DMA((68,)),
            pltpu.SemaphoreType.DMA((11,)),
        ],
        compiler_params=pltpu.CompilerParams(
            collective_id=1, has_side_effects=True, vmem_limit_bytes=48 * 1024 * 1024
        ),
        name="coarse",
    )(partial_ab, partial_c, jnp.asarray(pick), jnp.asarray(eighth), jnp.asarray(lane_table()), state)


def tent(length, nodes):
    position = np.arange(length, dtype=np.float32)[:, None]
    centre = (np.arange(nodes, dtype=np.float32)[None, :] - 1.0) * B + (B - 1) * 0.5
    return np.maximum(0.0, 1.0 - np.abs(position - centre) / B)


def tent_tables():
    place_x, place_y = np.full(80, -1), np.full(80, -1)
    for i in range(2):
        for j in range(16):
            place_x[i * 16 + j], place_y[i * 16 + j] = i + 1, j + 1
            place_x[32 + i * 16 + j], place_y[32 + i * 16 + j] = 3 * i, j + 1
    for side in range(2):
        for turn in range(3):
            for i in range(2):
                row = 64 + (side * 3 + turn) * 2 + i
                place_y[row] = 17 * side
                place_x[row] = {1: i + 1, 0: 0 if i == 1 else -1, 2: 3 if i == 0 else -1}[turn]
    tables = []
    for length, nodes, place in ((16, 4, place_x), (128, 18, place_y)):
        table = np.zeros((3, 80, length), np.float32)
        for kind in range(3):
            weights = tent(length, nodes)
            if kind == 0:
                weights[:, 1] += weights[:, 0]
                weights[:, 0] = 0
            if kind == 2:
                weights[:, -2] += weights[:, -1]
                weights[:, -1] = 0
            for row in range(80):
                if place[row] >= 0:
                    table[kind, row] = weights[:, place[row]]
        tables.append(table)
    return tables


def per_device(volume, super_matrix, observed, error_var, obs_cells, counts, state):
    other_volume = swap(volume[0])
    partial_ab, partial_c = gram(counts, volume[0], other_volume, super_matrix[0], observed, error_var, obs_cells)
    points, other_state = coarse(partial_ab, partial_c, state)
    tent_x, tent_y = tent_tables()
    return apply(points, jnp.asarray(tent_x), jnp.asarray(tent_y), state, other_state)


def solution(mesh):
    placed = (
        P(("tx", "ty"), "mem", None, None),
        P(("tx", "ty"), None, None, None),
        P(("tx", "ty"), None),
        P(("tx", "ty"), None),
        P(("tx", "ty"), None),
        P(("tx", "ty"), None),
        P("mem", None, "tx", "ty"),
    )
    return jax.shard_map(
        per_device,
        mesh=mesh,
        in_specs=placed,
        out_specs=P("mem", None, "tx", "ty"),
        check_vma=False,
    )
```

```python
import numpy as np
import jax
import jax.numpy as jnp
from jax import lax
from jax.experimental import pallas as pl
from jax.experimental.pallas import tpu as pltpu
from jax.sharding import PartitionSpec as P

B = 8
LOC = 16
NS = 5
STEP = 768
SUB = 128
CHUNKS = 4


MESH = pl.DeviceIdType.MESH
PART_A, PART_B, PART_C = 160, 160, 128
GROUPS = 3
WIDE = 256
LINK_LANES = 896


def place_of(row):
    if row < PART_A:
        return row % (PART_A // 8), row // (PART_A // 8)
    row -= PART_A
    if row < PART_B:
        return PART_A // 8 + row % (PART_B // 8), row // (PART_B // 8)
    row -= PART_B
    return (PART_A + PART_B) // 8 + row % (PART_C // 8), row // (PART_C // 8)


def pick_tables():
    rows = np.zeros((1648, 128), np.float32)
    eighths = np.zeros((1648, 128), np.float32)

    def put(target, core, local):
        row, eighth = place_of(local)
        rows[target] = 0
        eighths[target] = 0
        rows[target, core * 56 + row] = 1
        eighths[target, eighth * 16:eighth * 16 + 16] = 1

    for core, products in enumerate(core_products()):
        for index, entry in enumerate([entry for both in products for entry in both]):
            if entry is None:
                continue
            low, high, turn = entry
            for s in range(8):
                if high < 0:
                    put(1600 + 8 * low + s, core, index * 8 + s)
                    continue
                k, j = 8 * low + s, 8 * high + (s - turn) % 8
                put(j * 40 + k, core, index * 8 + s)
                put(k * 40 + j, core, index * 8 + s)
    return rows.astype(jnp.bfloat16), eighths.astype(jnp.bfloat16)


def lane_table():
    lanes = np.arange(WIDE)
    table = np.full((8, WIDE), -1, np.int32)
    table[0] = np.where(lanes < 240, lanes // 40, 7)
    table[1] = np.where(lanes < 240, lanes % 40, -1)
    return table


def block_swap(arrays):
    lane = lax.broadcasted_iota(jnp.int32, arrays[0].shape, 1)
    count = len(arrays)
    step = count // 2
    while step:
        width = step * (128 // count)
        mask = (lane & width) == 0
        turned = list(arrays)
        for low in range(count):
            if low & step:
                continue
            first, second = arrays[low], arrays[low + step]
            turned[low] = jnp.where(mask, first, pltpu.roll(second, width, 1))
            turned[low + step] = jnp.where(mask, pltpu.roll(first, 128 - width, 1), second)
        arrays = turned
        step //= 2
    return arrays


def split(value):
    high = value.astype(jnp.bfloat16)
    return high, (value - high.astype(jnp.float32)).astype(jnp.bfloat16)


def bdot(left, right):
    return jnp.dot(left, right, preferred_element_type=jnp.float32)


def coarse_points(summed, pick_ref, eighth_ref, lane_ref, picked, spread_rows, rows):
    lane_i, lane_j = lane_ref[0:1], lane_ref[1:2]
    high, low = split(summed)
    both = jnp.concatenate([high, low], axis=1)
    both = jnp.concatenate([both, jnp.zeros((16, WIDE), jnp.bfloat16)], axis=0)
    eighths = eighth_ref[...].astype(jnp.float32)
    found = bdot(pick_ref[...], both)
    picked[...] = jnp.concatenate(
        [found[:, :128] * eighths, found[:, 128:] * eighths], axis=1
    ).astype(jnp.bfloat16)
    row_c = lax.broadcasted_iota(jnp.int32, (WIDE, WIDE), 0) & 15
    eye = (lax.broadcasted_iota(jnp.int32, (40, WIDE), 0) == lane_j).astype(jnp.float32)
    real = lane_j >= 0
    same = (
        (jnp.concatenate(
            [jnp.full((40, WIDE), i, jnp.int32) for i in range(6)] + [jnp.full((16, WIDE), 9, jnp.int32)], axis=0
        ) == lane_i)
        .astype(jnp.float32)
        .astype(jnp.bfloat16)
    )

    def blocks(value):
        parts = [jnp.where(lane_i == i, value, 0.0) for i in range(6)] + [jnp.zeros((16, WIDE), jnp.float32)]
        return split(jnp.concatenate(parts, axis=0))

    def times(values, right):
        right_high, right_low = right
        highs, lows = zip(*[split(value) for value in values])
        count = len(values) * 40
        stack = jnp.concatenate([part.astype(jnp.float32) for part in highs + lows], axis=0).astype(jnp.bfloat16)
        main = bdot(stack, right_high)
        rest = bdot(stack[:count], right_low)
        return [
            main[40 * i:40 * i + 40] + (main[count + 40 * i:count + 40 * i + 40] + rest[40 * i:40 * i + 40])
            for i in range(len(values))
        ]

    uppers, lowers, scales, informs = [], [], [], []
    for group in range(GROUPS):
        expand = (row_c == lane_i + 6 * group).astype(jnp.float32) * real.astype(jnp.float32)
        spread_rows[...] = bdot(picked[...], expand.astype(jnp.bfloat16))
        gram = jnp.zeros((40, WIDE), jnp.float32)
        for j in range(40):
            gram = jnp.where(lane_j == j, spread_rows[40 * j:40 * j + 40], gram)
        informs.append(spread_rows[1600:1640])
        amat = eye + gram * (1.0 / 39)
        square = jnp.sum(amat * amat, axis=0, keepdims=True)
        first = square.astype(jnp.bfloat16).astype(jnp.float32)
        second = (square - first).astype(jnp.bfloat16).astype(jnp.float32)
        third = square - first - second
        parts = jnp.concatenate(
            [jnp.broadcast_to(part, (8, WIDE)) for part in (first, second, third, jnp.zeros_like(third))], axis=0
        )
        norm = bdot(parts.astype(jnp.bfloat16), same)
        norm = norm[0:1] + norm[8:9] + norm[16:17]
        scale = jnp.sqrt(jnp.where(real, norm, 1.0))
        scales.append(scale)
        uppers.append(amat / scale)
    for group in range(GROUPS):
        middle = 1.5 * eye - 0.5 * uppers[group]
        lowers.append(middle)
        uppers[group] = times([uppers[group]], blocks(middle))[0]
    for sweep in range(1, NS):
        middles = []
        for group in range(GROUPS):
            product = times([lowers[group]], blocks(uppers[group]))[0]
            middles.append(blocks(1.5 * eye - 0.5 * product))
        for group in range(GROUPS):
            if sweep < NS - 1:
                uppers[group], lowers[group] = times([uppers[group], lowers[group]], middles[group])
            else:
                lowers[group] = times([lowers[group]], middles[group])[0]
    target = lax.broadcasted_iota(jnp.int32, (WIDE, 768), 1)
    source = lax.broadcasted_iota(jnp.int32, (WIDE, 768), 0)
    own = target & 127
    point = (target >> 7) * 40
    for copy in range(1, 6):
        own = jnp.where((target & 127) >= 20 * copy, (target & 127) - 20 * copy, own)
    chooses = []
    for core in range(2):
        chosen = (source == point + core * 20 + own) & ((target & 127) < 120)
        chooses.append(chosen.astype(jnp.float32).astype(jnp.bfloat16))
    for group in range(GROUPS):
        inv_half = lowers[group] / jnp.sqrt(scales[group])
        step_one = jnp.sum(inv_half * informs[group], axis=0, keepdims=True)
        product = inv_half * step_one
        high, low = split(product)
        stack = jnp.concatenate([high.astype(jnp.float32), low.astype(jnp.float32)], axis=0).astype(jnp.bfloat16)
        moved = bdot(stack, same)
        shift = (moved[:40] + moved[40:]) * (1.0 / 39)
        shift = shift - jnp.sum(shift, axis=0, keepdims=True) * (1.0 / 40)
        spread = inv_half - jnp.sum(inv_half, axis=0, keepdims=True) * (1.0 / 40)
        trans = (1.0 / 40 + shift + spread).astype(jnp.bfloat16)
        for core in range(2):
            chosen = bdot(trans, chooses[core])
            for i in range(6):
                point = group * 6 + i
                if point < 16:
                    rows[core, point * 40:point * 40 + 40, :] = chosen[:, i * 128:i * 128 + 128]


def sixths(shape):
    lane = lax.broadcasted_iota(jnp.int32, shape, 1)
    return [lane >= 20 * p for p in range(6)]


def gather_members(rows):
    after = sixths((16, 128))
    pieces = []
    for q in range(7):
        piece = rows[pl.ds(6 * q, 16, stride=40), :]
        for p in range(1, 6):
            piece = jnp.where(after[p], rows[pl.ds(6 * q + p, 16, stride=40), :], piece)
        pieces.append(piece)
    return jnp.concatenate(pieces, axis=1)


UNROLL = 2


def core_products():
    first, second = [], []
    for high in (4, 3, 2, 1):
        for low in range(high):
            for turn in range(0, 8, 2):
                both = ((low, high, turn), (low, high, turn + 1))
                (first if high > 2 else second).append(both)
    for low in range(5):
        second.append(((low, low, 0), (low, low, 1)))
        second.append(((low, low, 2), (low, low, 3)))
    second.append(((0, 0, 4), (1, 1, 4)))
    second.append(((2, 2, 4), (3, 3, 4)))
    second.append(((0, -1, 0), (1, -1, 0)))
    second.append(((2, -1, 0), (3, -1, 0)))
    second.append(((4, 4, 4), (4, -1, 0)))
    second.append((None, None))
    return first, second


def gram_kernel(
    count_ref, volume_hbm, other_hbm, matrix_hbm, value_ref, error_ref, cell_ref, ab_hbm, c_hbm,
    ab_ref, c_ref,    volume, matrix, wide, anomalies, surprises, weights, lhs0, lhs1, rhs0, rhs1, total, offsets, sems, out_sems,
):
    mem = lax.axis_index("mem")
    chunks = sems.shape[0]
    radar_blocks = matrix.shape[0]
    held = volume_hbm.shape[0]
    tiles = count_ref.shape[1]
    chunk = radar_blocks // chunks
    steps = radar_blocks * SUB // STEP
    per_step = STEP // SUB

    def fetch(index):
        part = pl.ds(index * chunk, chunk)
        return (
            pltpu.make_async_copy(volume_hbm.at[:, part], volume.at[pl.ds(mem * held, held), part], sems.at[index, 0]),
            pltpu.make_async_copy(
                other_hbm.at[:, part], volume.at[pl.ds((1 - mem) * held, held), part], sems.at[index, 1]
            ),
            pltpu.make_async_copy(matrix_hbm.at[part], matrix.at[part], sems.at[index, 2]),
        )

    for index in range(chunks):
        for copy in fetch(index):
            copy.start()

    offsets[0] = 0
    running = jnp.int32(0)
    for tile in range(tiles):
        running = running + count_ref[0, tile]
        offsets[tile + 1] = running
    for extra in range(12):
        offsets[tiles + 1 + extra] = running
    total[...] = jnp.zeros_like(total)
    centre_y = lax.broadcasted_iota(jnp.int32, (16, STEP), 0).astype(jnp.float32) * B + (B - 1) / 2

    def project(index, carry):
        for copy in fetch(index):
            copy.wait()
        part = pl.ds(pl.multiple_of(index * chunk, chunk), chunk)
        for member in range(2 * held):
            wide[member * chunk:member * chunk + chunk, :] = volume[member, part].astype(jnp.float32)
        for inner in range(chunk // per_step):
            step = index * (chunk // per_step) + inner
            here = pl.ds(pl.multiple_of(step * STEP, STEP), STEP)
            cells = cell_ref[:, here]
            pos_x = (cells >> 7).astype(jnp.float32)
            pos_y = (cells & 127).astype(jnp.float32)
            inverse = (1.0 / error_ref[:, here]).astype(jnp.bfloat16).astype(jnp.float32)
            near_y = jnp.exp((pos_y - centre_y) ** 2 * (-0.5 / LOC**2)) * inverse
            for i in range(2):
                near_x = jnp.exp((pos_x - (i * B + (B - 1) / 2)) ** 2 * (-0.5 / LOC**2))
                weights[step, i * 16:i * 16 + 16, :] = (near_x * near_y).astype(jnp.bfloat16)
            values = value_ref[:, here].astype(jnp.float32)
            for sub in range(per_step):
                local = inner * per_step + sub
                block = index * chunk + local
                gates = wide[pl.ds(local, 2 * held, stride=chunk), :].astype(jnp.bfloat16)
                obs = jnp.dot(gates, matrix[block], preferred_element_type=jnp.float32)
                obs = obs.astype(jnp.bfloat16).astype(jnp.float32)
                mean = jnp.sum(obs, axis=0, keepdims=True) * (1.0 / 40)
                anomalies[block] = obs - mean
                surprises[block] = jnp.broadcast_to(values[:, sub * SUB:(sub + 1) * SUB] - mean, (8, SUB))
        return carry

    lax.fori_loop(0, chunks, project, 0)

    lane = lax.broadcasted_iota(jnp.int32, (8, STEP), 1)

    def build(item, lhs, rhs, products):
        step, group = item
        step = jnp.minimum(step, steps - 1)
        for sub in range(per_step):
            block = step * per_step + sub
            lanes = slice(sub * SUB, (sub + 1) * SUB)
            part = [
                anomalies[block, 8 * i:8 * i + 8, :].astype(jnp.bfloat16).astype(jnp.float32) for i in range(5)
            ]
            made = {}

            def operand(kind, entry):
                low, high, turn = entry
                if kind == 0:
                    return part[low]
                if high < 0:
                    return surprises[block]
                if (high, turn) not in made:
                    made[high, turn] = part[high] if turn == 0 else pltpu.roll(part[high], turn, 0)
                return made[high, turn]

            packed = {}

            def pack(kind, both):
                key = tuple((kind, entry[0]) if kind == 0 else (kind, entry[1:]) for entry in both)
                if key not in packed:
                    packed[key] = jnp.concatenate([operand(kind, entry) for entry in both], axis=0).astype(jnp.bfloat16)
                return packed[key]

            for index, both in enumerate(products):
                if both[0] is None:
                    continue
                lhs[index * 16:index * 16 + 16, lanes] = pack(0, both) * pack(1, both)
        slot = lane + step * STEP
        reached = [jnp.where(slot >= offsets[group * 4 + i], 1.0, 0.0) for i in range(9)]
        weight = weights[step]
        for i in range(8):
            inside = reached[i] - reached[i + 1]
            inside = jnp.concatenate([inside, inside], axis=0).astype(jnp.bfloat16)
            for half in range(2):
                rhs[i * 32 + half * 16:i * 32 + half * 16 + 16, :] = weight[half * 16:half * 16 + 16] * inside

    def use(group, lhs, rhs):
        added = lax.dot_general(
            lhs[...], rhs[...], (((1,), (1,)), ((), ())), preferred_element_type=jnp.float32
        )
        total[group] += added[:, :128]
        total[group + 1] += added[:, 128:]

    def follow(item):
        step, group = item
        end = (step + 1) * STEP
        again = (group + 2 < tiles // 4) & (offsets[group * 4 + 8] < end)
        ahead = (offsets[group * 4 + 4] <= end).astype(jnp.int32) + (offsets[group * 4 + 8] <= end).astype(jnp.int32)
        next_step = jnp.where(again, step, step + 1)
        next_group = jnp.where(again, group + 2, group + ahead)
        return next_step, jnp.where(next_step >= steps, tiles // 4, next_group)

    for core, products in enumerate(core_products()):

        @pl.when(mem == core)
        def _():
            if products[-1][0] is None:
                lhs0[len(products) * 16 - 16:, :] = jnp.zeros((16, STEP), jnp.bfloat16)
                lhs1[len(products) * 16 - 16:, :] = jnp.zeros((16, STEP), jnp.bfloat16)
            start = (jnp.int32(0), jnp.int32(0))
            build(start, lhs0, rhs0, products)

            def body(item):
                for turn in range(UNROLL):
                    lhs, rhs = (lhs0, rhs0) if turn % 2 == 0 else (lhs1, rhs1)
                    other_lhs, other_rhs = (lhs1, rhs1) if turn % 2 == 0 else (lhs0, rhs0)
                    following = follow(item)
                    use(item[1], lhs, rhs)
                    build(following, other_lhs, other_rhs, products)
                    item = following
                return item

            lax.while_loop(lambda item: item[0] < steps, body, start)

    results = []
    for x in range(4):
        for y in range(4):
            ab_ref[x, y] = total[x * 4 + y, :PART_A + PART_B].astype(jnp.bfloat16)
        for z, value in enumerate(block_swap([total[x * 4 + y, PART_A + PART_B:] for y in range(4)])):
            c_ref[z, x] = value.astype(jnp.bfloat16)
        results.append(pltpu.make_async_copy(ab_ref.at[x], ab_hbm.at[x], out_sems.at[2 * x]))
        results.append(pltpu.make_async_copy(c_ref.at[:, x], c_hbm.at[:, x], out_sems.at[2 * x + 1]))
        for copy in results[-2:]:
            copy.start()
    for copy in results:
        copy.wait()


def gram(counts, volume, other, matrix, values, errors, cells):
    blocks = matrix.shape[0]
    tiles = counts.shape[1]
    members = 2 * volume.shape[0]
    rows = PART_A + PART_B + PART_C
    steps = blocks * SUB // STEP
    vmem = pl.BlockSpec(memory_space=pltpu.VMEM)
    hbm = pl.BlockSpec(memory_space=pl.ANY)
    return pl.pallas_call(
        gram_kernel,
        out_shape=(
            jax.ShapeDtypeStruct((4, 4, PART_A + PART_B, 128), jnp.bfloat16),
            jax.ShapeDtypeStruct((4, 4, PART_C, 128), jnp.bfloat16),
        ),
        in_specs=[pl.BlockSpec(memory_space=pltpu.SMEM), hbm, hbm, hbm, vmem, vmem, vmem],
        out_specs=(hbm, hbm),
        scratch_shapes=[
            pltpu.VMEM((4, 4, PART_A + PART_B, 128), jnp.bfloat16),
            pltpu.VMEM((4, 4, PART_C, 128), jnp.bfloat16),
            pltpu.VMEM((members, blocks, 128), jnp.bfloat16),
            pltpu.VMEM((blocks, 128, 128), jnp.bfloat16),
            pltpu.VMEM((members * (blocks // CHUNKS), 128), jnp.float32),
            pltpu.VMEM((blocks, members, 128), jnp.float32),
            pltpu.VMEM((blocks, 8, 128), jnp.float32),
            pltpu.VMEM((steps, 32, STEP), jnp.bfloat16),
            pltpu.VMEM((rows, STEP), jnp.bfloat16),
            pltpu.VMEM((rows, STEP), jnp.bfloat16),
            pltpu.VMEM((256, STEP), jnp.bfloat16),
            pltpu.VMEM((256, STEP), jnp.bfloat16),
            pltpu.VMEM((tiles // 4 + 2, rows, 128), jnp.float32),
            pltpu.SMEM((tiles + 13,), jnp.int32),
            pltpu.SemaphoreType.DMA((CHUNKS, 3)),
            pltpu.SemaphoreType.DMA((8,)),
        ],
        compiler_params=pltpu.CompilerParams(vmem_limit_bytes=60 * 1024 * 1024),
        name="gram",
    )(counts, volume, other, matrix, values, errors, cells)


def apply_kernel(points_ref, tent_x_ref, tent_y_ref, state_hbm, other_hbm, out_ref, states, fine, flat, result, sems):
    levels, width_x, width_y = state_hbm.shape[1:]
    own = out_ref.shape[0]
    members = 2 * own
    mem, tx, ty = lax.axis_index("mem"), lax.axis_index("tx"), lax.axis_index("ty")
    copies = []
    for index, source in enumerate((state_hbm, other_hbm)):
        copies.append(pltpu.make_async_copy(source, states.at[index], sems.at[index]))
        copies[index].start()
    kind_x = jnp.where(tx == 0, 0, jnp.where(tx == lax.axis_size("tx") - 1, 2, 1))
    kind_y = jnp.where(ty == 0, 0, jnp.where(ty == lax.axis_size("ty") - 1, 2, 1))
    tent_x, tent_y = tent_x_ref[kind_x], tent_y_ref[kind_y]
    points = points_ref[...].astype(jnp.float32)
    points = jnp.concatenate([points, jnp.zeros((48, points.shape[1]), jnp.float32)], axis=0).T
    points = points[:, :80].astype(jnp.bfloat16)

    for x in range(0, width_x, 2):
        tent = jnp.concatenate(
            [tent_x[:, x + i:x + i + 1] * tent_y for i in range(2)], axis=1
        ).astype(jnp.bfloat16)
        made = jnp.dot(points, tent, preferred_element_type=jnp.float32)
        fine[x] = made[:, :128]
        fine[x + 1] = made[:, 128:]

    for copy in copies:
        copy.wait()

    def widen(member, carry):
        for index, first in enumerate((mem * own, (1 - mem) * own)):
            start = pl.multiple_of((first + member) * levels * width_x, 8)
            flat[pl.ds(start, levels * width_x), :] = (
                states[index, member].astype(jnp.float32).reshape(levels * width_x, width_y)
            )
        return carry

    lax.fori_loop(0, own, widen, 0)

    def column(x, carry):
        def add(step, sums):
            sums = list(sums)
            for inner in range(20):
                k = step * 20 + inner
                field = flat[pl.ds(k * (levels * width_x) + x, levels, stride=width_x), :]
                place = sum(
                    jnp.where(step == turn, (it // 6) * 128 + (it % 6) * 20, 0)
                    for turn, it in enumerate(range(inner, members, 20))
                )
                for j in range(own):
                    row = fine[x, pl.ds(place + j, 8, stride=0), :]
                    sums[j] = sums[j] + row * field
            return tuple(sums)

        zero = jnp.zeros((levels, width_y), jnp.float32)
        sums = lax.fori_loop(0, members // 20, add, (zero,) * own)
        for j in range(own):
            result[pl.ds(j * (levels * width_x) + x, levels, stride=width_x), :] = sums[j]
        return carry

    lax.fori_loop(0, width_x, column, 0)

    def narrow(j, carry):
        start = pl.multiple_of(j * levels * width_x, 8)
        out_ref[j] = (
            result[pl.ds(start, levels * width_x), :]
            .reshape(levels, width_x, width_y)
            .astype(jnp.bfloat16)
        )
        return carry

    lax.fori_loop(0, own, narrow, 0)


def apply(points, tent_x, tent_y, state, other):
    own, levels, width_x, width_y = state.shape
    members = 2 * own
    return pl.pallas_call(
        apply_kernel,
        out_shape=jax.ShapeDtypeStruct((own, levels, width_x, width_y), jnp.bfloat16),
        in_specs=[pl.BlockSpec(memory_space=pltpu.VMEM)] * 3 + [pl.BlockSpec(memory_space=pl.ANY)] * 2,
        out_specs=pl.BlockSpec(memory_space=pltpu.VMEM),
        scratch_shapes=[
            pltpu.VMEM((2,) + state.shape, state.dtype),
            pltpu.VMEM((width_x, points.shape[1], width_y), jnp.float32),
            pltpu.VMEM((members * levels * width_x, width_y), jnp.float32),
            pltpu.VMEM((own * levels * width_x, width_y), jnp.float32),
            pltpu.SemaphoreType.DMA((2,)),
        ],
        compiler_params=pltpu.CompilerParams(vmem_limit_bytes=60 * 1024 * 1024),
        name="apply",
    )(points, tent_x, tent_y, state, other)


def swap_kernel(volume_ref, other_ref, send, recv):
    mem = lax.axis_index("mem")
    mate = (lax.axis_index("tx"), lax.axis_index("ty"), 1 - mem)
    barrier = pltpu.get_barrier_semaphore()
    pl.semaphore_signal(barrier, inc=1, device_id=mate, device_id_type=MESH)
    pl.semaphore_wait(barrier, 1)
    count = send.shape[0]
    share = volume_ref.shape[0] // count
    copies = []
    for index in range(count):
        part = pl.ds(index * share, share)
        copies.append(
            pltpu.make_async_remote_copy(
                src_ref=volume_ref.at[part], dst_ref=other_ref.at[part], send_sem=send.at[index],
                recv_sem=recv.at[index], device_id=mate, device_id_type=MESH,
            )
        )
    for copy in copies:
        copy.start()
    for copy in copies:
        copy.wait()


def swap(volume):
    return pl.pallas_call(
        swap_kernel,
        out_shape=jax.ShapeDtypeStruct(volume.shape, volume.dtype),
        in_specs=[pl.BlockSpec(memory_space=pl.ANY)],
        out_specs=pl.BlockSpec(memory_space=pl.ANY),
        scratch_shapes=[pltpu.SemaphoreType.DMA((4,)), pltpu.SemaphoreType.DMA((4,))],
        compiler_params=pltpu.CompilerParams(
            collective_id=0, has_side_effects=True, vmem_limit_bytes=60 * 1024 * 1024
        ),
        name="swap",
    )(volume)


def coarse_kernel(
    ab_ref, c_ref, pick_ref, eighth_ref, lane_ref, state_ref, points_ref, other_ref,
    whole_ab, whole_c, pass_a, pass_b, pass_c, via_a, via_b, via_c, got_a, got_b, got_c,
    next_a, next_b, next_c, got_a2, got_b2, got_c2, last_a, last_b, last_c, got_a3, got_b3, got_c3,
    folded, summed, pick, eighth, picked, spread_rows, rows, edges, columns, halo, corners,
    send, recv, local,
):
    x, ty, mem = lax.axis_index("tx"), lax.axis_index("ty"), lax.axis_index("mem")
    y, z = ty // 4, ty % 4
    spot = (x, y, z)

    def along(axis, turn, core=None):
        core = mem if core is None else core
        if axis == 0:
            return ((x + turn) % 4, ty, core)
        if axis == 1:
            return (x, ((y + turn) % 4) * 4 + z, core)
        return (x, y * 4 + (z + turn) % 4, core)

    mate = (x, ty, 1 - mem)
    ahead = 2 * mem - 1
    around = []
    for step in (1, 15):
        for core in range(2):
            around.append(((x, (ty + step) % 16, core), (((x + ahead) + 4) % 4, (ty + step) % 16, core)))
    peers = [along(axis, turn, core) for axis in range(3) for turn in range(1, 4) for core in (mem, 1 - mem)]
    peers += [mate] + [device for pair in around for device in pair]
    peers += [(((x - ahead) + 4) % 4, (ty + step) % 16, mem) for step in (1, 15)]
    barrier = pltpu.get_barrier_semaphore()
    for device in peers:
        pl.semaphore_signal(barrier, inc=1, device_id=device, device_id_type=MESH)

    parts = (
        (0, lambda place, blocks, first, size: whole_ab.at[place, blocks, pl.ds(first, size)], PART_A),
        (1, lambda place, blocks, first, size: whole_ab.at[blocks, place, pl.ds(PART_A + first, size)], PART_B),
        (2, lambda place, blocks, first, size: whole_c.at[place, blocks, pl.ds(first, size)], PART_C),
    )
    passes, vias, gots = (pass_a, pass_b, pass_c), (via_a, via_b, via_c), (got_a, got_b, got_c)
    fetched = [
        pltpu.make_async_copy(ab_ref, whole_ab, local.at[0]),
        pltpu.make_async_copy(c_ref, whole_c, local.at[1]),
    ]
    for copy in fetched:
        copy.start()
    tables = [
        pltpu.make_async_copy(pick_ref, pick, local.at[2]),
        pltpu.make_async_copy(eighth_ref, eighth, local.at[3]),
    ]
    for copy in tables:
        copy.start()
    for index in (0, 5, 6, 11):
        corners[index * 16:index * 16 + 16, :] = jnp.zeros((16, 128), jnp.float32)
    corners[192:256, :] = jnp.zeros((64, 128), jnp.float32)
    for core in range(2):
        rows[core, 640:, :] = jnp.zeros((rows.shape[1] - 640, 128), jnp.float32)
    for copy in fetched:
        copy.wait()
    pl.semaphore_wait(barrier, len(peers))

    started = []

    def link(source, target, index, device, landing=None):
        copy = pltpu.make_async_remote_copy(
            src_ref=source, dst_ref=target, send_sem=send.at[index],
            recv_sem=recv.at[index if landing is None else landing], device_id=device, device_id_type=MESH,
        )
        copy.start()
        started.append(copy)
        return copy

    relays, plains, finals = [[], [], []], [], [[], [], []]
    every, halves = pl.ds(0, 4), (pl.ds(0, 2), pl.ds(2, 2))
    for turn, blocks in enumerate(halves):
        for index, (axis, piece, size) in enumerate(parts):
            half = size // 2
            opposite = (spot[axis] + 2) % 4
            relays[index].append(
                [
                    link(
                        piece(opposite, blocks, way * half, half), vias[index].at[way, blocks],
                        68 + 4 * index + 2 * turn + way, along(axis, 1 + 2 * way),
                    )
                    for way in range(2)
                ]
            )
    for index, (axis, piece, size) in enumerate(parts):
        half = size // 2
        up, down = (spot[axis] + 1) % 4, (spot[axis] + 3) % 4
        plains.append(
            [
                link(piece(up, every, half, half), gots[index].at[0, :, pl.ds(half, half)], 2 * index, along(axis, 1)),
                link(piece(down, every, 0, half), gots[index].at[1, :, pl.ds(0, half)], 2 * index + 1, along(axis, 3)),
            ]
        )
    state_copy = link(state_ref, other_ref, 18, mate)
    for turn, blocks in enumerate(halves):
        for index, (axis, piece, size) in enumerate(parts):
            half = size // 2
            for way in range(2):
                relays[index][turn][way].wait_recv()
                own = piece((spot[axis] + 1 + 2 * way) % 4, every, way * half, half)
                for block in (2 * turn, 2 * turn + 1):
                    passes[index][way, block] = (
                        own[block].astype(jnp.float32) + vias[index][way, block].astype(jnp.float32)
                    ).astype(jnp.bfloat16)
                target = gots[index].at[way, blocks, pl.ds(way * half, half)]
                finals[index].append(
                    link(
                        passes[index].at[way, blocks], target, 6 + 4 * index + 2 * turn + way,
                        along(axis, 1 + 2 * way),
                    )
                )

    def arrive(index):
        for copy in plains[index] + finals[index]:
            copy.wait_recv()

    def add_up(index, block):
        axis, piece, size = parts[index]
        value = piece(spot[axis], every, 0, size)[block].astype(jnp.float32)
        for way in range(2):
            value = value + gots[index][way, block].astype(jnp.float32)
        return value

    def stage(first, axis, source, target):
        copies = []
        for turn in (2, 1, 3):
            place = (spot[axis] + turn) % 4
            copies.append(link(source.at[place], target.at[turn - 1], first + turn - 1, along(axis, turn)))
        return copies

    def wait_all(copies):
        for copy in copies:
            copy.wait_recv()

    def add_last(own, got):
        value = own.astype(jnp.float32)
        for turn in range(3):
            value = value + got[turn].astype(jnp.float32)
        return value

    arrive(0)
    for block in range(4):
        next_a[block] = add_up(0, block).astype(jnp.bfloat16)
    second_a = stage(19, 1, next_a, got_a2)
    arrive(1)
    for block, value in enumerate(block_swap([add_up(1, block) for block in range(4)])):
        next_b[block] = value.astype(jnp.bfloat16)
    second_b = stage(22, 2, next_b, got_b2)
    arrive(2)
    for block in range(4):
        next_c[block] = add_up(2, block).astype(jnp.bfloat16)
    second_c = stage(25, 0, next_c, got_c2)

    def fold(value, target):
        size = value.shape[0] // 8
        folded[0:value.shape[0], :] = value
        pieces = [folded[i * size:(i + 1) * size, :] for i in range(8)]
        for index, part in enumerate(block_swap(pieces)):
            target[index] = part

    def third(number, axis, source, target):
        first = 28 + 8 * number
        for turn in (2, 1, 3, 0):
            place = (spot[axis] + turn) % 4
            for other in range(2):
                if turn == 0 and other == 0:
                    continue
                core = 1 - mem if other else mem
                link(
                    source.at[place * 2 + core], target.at[mem * 4 + turn], first + 2 * turn + other,
                    along(axis, turn, core), first + 2 * turn + mem,
                )
        target[mem * 4] = source[spot[axis] * 2 + mem]

    def sum_third(number, source, target, row):
        first = 28 + 8 * number

        def landed(core, turn):
            pltpu.make_async_remote_copy(
                src_ref=source.at[0], dst_ref=target.at[core * 4 + turn], send_sem=send.at[first],
                recv_sem=recv.at[first + 2 * turn + core], device_id=mate, device_id_type=MESH,
            ).wait_recv()

        landed(1 - mem, 0)
        for turn in range(1, 4):
            for core in range(2):
                landed(core, turn)
        size = source.shape[1]
        for core in range(2):
            value = target[core * 4]
            for turn in range(1, 4):
                value = value + target[core * 4 + turn]
            summed[core * 56 + row:core * 56 + row + size, :] = value

    wait_all(second_a)
    fold(add_last(next_a[y], got_a2), last_a)
    third(0, 2, last_a, got_a3)
    wait_all(second_b)
    fold(add_last(next_b[z], got_b2), last_b)
    third(1, 0, last_b, got_b3)
    wait_all(second_c)
    fold(add_last(next_c[x], got_c2), last_c)
    third(2, 1, last_c, got_c3)
    sum_third(0, last_a, got_a3, 0)
    sum_third(1, last_b, got_b3, 20)
    sum_third(2, last_c, got_c3, 40)

    for copy in tables:
        copy.wait()
    coarse_points(summed[...], pick, eighth, lane_ref, picked, spread_rows, rows)

    after = sixths((16, 128))
    for core in range(2):
        for side in range(2):
            point = 15 * (1 - side)
            value = rows[core, pl.ds(point * 40, 16, stride=6), :]
            for p in range(1, 6):
                value = jnp.where(after[p], rows[core, pl.ds(point * 40 + p, 16, stride=6), :], value)
            columns[core, side] = value
    outer = jnp.where(mem == 1, 0, 2)
    for index, (straight, slanted) in enumerate(around):
        side, core = index // 2, index % 2
        for device, turn in ((straight, 1), (slanted, outer)):
            slot = (side * 3 + turn) * 2 + mem
            link(
                columns.at[core, side], corners.at[pl.ds(slot * 16, 16)],
                52 + 2 * index + (1 if device is slanted else 0), device, 52 + slot,
            )
    for core in range(2):
        edges[core] = gather_members(rows.at[core]).astype(jnp.bfloat16)
    link(edges.at[1 - mem], halo.at[mem], 60, mate, 64 + mem)
    for other in range(2):
        core = 1 - mem if other else mem
        link(edges.at[core], halo.at[3 - mem], 61 + other, ((x + ahead + 4) % 4, ty, core), 64 + 3 - mem)
    points_ref[pl.ds(pl.multiple_of(mem * 16, 16), 16), :] = edges[mem]

    def landed(source, target, index):
        pltpu.make_async_remote_copy(
            src_ref=source, dst_ref=target, send_sem=send.at[0], recv_sem=recv.at[index],
            device_id=mate, device_id_type=MESH,
        ).wait_recv()

    for slot in (1, 2, 3, 4, 7, 8, 9, 10):
        landed(columns.at[0, 0], corners.at[pl.ds(slot * 16, 16)], 52 + slot)
    for q in range(7):
        points_ref[64:80, q * 128:q * 128 + 128] = corners[pl.ds(q, 16, stride=16), :].astype(jnp.bfloat16)
    landed(edges.at[0], halo.at[1 - mem], 64 + 1 - mem)
    points_ref[pl.ds(pl.multiple_of((1 - mem) * 16, 16), 16), :] = halo[1 - mem]
    for slot in (2, 3):
        landed(edges.at[0], halo.at[slot], 64 + slot)
        points_ref[slot * 16:slot * 16 + 16, :] = halo[slot]
    state_copy.wait_recv()
    for copy in started:
        copy.wait_send()


def coarse(partial_ab, partial_c, state):
    pick, eighth = pick_tables()
    bf16, f32 = jnp.bfloat16, jnp.float32
    sizes = (PART_A, PART_B, PART_C)
    hbm, vmem = pl.BlockSpec(memory_space=pl.ANY), pl.BlockSpec(memory_space=pltpu.VMEM)
    return pl.pallas_call(
        coarse_kernel,
        out_shape=(
            jax.ShapeDtypeStruct((80, LINK_LANES), bf16),
            jax.ShapeDtypeStruct(state.shape, state.dtype),
        ),
        in_specs=[hbm, hbm, hbm, hbm, vmem, hbm],
        out_specs=(vmem, hbm),
        scratch_shapes=[pltpu.VMEM((4, 4, PART_A + PART_B, 128), bf16), pltpu.VMEM((4, 4, PART_C, 128), bf16)]
        + [pltpu.VMEM((2, 4, size // 2, 128), bf16) for size in sizes]
        + [pltpu.VMEM((2, 4, size // 2, 128), bf16) for size in sizes]
        + [pltpu.VMEM((2, 4, size, 128), bf16) for size in sizes]
        + [pltpu.VMEM((4, size, 128), bf16) for size in sizes]
        + [pltpu.VMEM((3, size, 128), bf16) for size in sizes]
        + [pltpu.VMEM((8, size // 8, 128), f32) for size in sizes]
        + [pltpu.VMEM((8, size // 8, 128), f32) for size in sizes]
        + [
            pltpu.VMEM((PART_A, 128), f32),
            pltpu.VMEM((112, 128), f32),
            pltpu.VMEM((1648, 128), bf16),
            pltpu.VMEM((1648, 128), bf16),
            pltpu.VMEM((1648, WIDE), bf16),
            pltpu.VMEM((1648, WIDE), f32),
            pltpu.VMEM((2, 704, 128), f32),
            pltpu.VMEM((2, 16, LINK_LANES), bf16),
            pltpu.VMEM((2, 2, 16, 128), f32),
            pltpu.VMEM((4, 16, LINK_LANES), bf16),
            pltpu.VMEM((256, 128), f32),
            pltpu.SemaphoreType.DMA((80,)),
            pltpu.SemaphoreType.DMA((80,)),
            pltpu.SemaphoreType.DMA((4,)),
        ],
        compiler_params=pltpu.CompilerParams(
            collective_id=1, has_side_effects=True, vmem_limit_bytes=60 * 1024 * 1024
        ),
        name="coarse",
    )(partial_ab, partial_c, jnp.asarray(pick), jnp.asarray(eighth), jnp.asarray(lane_table()), state)


def tent(length, nodes):
    position = np.arange(length, dtype=np.float32)[:, None]
    centre = (np.arange(nodes, dtype=np.float32)[None, :] - 1.0) * B + (B - 1) * 0.5
    return np.maximum(0.0, 1.0 - np.abs(position - centre) / B)


def tent_tables():
    place_x, place_y = np.full(80, -1), np.full(80, -1)
    for i in range(2):
        for j in range(16):
            place_x[i * 16 + j], place_y[i * 16 + j] = i + 1, j + 1
            place_x[32 + i * 16 + j], place_y[32 + i * 16 + j] = 3 * i, j + 1
    for side in range(2):
        for turn in range(3):
            for i in range(2):
                row = 64 + (side * 3 + turn) * 2 + i
                place_y[row] = 17 * side
                place_x[row] = {1: i + 1, 0: 0 if i == 1 else -1, 2: 3 if i == 0 else -1}[turn]
    tables = []
    for length, nodes, place in ((16, 4, place_x), (128, 18, place_y)):
        table = np.zeros((3, 80, length), np.float32)
        for kind in range(3):
            weights = tent(length, nodes)
            if kind == 0:
                weights[:, 1] += weights[:, 0]
                weights[:, 0] = 0
            if kind == 2:
                weights[:, -2] += weights[:, -1]
                weights[:, -1] = 0
            for row in range(80):
                if place[row] >= 0:
                    table[kind, row] = weights[:, place[row]]
        tables.append(table)
    return tables


def per_device(volume, super_matrix, observed, error_var, obs_cells, counts, state):
    other_volume = swap(volume[0])
    partial_ab, partial_c = gram(counts, volume[0], other_volume, super_matrix[0], observed, error_var, obs_cells)
    points, other_state = coarse(partial_ab, partial_c, state)
    tent_x, tent_y = tent_tables()
    return apply(points, jnp.asarray(tent_x), jnp.asarray(tent_y), state, other_state)


def solution(mesh):
    placed = (
        P(("tx", "ty"), "mem", None, None),
        P(("tx", "ty"), None, None, None),
        P(("tx", "ty"), None),
        P(("tx", "ty"), None),
        P(("tx", "ty"), None),
        P(("tx", "ty"), None),
        P("mem", None, "tx", "ty"),
    )
    return jax.shard_map(
        per_device,
        mesh=mesh,
        in_specs=placed,
        out_specs=P("mem", None, "tx", "ty"),
        check_vma=False,
    )
```

```python
import numpy as np
import jax
import jax.numpy as jnp
from jax import lax
from jax.experimental import pallas as pl
from jax.experimental.pallas import tpu as pltpu
from jax.sharding import PartitionSpec as P

B = 8
LOC = 16
NS = 5
STEP = 768
SUB = 128
CHUNKS = 4


MESH = pl.DeviceIdType.MESH
PART_A, PART_B, PART_C = 160, 160, 128
GROUPS = 3
WIDE = 256
LINK_LANES = 896


def place_of(row):
    if row < PART_A:
        return row % (PART_A // 8), row // (PART_A // 8)
    row -= PART_A
    if row < PART_B:
        return PART_A // 8 + row % (PART_B // 8), row // (PART_B // 8)
    row -= PART_B
    return (PART_A + PART_B) // 8 + row % (PART_C // 8), row // (PART_C // 8)


def pick_tables():
    rows = np.zeros((1648, 128), np.float32)
    eighths = np.zeros((1648, 128), np.float32)

    def put(target, core, local):
        row, eighth = place_of(local)
        rows[target] = 0
        eighths[target] = 0
        rows[target, core * 56 + row] = 1
        eighths[target, eighth * 16:eighth * 16 + 16] = 1

    for core, products in enumerate(core_products()):
        for index, entry in enumerate([entry for both in products for entry in both]):
            if entry is None:
                continue
            low, high, turn = entry
            for s in range(8):
                if high < 0:
                    put(1600 + 8 * low + s, core, index * 8 + s)
                    continue
                k, j = 8 * low + s, 8 * high + (s - turn) % 8
                put(j * 40 + k, core, index * 8 + s)
                put(k * 40 + j, core, index * 8 + s)
    return rows.astype(jnp.bfloat16), eighths.astype(jnp.bfloat16)


def lane_table():
    lanes = np.arange(WIDE)
    table = np.full((8, WIDE), -1, np.int32)
    table[0] = np.where(lanes < 240, lanes // 40, 7)
    table[1] = np.where(lanes < 240, lanes % 40, -1)
    return table


def block_swap(arrays):
    lane = lax.broadcasted_iota(jnp.int32, arrays[0].shape, 1)
    count = len(arrays)
    step = count // 2
    while step:
        width = step * (128 // count)
        mask = (lane & width) == 0
        turned = list(arrays)
        for low in range(count):
            if low & step:
                continue
            first, second = arrays[low], arrays[low + step]
            turned[low] = jnp.where(mask, first, pltpu.roll(second, width, 1))
            turned[low + step] = jnp.where(mask, pltpu.roll(first, 128 - width, 1), second)
        arrays = turned
        step //= 2
    return arrays


def split(value):
    high = value.astype(jnp.bfloat16)
    return high, (value - high.astype(jnp.float32)).astype(jnp.bfloat16)


def bdot(left, right):
    return jnp.dot(left, right, preferred_element_type=jnp.float32)


def coarse_points(summed, pick_ref, eighth_ref, lane_ref, picked, spread_rows, rows):
    lane_i, lane_j = lane_ref[0:1], lane_ref[1:2]
    high, low = split(summed)
    both = jnp.concatenate([high, low], axis=1)
    both = jnp.concatenate([both, jnp.zeros((16, WIDE), jnp.bfloat16)], axis=0)
    eighths = eighth_ref[...].astype(jnp.float32)
    found = bdot(pick_ref[...], both)
    picked[...] = jnp.concatenate(
        [found[:, :128] * eighths, found[:, 128:] * eighths], axis=1
    ).astype(jnp.bfloat16)
    row_c = lax.broadcasted_iota(jnp.int32, (WIDE, WIDE), 0) & 15
    eye = (lax.broadcasted_iota(jnp.int32, (40, WIDE), 0) == lane_j).astype(jnp.float32)
    real = lane_j >= 0
    same = (
        (jnp.concatenate(
            [jnp.full((40, WIDE), i, jnp.int32) for i in range(6)] + [jnp.full((16, WIDE), 9, jnp.int32)], axis=0
        ) == lane_i)
        .astype(jnp.float32)
        .astype(jnp.bfloat16)
    )

    def blocks(value):
        parts = [jnp.where(lane_i == i, value, 0.0) for i in range(6)] + [jnp.zeros((16, WIDE), jnp.float32)]
        return split(jnp.concatenate(parts, axis=0))

    def times(values, right):
        right_high, right_low = right
        highs, lows = zip(*[split(value) for value in values])
        count = len(values) * 40
        stack = jnp.concatenate([part.astype(jnp.float32) for part in highs + lows], axis=0).astype(jnp.bfloat16)
        main = bdot(stack, right_high)
        rest = bdot(stack[:count], right_low)
        return [
            main[40 * i:40 * i + 40] + (main[count + 40 * i:count + 40 * i + 40] + rest[40 * i:40 * i + 40])
            for i in range(len(values))
        ]

    uppers, lowers, scales, informs = [], [], [], []
    for group in range(GROUPS):
        expand = (row_c == lane_i + 6 * group).astype(jnp.float32) * real.astype(jnp.float32)
        spread_rows[...] = bdot(picked[...], expand.astype(jnp.bfloat16))
        gram = jnp.zeros((40, WIDE), jnp.float32)
        for j in range(40):
            gram = jnp.where(lane_j == j, spread_rows[40 * j:40 * j + 40], gram)
        informs.append(spread_rows[1600:1640])
        amat = eye + gram * (1.0 / 39)
        square = jnp.sum(amat * amat, axis=0, keepdims=True)
        first = square.astype(jnp.bfloat16).astype(jnp.float32)
        second = (square - first).astype(jnp.bfloat16).astype(jnp.float32)
        third = square - first - second
        parts = jnp.concatenate(
            [jnp.broadcast_to(part, (8, WIDE)) for part in (first, second, third, jnp.zeros_like(third))], axis=0
        )
        norm = bdot(parts.astype(jnp.bfloat16), same)
        norm = norm[0:1] + norm[8:9] + norm[16:17]
        scale = jnp.sqrt(jnp.where(real, norm, 1.0))
        scales.append(scale)
        uppers.append(amat / scale)
    for group in range(GROUPS):
        middle = 1.5 * eye - 0.5 * uppers[group]
        lowers.append(middle)
        uppers[group] = times([uppers[group]], blocks(middle))[0]
    for sweep in range(1, NS):
        middles = []
        for group in range(GROUPS):
            product = times([lowers[group]], blocks(uppers[group]))[0]
            middles.append(blocks(1.5 * eye - 0.5 * product))
        for group in range(GROUPS):
            if sweep < NS - 1:
                uppers[group], lowers[group] = times([uppers[group], lowers[group]], middles[group])
            else:
                lowers[group] = times([lowers[group]], middles[group])[0]
    target = lax.broadcasted_iota(jnp.int32, (WIDE, 768), 1)
    source = lax.broadcasted_iota(jnp.int32, (WIDE, 768), 0)
    own = target & 127
    point = (target >> 7) * 40
    for copy in range(1, 6):
        own = jnp.where((target & 127) >= 20 * copy, (target & 127) - 20 * copy, own)
    chooses = []
    for core in range(2):
        chosen = (source == point + core * 20 + own) & ((target & 127) < 120)
        chooses.append(chosen.astype(jnp.float32).astype(jnp.bfloat16))
    for group in range(GROUPS):
        inv_half = lowers[group] / jnp.sqrt(scales[group])
        step_one = jnp.sum(inv_half * informs[group], axis=0, keepdims=True)
        product = inv_half * step_one
        high, low = split(product)
        stack = jnp.concatenate([high.astype(jnp.float32), low.astype(jnp.float32)], axis=0).astype(jnp.bfloat16)
        moved = bdot(stack, same)
        shift = (moved[:40] + moved[40:]) * (1.0 / 39)
        shift = shift - jnp.sum(shift, axis=0, keepdims=True) * (1.0 / 40)
        spread = inv_half - jnp.sum(inv_half, axis=0, keepdims=True) * (1.0 / 40)
        trans = (1.0 / 40 + shift + spread).astype(jnp.bfloat16)
        for core in range(2):
            chosen = bdot(trans, chooses[core])
            for i in range(6):
                point = group * 6 + i
                if point < 16:
                    rows[core, point * 40:point * 40 + 40, :] = chosen[:, i * 128:i * 128 + 128]


def sixths(shape):
    lane = lax.broadcasted_iota(jnp.int32, shape, 1)
    return [lane >= 20 * p for p in range(6)]


def gather_members(rows):
    after = sixths((16, 128))
    pieces = []
    for q in range(7):
        piece = rows[pl.ds(6 * q, 16, stride=40), :]
        for p in range(1, 6):
            piece = jnp.where(after[p], rows[pl.ds(6 * q + p, 16, stride=40), :], piece)
        pieces.append(piece)
    return jnp.concatenate(pieces, axis=1)


UNROLL = 2


def core_products():
    first, second = [], []
    for high in (4, 3, 2, 1):
        for low in range(high):
            for turn in range(0, 8, 2):
                both = ((low, high, turn), (low, high, turn + 1))
                (first if high > 2 else second).append(both)
    for low in range(5):
        second.append(((low, low, 0), (low, low, 1)))
        second.append(((low, low, 2), (low, low, 3)))
    second.append(((0, 0, 4), (1, 1, 4)))
    second.append(((2, 2, 4), (3, 3, 4)))
    second.append(((0, -1, 0), (1, -1, 0)))
    second.append(((2, -1, 0), (3, -1, 0)))
    second.append(((4, 4, 4), (4, -1, 0)))
    second.append((None, None))
    return first, second


def gram_kernel(
    count_ref, volume_hbm, other_hbm, matrix_hbm, value_ref, error_ref, cell_ref, ab_hbm, c_hbm,
    ab_ref, c_ref,    volume, matrix, wide, anomalies, surprises, weights, lhs0, lhs1, rhs0, rhs1, total, offsets, sems, out_sems,
):
    mem = lax.axis_index("mem")
    chunks = sems.shape[0]
    radar_blocks = matrix.shape[0]
    held = volume_hbm.shape[0]
    tiles = count_ref.shape[1]
    chunk = radar_blocks // chunks
    steps = radar_blocks * SUB // STEP
    per_step = STEP // SUB

    def fetch(index):
        part = pl.ds(index * chunk, chunk)
        return (
            pltpu.make_async_copy(volume_hbm.at[:, part], volume.at[pl.ds(mem * held, held), part], sems.at[index, 0]),
            pltpu.make_async_copy(
                other_hbm.at[:, part], volume.at[pl.ds((1 - mem) * held, held), part], sems.at[index, 1]
            ),
            pltpu.make_async_copy(matrix_hbm.at[part], matrix.at[part], sems.at[index, 2]),
        )

    for index in range(chunks):
        for copy in fetch(index):
            copy.start()

    offsets[0] = 0
    running = jnp.int32(0)
    for tile in range(tiles):
        running = running + count_ref[0, tile]
        offsets[tile + 1] = running
    for extra in range(12):
        offsets[tiles + 1 + extra] = running
    total[...] = jnp.zeros_like(total)
    centre_y = lax.broadcasted_iota(jnp.int32, (16, STEP), 0).astype(jnp.float32) * B + (B - 1) / 2

    def project(index, carry):
        for copy in fetch(index):
            copy.wait()
        part = pl.ds(pl.multiple_of(index * chunk, chunk), chunk)
        for member in range(2 * held):
            wide[member * chunk:member * chunk + chunk, :] = volume[member, part].astype(jnp.float32)
        for inner in range(chunk // per_step):
            step = index * (chunk // per_step) + inner
            here = pl.ds(pl.multiple_of(step * STEP, STEP), STEP)
            cells = cell_ref[:, here]
            pos_x = (cells >> 7).astype(jnp.float32)
            pos_y = (cells & 127).astype(jnp.float32)
            inverse = (1.0 / error_ref[:, here]).astype(jnp.bfloat16).astype(jnp.float32)
            near_y = jnp.exp((pos_y - centre_y) ** 2 * (-0.5 / LOC**2)) * inverse
            for i in range(2):
                near_x = jnp.exp((pos_x - (i * B + (B - 1) / 2)) ** 2 * (-0.5 / LOC**2))
                weights[step, i * 16:i * 16 + 16, :] = (near_x * near_y).astype(jnp.bfloat16)
            values = value_ref[:, here].astype(jnp.float32)
            for sub in range(per_step):
                local = inner * per_step + sub
                block = index * chunk + local
                gates = wide[pl.ds(local, 2 * held, stride=chunk), :].astype(jnp.bfloat16)
                obs = jnp.dot(gates, matrix[block], preferred_element_type=jnp.float32)
                obs = obs.astype(jnp.bfloat16).astype(jnp.float32)
                mean = jnp.sum(obs, axis=0, keepdims=True) * (1.0 / 40)
                anomalies[block] = obs - mean
                surprises[block] = jnp.broadcast_to(values[:, sub * SUB:(sub + 1) * SUB] - mean, (8, SUB))
        return carry

    lax.fori_loop(0, chunks, project, 0)

    lane = lax.broadcasted_iota(jnp.int32, (8, STEP), 1)

    def build(item, lhs, rhs, products):
        step, group = item
        step = jnp.minimum(step, steps - 1)
        for sub in range(per_step):
            block = step * per_step + sub
            lanes = slice(sub * SUB, (sub + 1) * SUB)
            part = [
                anomalies[block, 8 * i:8 * i + 8, :].astype(jnp.bfloat16).astype(jnp.float32) for i in range(5)
            ]
            made = {}

            def operand(kind, entry):
                low, high, turn = entry
                if kind == 0:
                    return part[low]
                if high < 0:
                    return surprises[block]
                if (high, turn) not in made:
                    made[high, turn] = part[high] if turn == 0 else pltpu.roll(part[high], turn, 0)
                return made[high, turn]

            packed = {}

            def pack(kind, both):
                key = tuple((kind, entry[0]) if kind == 0 else (kind, entry[1:]) for entry in both)
                if key not in packed:
                    packed[key] = jnp.concatenate([operand(kind, entry) for entry in both], axis=0).astype(jnp.bfloat16)
                return packed[key]

            for index, both in enumerate(products):
                if both[0] is None:
                    continue
                lhs[index * 16:index * 16 + 16, lanes] = pack(0, both) * pack(1, both)
        slot = lane + step * STEP
        reached = [jnp.where(slot >= offsets[group * 4 + i], 1.0, 0.0) for i in range(9)]
        weight = weights[step]
        for i in range(8):
            inside = reached[i] - reached[i + 1]
            inside = jnp.concatenate([inside, inside], axis=0).astype(jnp.bfloat16)
            for half in range(2):
                rhs[i * 32 + half * 16:i * 32 + half * 16 + 16, :] = weight[half * 16:half * 16 + 16] * inside

    def use(group, lhs, rhs):
        added = lax.dot_general(
            lhs[...], rhs[...], (((1,), (1,)), ((), ())), preferred_element_type=jnp.float32
        )
        total[group] += added[:, :128]
        total[group + 1] += added[:, 128:]

    def follow(item):
        step, group = item
        end = (step + 1) * STEP
        again = (group + 2 < tiles // 4) & (offsets[group * 4 + 8] < end)
        ahead = (offsets[group * 4 + 4] <= end).astype(jnp.int32) + (offsets[group * 4 + 8] <= end).astype(jnp.int32)
        next_step = jnp.where(again, step, step + 1)
        next_group = jnp.where(again, group + 2, group + ahead)
        return next_step, jnp.where(next_step >= steps, tiles // 4, next_group)

    for core, products in enumerate(core_products()):

        @pl.when(mem == core)
        def _():
            if products[-1][0] is None:
                lhs0[len(products) * 16 - 16:, :] = jnp.zeros((16, STEP), jnp.bfloat16)
                lhs1[len(products) * 16 - 16:, :] = jnp.zeros((16, STEP), jnp.bfloat16)
            start = (jnp.int32(0), jnp.int32(0))
            build(start, lhs0, rhs0, products)

            def body(item):
                for turn in range(UNROLL):
                    lhs, rhs = (lhs0, rhs0) if turn % 2 == 0 else (lhs1, rhs1)
                    other_lhs, other_rhs = (lhs1, rhs1) if turn % 2 == 0 else (lhs0, rhs0)
                    following = follow(item)
                    use(item[1], lhs, rhs)
                    build(following, other_lhs, other_rhs, products)
                    item = following
                return item

            lax.while_loop(lambda item: item[0] < steps, body, start)

    results = []
    for x in range(4):
        for y in range(4):
            ab_ref[x, y] = total[x * 4 + y, :PART_A + PART_B].astype(jnp.bfloat16)
        for z, value in enumerate(block_swap([total[x * 4 + y, PART_A + PART_B:] for y in range(4)])):
            c_ref[z, x] = value.astype(jnp.bfloat16)
        results.append(pltpu.make_async_copy(ab_ref.at[x], ab_hbm.at[x], out_sems.at[2 * x]))
        results.append(pltpu.make_async_copy(c_ref.at[:, x], c_hbm.at[:, x], out_sems.at[2 * x + 1]))
        for copy in results[-2:]:
            copy.start()
    for copy in results:
        copy.wait()


def gram(counts, volume, other, matrix, values, errors, cells):
    blocks = matrix.shape[0]
    tiles = counts.shape[1]
    members = 2 * volume.shape[0]
    rows = PART_A + PART_B + PART_C
    steps = blocks * SUB // STEP
    vmem = pl.BlockSpec(memory_space=pltpu.VMEM)
    hbm = pl.BlockSpec(memory_space=pl.ANY)
    return pl.pallas_call(
        gram_kernel,
        out_shape=(
            jax.ShapeDtypeStruct((4, 4, PART_A + PART_B, 128), jnp.bfloat16),
            jax.ShapeDtypeStruct((4, 4, PART_C, 128), jnp.bfloat16),
        ),
        in_specs=[pl.BlockSpec(memory_space=pltpu.SMEM), hbm, hbm, hbm, vmem, vmem, vmem],
        out_specs=(hbm, hbm),
        scratch_shapes=[
            pltpu.VMEM((4, 4, PART_A + PART_B, 128), jnp.bfloat16),
            pltpu.VMEM((4, 4, PART_C, 128), jnp.bfloat16),
            pltpu.VMEM((members, blocks, 128), jnp.bfloat16),
            pltpu.VMEM((blocks, 128, 128), jnp.bfloat16),
            pltpu.VMEM((members * (blocks // CHUNKS), 128), jnp.float32),
            pltpu.VMEM((blocks, members, 128), jnp.float32),
            pltpu.VMEM((blocks, 8, 128), jnp.float32),
            pltpu.VMEM((steps, 32, STEP), jnp.bfloat16),
            pltpu.VMEM((rows, STEP), jnp.bfloat16),
            pltpu.VMEM((rows, STEP), jnp.bfloat16),
            pltpu.VMEM((256, STEP), jnp.bfloat16),
            pltpu.VMEM((256, STEP), jnp.bfloat16),
            pltpu.VMEM((tiles // 4 + 2, rows, 128), jnp.float32),
            pltpu.SMEM((tiles + 13,), jnp.int32),
            pltpu.SemaphoreType.DMA((CHUNKS, 3)),
            pltpu.SemaphoreType.DMA((8,)),
        ],
        compiler_params=pltpu.CompilerParams(vmem_limit_bytes=60 * 1024 * 1024),
        name="gram",
    )(counts, volume, other, matrix, values, errors, cells)


def apply_kernel(points_ref, tent_x_ref, tent_y_ref, state_hbm, other_hbm, out_hbm, states, out_ref, fine, flat, result, sems, out_sems):
    levels, width_x, width_y = state_hbm.shape[1:]
    own = out_ref.shape[0]
    members = 2 * own
    mem, tx, ty = lax.axis_index("mem"), lax.axis_index("tx"), lax.axis_index("ty")
    copies = []
    for index, source in enumerate((state_hbm, other_hbm)):
        copies.append(pltpu.make_async_copy(source, states.at[index], sems.at[index]))
        copies[index].start()
    kind_x = jnp.where(tx == 0, 0, jnp.where(tx == lax.axis_size("tx") - 1, 2, 1))
    kind_y = jnp.where(ty == 0, 0, jnp.where(ty == lax.axis_size("ty") - 1, 2, 1))
    tent_x, tent_y = tent_x_ref[kind_x], tent_y_ref[kind_y]
    points = points_ref[...].astype(jnp.float32)
    points = jnp.concatenate([points, jnp.zeros((48, points.shape[1]), jnp.float32)], axis=0).T
    points = points[:, :80].astype(jnp.bfloat16)

    for x in range(0, width_x, 2):
        tent = jnp.concatenate(
            [tent_x[:, x + i:x + i + 1] * tent_y for i in range(2)], axis=1
        ).astype(jnp.bfloat16)
        made = jnp.dot(points, tent, preferred_element_type=jnp.float32)
        fine[x] = made[:, :128]
        fine[x + 1] = made[:, 128:]

    for copy in copies:
        copy.wait()

    def widen(member, carry):
        for index, first in enumerate((mem * own, (1 - mem) * own)):
            start = pl.multiple_of((first + member) * levels * width_x, 8)
            flat[pl.ds(start, levels * width_x), :] = (
                states[index, member].astype(jnp.float32).reshape(levels * width_x, width_y)
            )
        return carry

    lax.fori_loop(0, own, widen, 0)

    def column(x, carry):
        def add(step, sums):
            sums = list(sums)
            for inner in range(20):
                k = step * 20 + inner
                field = flat[pl.ds(k * (levels * width_x) + x, levels, stride=width_x), :]
                place = sum(
                    jnp.where(step == turn, (it // 6) * 128 + (it % 6) * 20, 0)
                    for turn, it in enumerate(range(inner, members, 20))
                )
                for j in range(own):
                    row = fine[x, pl.ds(place + j, 8, stride=0), :]
                    sums[j] = sums[j] + row * field
            return tuple(sums)

        zero = jnp.zeros((levels, width_y), jnp.float32)
        sums = lax.fori_loop(0, members // 20, add, (zero,) * own)
        for j in range(own):
            result[pl.ds(j * (levels * width_x) + x, levels, stride=width_x), :] = sums[j]
        return carry

    lax.fori_loop(0, width_x, column, 0)

    def narrow(j, carry):
        start = pl.multiple_of(j * levels * width_x, 8)
        out_ref[j] = (
            result[pl.ds(start, levels * width_x), :]
            .reshape(levels, width_x, width_y)
            .astype(jnp.bfloat16)
        )
        return carry

    parts = out_sems.shape[0]
    share = own // parts
    leaving = []
    for index in range(parts):
        lax.fori_loop(index * share, (index + 1) * share, narrow, 0)
        part = pl.ds(index * share, share)
        leaving.append(pltpu.make_async_copy(out_ref.at[part], out_hbm.at[part], out_sems.at[index]))
        leaving[index].start()
    for copy in leaving:
        copy.wait()


def apply(points, tent_x, tent_y, state, other):
    own, levels, width_x, width_y = state.shape
    members = 2 * own
    return pl.pallas_call(
        apply_kernel,
        out_shape=jax.ShapeDtypeStruct((own, levels, width_x, width_y), jnp.bfloat16),
        in_specs=[pl.BlockSpec(memory_space=pltpu.VMEM)] * 3 + [pl.BlockSpec(memory_space=pl.ANY)] * 2,
        out_specs=pl.BlockSpec(memory_space=pl.ANY),
        scratch_shapes=[
            pltpu.VMEM((2,) + state.shape, state.dtype),
            pltpu.VMEM(state.shape, state.dtype),
            pltpu.VMEM((width_x, points.shape[1], width_y), jnp.float32),
            pltpu.VMEM((members * levels * width_x, width_y), jnp.float32),
            pltpu.VMEM((own * levels * width_x, width_y), jnp.float32),
            pltpu.SemaphoreType.DMA((2,)),
            pltpu.SemaphoreType.DMA((4,)),
        ],
        compiler_params=pltpu.CompilerParams(vmem_limit_bytes=60 * 1024 * 1024),
        name="apply",
    )(points, tent_x, tent_y, state, other)


def swap_kernel(volume_ref, other_ref, send, recv):
    mate = (lax.axis_index("tx"), lax.axis_index("ty"), 1 - lax.axis_index("mem"))
    barrier = pltpu.get_barrier_semaphore()
    pl.semaphore_signal(barrier, inc=1, device_id=mate, device_id_type=MESH)
    pl.semaphore_wait(barrier, 1)
    copy = pltpu.make_async_remote_copy(
        src_ref=volume_ref, dst_ref=other_ref, send_sem=send, recv_sem=recv, device_id=mate, device_id_type=MESH
    )
    copy.start()
    copy.wait()


def swap(volume):
    return pl.pallas_call(
        swap_kernel,
        out_shape=jax.ShapeDtypeStruct(volume.shape, volume.dtype),
        in_specs=[pl.BlockSpec(memory_space=pl.ANY)],
        out_specs=pl.BlockSpec(memory_space=pl.ANY),
        scratch_shapes=[pltpu.SemaphoreType.DMA, pltpu.SemaphoreType.DMA],
        compiler_params=pltpu.CompilerParams(
            collective_id=0, has_side_effects=True, vmem_limit_bytes=60 * 1024 * 1024
        ),
        name="swap",
    )(volume)


def coarse_kernel(
    ab_ref, c_ref, pick_ref, eighth_ref, lane_hbm, state_ref, points_ref, other_ref,
    whole_ab, whole_c, pass_a, pass_b, pass_c, via_a, via_b, via_c, got_a, got_b, got_c,
    next_a, next_b, next_c, got_a2, got_b2, got_c2, last_a, last_b, last_c, got_a3, got_b3, got_c3,
    folded, summed, pick, eighth, lane_ref, picked, spread_rows, rows, edges, columns, halo, corners,
    send, recv, local,
):
    x, ty, mem = lax.axis_index("tx"), lax.axis_index("ty"), lax.axis_index("mem")
    y, z = ty // 4, ty % 4
    spot = (x, y, z)

    def along(axis, turn, core=None):
        core = mem if core is None else core
        if axis == 0:
            return ((x + turn) % 4, ty, core)
        if axis == 1:
            return (x, ((y + turn) % 4) * 4 + z, core)
        return (x, y * 4 + (z + turn) % 4, core)

    mate = (x, ty, 1 - mem)
    ahead = 2 * mem - 1
    around = []
    for step in (1, 15):
        for core in range(2):
            around.append(((x, (ty + step) % 16, core), (((x + ahead) + 4) % 4, (ty + step) % 16, core)))
    peers = [along(axis, turn, core) for axis in range(3) for turn in range(1, 4) for core in (mem, 1 - mem)]
    peers += [mate] + [device for pair in around for device in pair]
    peers += [(((x - ahead) + 4) % 4, (ty + step) % 16, mem) for step in (1, 15)]
    barrier = pltpu.get_barrier_semaphore()
    for device in peers:
        pl.semaphore_signal(barrier, inc=1, device_id=device, device_id_type=MESH)

    parts = (
        (0, lambda place, blocks, first, size: whole_ab.at[place, blocks, pl.ds(first, size)], PART_A),
        (1, lambda place, blocks, first, size: whole_ab.at[blocks, place, pl.ds(PART_A + first, size)], PART_B),
        (2, lambda place, blocks, first, size: whole_c.at[place, blocks, pl.ds(first, size)], PART_C),
    )
    passes, vias, gots = (pass_a, pass_b, pass_c), (via_a, via_b, via_c), (got_a, got_b, got_c)
    fetched = [
        pltpu.make_async_copy(ab_ref, whole_ab, local.at[0]),
        pltpu.make_async_copy(c_ref, whole_c, local.at[1]),
    ]
    for copy in fetched:
        copy.start()
    tables = [
        pltpu.make_async_copy(pick_ref, pick, local.at[2]),
        pltpu.make_async_copy(eighth_ref, eighth, local.at[3]),
        pltpu.make_async_copy(lane_hbm, lane_ref, local.at[4]),
    ]
    for copy in tables:
        copy.start()
    for index in (0, 5, 6, 11):
        corners[index * 16:index * 16 + 16, :] = jnp.zeros((16, 128), jnp.float32)
    corners[192:256, :] = jnp.zeros((64, 128), jnp.float32)
    for core in range(2):
        rows[core, 640:, :] = jnp.zeros((rows.shape[1] - 640, 128), jnp.float32)
    for copy in fetched:
        copy.wait()
    pl.semaphore_wait(barrier, len(peers))

    def link(source, target, sent, landed, device):
        pltpu.make_async_remote_copy(
            src_ref=source, dst_ref=target, send_sem=send.at[sent], recv_sem=recv.at[landed],
            device_id=device, device_id_type=MESH,
        ).start()

    def whole(ref, sent, landed):
        return pltpu.make_async_remote_copy(
            src_ref=ref, dst_ref=ref, send_sem=send.at[sent], recv_sem=recv.at[landed],
            device_id=mate, device_id_type=MESH,
        )

    def wait_landed(ref, landed):
        whole(ref, 0, landed).wait_recv()

    def wait_sent(ref, sent):
        whole(ref, sent, 0).wait_send()

    every, halves = pl.ds(0, 4), (pl.ds(0, 2), pl.ds(2, 2))
    for turn, blocks in enumerate(halves):
        for index, (axis, piece, size) in enumerate(parts):
            half = size // 2
            opposite = (spot[axis] + 2) % 4
            for way in range(2):
                link(
                    piece(opposite, blocks, way * half, half), vias[index].at[way, blocks],
                    index, 2 * index + turn, along(axis, 1 + 2 * way),
                )
    for index, (axis, piece, size) in enumerate(parts):
        half = size // 2
        up, down = (spot[axis] + 1) % 4, (spot[axis] + 3) % 4
        link(piece(up, every, half, half), gots[index].at[0, :, pl.ds(half, half)], index, 6 + index, along(axis, 1))
        link(piece(down, every, 0, half), gots[index].at[1, :, pl.ds(0, half)], index, 6 + index, along(axis, 3))
    link(state_ref, other_ref, 14, 17, mate)
    for turn, blocks in enumerate(halves):
        for index, (axis, piece, size) in enumerate(parts):
            half = size // 2
            wait_landed(vias[index].at[:, blocks], 2 * index + turn)
            for way in range(2):
                own = piece((spot[axis] + 1 + 2 * way) % 4, every, way * half, half)
                for block in (2 * turn, 2 * turn + 1):
                    passes[index][way, block] = (
                        own[block].astype(jnp.float32) + vias[index][way, block].astype(jnp.float32)
                    ).astype(jnp.bfloat16)
                link(
                    passes[index].at[way, blocks], gots[index].at[way, blocks, pl.ds(way * half, half)],
                    3 + index, 6 + index, along(axis, 1 + 2 * way),
                )

    def arrive(index):
        wait_landed(gots[index], 6 + index)

    def add_up(index, block):
        axis, piece, size = parts[index]
        value = piece(spot[axis], every, 0, size)[block].astype(jnp.float32)
        for way in range(2):
            value = value + gots[index][way, block].astype(jnp.float32)
        return value

    def stage(index, axis, source, target):
        for turn in (2, 1, 3):
            place = (spot[axis] + turn) % 4
            link(source.at[place], target.at[turn - 1], 6 + index, 9 + index, along(axis, turn))

    def add_last(own, got):
        value = own.astype(jnp.float32)
        for turn in range(3):
            value = value + got[turn].astype(jnp.float32)
        return value

    arrive(0)
    for block in range(4):
        next_a[block] = add_up(0, block).astype(jnp.bfloat16)
    stage(0, 1, next_a, got_a2)
    arrive(1)
    for block, value in enumerate(block_swap([add_up(1, block) for block in range(4)])):
        next_b[block] = value.astype(jnp.bfloat16)
    stage(1, 2, next_b, got_b2)
    arrive(2)
    for block in range(4):
        next_c[block] = add_up(2, block).astype(jnp.bfloat16)
    stage(2, 0, next_c, got_c2)

    def fold(value, target):
        size = value.shape[0] // 8
        folded[0:value.shape[0], :] = value
        pieces = [folded[i * size:(i + 1) * size, :] for i in range(8)]
        for index, part in enumerate(block_swap(pieces)):
            target[index] = part

    def third(index, axis, source, target):
        for turn in (2, 1, 3, 0):
            place = (spot[axis] + turn) % 4
            for core in (1 - mem,) if turn == 0 else (mem, 1 - mem):
                link(
                    source.at[place * 2 + core], target.at[mem * 4 + turn], 9 + index, 12 + index,
                    along(axis, turn, core),
                )
        target[mem * 4] = source[spot[axis] * 2 + mem]

    def sum_third(index, source, target, row):
        wait_landed(target.at[pl.ds(0, 7)], 12 + index)
        size = source.shape[1]
        for core in range(2):
            value = target[core * 4]
            for turn in range(1, 4):
                value = value + target[core * 4 + turn]
            summed[core * 56 + row:core * 56 + row + size, :] = value

    wait_landed(got_a2, 9)
    fold(add_last(next_a[y], got_a2), last_a)
    third(0, 2, last_a, got_a3)
    wait_landed(got_b2, 10)
    fold(add_last(next_b[z], got_b2), last_b)
    third(1, 0, last_b, got_b3)
    wait_landed(got_c2, 11)
    fold(add_last(next_c[x], got_c2), last_c)
    third(2, 1, last_c, got_c3)
    sum_third(0, last_a, got_a3, 0)
    sum_third(1, last_b, got_b3, 20)
    sum_third(2, last_c, got_c3, 40)

    for copy in tables:
        copy.wait()
    coarse_points(summed[...], pick, eighth, lane_ref, picked, spread_rows, rows)

    after = sixths((16, 128))
    for core in range(2):
        for side in range(2):
            point = 15 * (1 - side)
            value = rows[core, pl.ds(point * 40, 16, stride=6), :]
            for p in range(1, 6):
                value = jnp.where(after[p], rows[core, pl.ds(point * 40 + p, 16, stride=6), :], value)
            columns[core, side] = value
    outer = jnp.where(mem == 1, 0, 2)
    for index, (straight, slanted) in enumerate(around):
        side, core = index // 2, index % 2
        for device, turn in ((straight, 1), (slanted, outer)):
            slot = (side * 3 + turn) * 2 + mem
            link(columns.at[core, side], corners.at[pl.ds(slot * 16, 16)], 12, 15, device)
    for core in range(2):
        edges[core] = gather_members(rows.at[core]).astype(jnp.bfloat16)
    link(edges.at[1 - mem], halo.at[mem], 13, 16, mate)
    for other in range(2):
        core = 1 - mem if other else mem
        link(edges.at[core], halo.at[3 - mem], 13, 16, ((x + ahead + 4) % 4, ty, core))
    points_ref[pl.ds(pl.multiple_of(mem * 16, 16), 16), :] = edges[mem]

    wait_landed(corners.at[pl.ds(0, 128)], 15)
    for q in range(7):
        points_ref[64:80, q * 128:q * 128 + 128] = corners[pl.ds(q, 16, stride=16), :].astype(jnp.bfloat16)
    wait_landed(halo.at[pl.ds(0, 3)], 16)
    points_ref[pl.ds(pl.multiple_of((1 - mem) * 16, 16), 16), :] = halo[1 - mem]
    for slot in (2, 3):
        points_ref[slot * 16:slot * 16 + 16, :] = halo[slot]
    for index in range(3):
        wait_sent(gots[index], index)
        wait_sent(passes[index], 3 + index)
        wait_sent((got_a2, got_b2, got_c2)[index], 6 + index)
        wait_sent((got_a3, got_b3, got_c3)[index].at[pl.ds(0, 7)], 9 + index)
    wait_sent(corners.at[pl.ds(0, 128)], 12)
    wait_sent(halo.at[pl.ds(0, 3)], 13)
    whole(other_ref, 14, 17).wait()


def coarse(partial_ab, partial_c, state):
    pick, eighth = pick_tables()
    bf16, f32 = jnp.bfloat16, jnp.float32
    sizes = (PART_A, PART_B, PART_C)
    hbm, vmem = pl.BlockSpec(memory_space=pl.ANY), pl.BlockSpec(memory_space=pltpu.VMEM)
    return pl.pallas_call(
        coarse_kernel,
        out_shape=(
            jax.ShapeDtypeStruct((80, LINK_LANES), bf16),
            jax.ShapeDtypeStruct(state.shape, state.dtype),
        ),
        in_specs=[hbm] * 6,
        out_specs=(vmem, hbm),
        scratch_shapes=[pltpu.VMEM((4, 4, PART_A + PART_B, 128), bf16), pltpu.VMEM((4, 4, PART_C, 128), bf16)]
        + [pltpu.VMEM((2, 4, size // 2, 128), bf16) for size in sizes]
        + [pltpu.VMEM((2, 4, size // 2, 128), bf16) for size in sizes]
        + [pltpu.VMEM((2, 4, size, 128), bf16) for size in sizes]
        + [pltpu.VMEM((4, size, 128), bf16) for size in sizes]
        + [pltpu.VMEM((3, size, 128), bf16) for size in sizes]
        + [pltpu.VMEM((8, size // 8, 128), f32) for size in sizes]
        + [pltpu.VMEM((8, size // 8, 128), f32) for size in sizes]
        + [
            pltpu.VMEM((PART_A, 128), f32),
            pltpu.VMEM((112, 128), f32),
            pltpu.VMEM((1648, 128), bf16),
            pltpu.VMEM((1648, 128), bf16),
            pltpu.VMEM((8, WIDE), jnp.int32),
            pltpu.VMEM((1648, WIDE), bf16),
            pltpu.VMEM((1648, WIDE), f32),
            pltpu.VMEM((2, 704, 128), f32),
            pltpu.VMEM((2, 16, LINK_LANES), bf16),
            pltpu.VMEM((2, 2, 16, 128), f32),
            pltpu.VMEM((4, 16, LINK_LANES), bf16),
            pltpu.VMEM((256, 128), f32),
            pltpu.SemaphoreType.DMA((15,)),
            pltpu.SemaphoreType.DMA((18,)),
            pltpu.SemaphoreType.DMA((5,)),
        ],
        compiler_params=pltpu.CompilerParams(
            collective_id=1, has_side_effects=True, vmem_limit_bytes=60 * 1024 * 1024
        ),
        name="coarse",
    )(partial_ab, partial_c, jnp.asarray(pick), jnp.asarray(eighth), jnp.asarray(lane_table()), state)


def tent(length, nodes):
    position = np.arange(length, dtype=np.float32)[:, None]
    centre = (np.arange(nodes, dtype=np.float32)[None, :] - 1.0) * B + (B - 1) * 0.5
    return np.maximum(0.0, 1.0 - np.abs(position - centre) / B)


def tent_tables():
    place_x, place_y = np.full(80, -1), np.full(80, -1)
    for i in range(2):
        for j in range(16):
            place_x[i * 16 + j], place_y[i * 16 + j] = i + 1, j + 1
            place_x[32 + i * 16 + j], place_y[32 + i * 16 + j] = 3 * i, j + 1
    for side in range(2):
        for turn in range(3):
            for i in range(2):
                row = 64 + (side * 3 + turn) * 2 + i
                place_y[row] = 17 * side
                place_x[row] = {1: i + 1, 0: 0 if i == 1 else -1, 2: 3 if i == 0 else -1}[turn]
    tables = []
    for length, nodes, place in ((16, 4, place_x), (128, 18, place_y)):
        table = np.zeros((3, 80, length), np.float32)
        for kind in range(3):
            weights = tent(length, nodes)
            if kind == 0:
                weights[:, 1] += weights[:, 0]
                weights[:, 0] = 0
            if kind == 2:
                weights[:, -2] += weights[:, -1]
                weights[:, -1] = 0
            for row in range(80):
                if place[row] >= 0:
                    table[kind, row] = weights[:, place[row]]
        tables.append(table)
    return tables


def per_device(volume, super_matrix, observed, error_var, obs_cells, counts, state):
    other_volume = swap(volume[0])
    partial_ab, partial_c = gram(counts, volume[0], other_volume, super_matrix[0], observed, error_var, obs_cells)
    points, other_state = coarse(partial_ab, partial_c, state)
    tent_x, tent_y = tent_tables()
    return apply(points, jnp.asarray(tent_x), jnp.asarray(tent_y), state, other_state)


def solution(mesh):
    placed = (
        P(("tx", "ty"), "mem", None, None),
        P(("tx", "ty"), None, None, None),
        P(("tx", "ty"), None),
        P(("tx", "ty"), None),
        P(("tx", "ty"), None),
        P(("tx", "ty"), None),
        P("mem", None, "tx", "ty"),
    )
    return jax.shard_map(
        per_device,
        mesh=mesh,
        in_specs=placed,
        out_specs=P("mem", None, "tx", "ty"),
        check_vma=False,
    )
```

```python
import functools

import numpy as np
import jax
import jax.numpy as jnp
from jax import lax
from jax.experimental import pallas as pl
from jax.experimental.pallas import tpu as pltpu
from jax.sharding import PartitionSpec as P

B = 8
LOC = 16
NS = 5
STEP = 768
SUB = 128
CHUNKS = 4


MESH = pl.DeviceIdType.MESH
PART_A, PART_B, PART_C = 160, 160, 128
GROUPS = 3
WIDE = 256
LINK_LANES = 896


def place_of(row):
    if row < PART_A:
        return row % (PART_A // 8), row // (PART_A // 8)
    row -= PART_A
    if row < PART_B:
        return PART_A // 8 + row % (PART_B // 8), row // (PART_B // 8)
    row -= PART_B
    return (PART_A + PART_B) // 8 + row % (PART_C // 8), row // (PART_C // 8)


def pick_tables():
    rows = np.zeros((1648, 128), np.float32)
    eighths = np.zeros((1648, 128), np.float32)

    def put(target, core, local):
        row, eighth = place_of(local)
        rows[target] = 0
        eighths[target] = 0
        rows[target, core * 56 + row] = 1
        eighths[target, eighth * 16:eighth * 16 + 16] = 1

    for core, products in enumerate(core_products()):
        for index, entry in enumerate([entry for both in products for entry in both]):
            if entry is None:
                continue
            low, high, turn = entry
            for s in range(8):
                if high < 0:
                    put(1600 + 8 * low + s, core, index * 8 + s)
                    continue
                k, j = 8 * low + s, 8 * high + (s - turn) % 8
                put(j * 40 + k, core, index * 8 + s)
                put(k * 40 + j, core, index * 8 + s)
    return rows.astype(jnp.bfloat16), eighths.astype(jnp.bfloat16)


def lane_table():
    lanes = np.arange(WIDE)
    table = np.full((8, WIDE), -1, np.int32)
    table[0] = np.where(lanes < 240, lanes // 40, 7)
    table[1] = np.where(lanes < 240, lanes % 40, -1)
    return table


def block_swap(arrays):
    lane = lax.broadcasted_iota(jnp.int32, arrays[0].shape, 1)
    count = len(arrays)
    step = count // 2
    while step:
        width = step * (128 // count)
        mask = (lane & width) == 0
        turned = list(arrays)
        for low in range(count):
            if low & step:
                continue
            first, second = arrays[low], arrays[low + step]
            turned[low] = jnp.where(mask, first, pltpu.roll(second, width, 1))
            turned[low + step] = jnp.where(mask, pltpu.roll(first, 128 - width, 1), second)
        arrays = turned
        step //= 2
    return arrays


def split(value):
    high = value.astype(jnp.bfloat16)
    return high, (value - high.astype(jnp.float32)).astype(jnp.bfloat16)


def bdot(left, right):
    return jnp.dot(left, right, preferred_element_type=jnp.float32)


def coarse_points(summed, pick_ref, eighth_ref, lane_ref, picked, spread_rows, rows):
    lane_i, lane_j = lane_ref[0:1], lane_ref[1:2]
    high, low = split(summed)
    both = jnp.concatenate([high, low], axis=1)
    both = jnp.concatenate([both, jnp.zeros((16, WIDE), jnp.bfloat16)], axis=0)
    eighths = eighth_ref[...].astype(jnp.float32)
    found = bdot(pick_ref[...], both)
    picked[...] = jnp.concatenate(
        [found[:, :128] * eighths, found[:, 128:] * eighths], axis=1
    ).astype(jnp.bfloat16)
    row_c = lax.broadcasted_iota(jnp.int32, (WIDE, WIDE), 0) & 15
    eye = (lax.broadcasted_iota(jnp.int32, (40, WIDE), 0) == lane_j).astype(jnp.float32)
    real = lane_j >= 0
    same = (
        (jnp.concatenate(
            [jnp.full((40, WIDE), i, jnp.int32) for i in range(6)] + [jnp.full((16, WIDE), 9, jnp.int32)], axis=0
        ) == lane_i)
        .astype(jnp.float32)
        .astype(jnp.bfloat16)
    )

    def blocks(value):
        parts = [jnp.where(lane_i == i, value, 0.0) for i in range(6)] + [jnp.zeros((16, WIDE), jnp.float32)]
        return split(jnp.concatenate(parts, axis=0))

    def times(values, right):
        right_high, right_low = right
        highs, lows = zip(*[split(value) for value in values])
        count = len(values) * 40
        stack = jnp.concatenate([part.astype(jnp.float32) for part in highs + lows], axis=0).astype(jnp.bfloat16)
        main = bdot(stack, right_high)
        rest = bdot(stack[:count], right_low)
        return [
            main[40 * i:40 * i + 40] + (main[count + 40 * i:count + 40 * i + 40] + rest[40 * i:40 * i + 40])
            for i in range(len(values))
        ]

    uppers, lowers, scales, informs = [], [], [], []
    for group in range(GROUPS):
        expand = (row_c == lane_i + 6 * group).astype(jnp.float32) * real.astype(jnp.float32)
        spread_rows[...] = bdot(picked[...], expand.astype(jnp.bfloat16))
        gram = jnp.zeros((40, WIDE), jnp.float32)
        for j in range(40):
            gram = jnp.where(lane_j == j, spread_rows[40 * j:40 * j + 40], gram)
        informs.append(spread_rows[1600:1640])
        amat = eye + gram * (1.0 / 39)
        square = jnp.sum(amat * amat, axis=0, keepdims=True)
        first = square.astype(jnp.bfloat16).astype(jnp.float32)
        second = (square - first).astype(jnp.bfloat16).astype(jnp.float32)
        third = square - first - second
        parts = jnp.concatenate(
            [jnp.broadcast_to(part, (8, WIDE)) for part in (first, second, third, jnp.zeros_like(third))], axis=0
        )
        norm = bdot(parts.astype(jnp.bfloat16), same)
        norm = norm[0:1] + norm[8:9] + norm[16:17]
        scale = jnp.sqrt(jnp.where(real, norm, 1.0))
        scales.append(scale)
        uppers.append(amat / scale)
    for group in range(GROUPS):
        middle = 1.5 * eye - 0.5 * uppers[group]
        lowers.append(middle)
        uppers[group] = times([uppers[group]], blocks(middle))[0]
    for sweep in range(1, NS):
        middles = []
        for group in range(GROUPS):
            product = times([lowers[group]], blocks(uppers[group]))[0]
            middles.append(blocks(1.5 * eye - 0.5 * product))
        for group in range(GROUPS):
            if sweep < NS - 1:
                uppers[group], lowers[group] = times([uppers[group], lowers[group]], middles[group])
            else:
                lowers[group] = times([lowers[group]], middles[group])[0]
    target = lax.broadcasted_iota(jnp.int32, (WIDE, 768), 1)
    source = lax.broadcasted_iota(jnp.int32, (WIDE, 768), 0)
    own = target & 127
    point = (target >> 7) * 40
    for copy in range(1, 6):
        own = jnp.where((target & 127) >= 20 * copy, (target & 127) - 20 * copy, own)
    chooses = []
    for core in range(2):
        chosen = (source == point + core * 20 + own) & ((target & 127) < 120)
        chooses.append(chosen.astype(jnp.float32).astype(jnp.bfloat16))
    for group in range(GROUPS):
        inv_half = lowers[group] / jnp.sqrt(scales[group])
        step_one = jnp.sum(inv_half * informs[group], axis=0, keepdims=True)
        product = inv_half * step_one
        high, low = split(product)
        stack = jnp.concatenate([high.astype(jnp.float32), low.astype(jnp.float32)], axis=0).astype(jnp.bfloat16)
        moved = bdot(stack, same)
        shift = (moved[:40] + moved[40:]) * (1.0 / 39)
        shift = shift - jnp.sum(shift, axis=0, keepdims=True) * (1.0 / 40)
        spread = inv_half - jnp.sum(inv_half, axis=0, keepdims=True) * (1.0 / 40)
        trans = (1.0 / 40 + shift + spread).astype(jnp.bfloat16)
        for core in range(2):
            chosen = bdot(trans, chooses[core])
            for i in range(6):
                point = group * 6 + i
                if point < 16:
                    rows[core, point * 40:point * 40 + 40, :] = chosen[:, i * 128:i * 128 + 128]


def sixths(shape):
    lane = lax.broadcasted_iota(jnp.int32, shape, 1)
    return [lane >= 20 * p for p in range(6)]


def gather_members(rows):
    after = sixths((16, 128))
    pieces = []
    for q in range(7):
        piece = rows[pl.ds(6 * q, 16, stride=40), :]
        for p in range(1, 6):
            piece = jnp.where(after[p], rows[pl.ds(6 * q + p, 16, stride=40), :], piece)
        pieces.append(piece)
    return jnp.concatenate(pieces, axis=1)


UNROLL = 16


def core_products():
    first, second = [], []
    for high in (4, 3, 2, 1):
        for low in range(high):
            for turn in range(0, 8, 2):
                both = ((low, high, turn), (low, high, turn + 1))
                (first if high > 2 else second).append(both)
    for low in range(5):
        second.append(((low, low, 0), (low, low, 1)))
        second.append(((low, low, 2), (low, low, 3)))
    second.append(((0, 0, 4), (1, 1, 4)))
    second.append(((2, 2, 4), (3, 3, 4)))
    second.append(((0, -1, 0), (1, -1, 0)))
    second.append(((2, -1, 0), (3, -1, 0)))
    second.append(((4, 4, 4), (4, -1, 0)))
    second.append((None, None))
    return first, second


def gram_kernel(
    count_ref, volume_hbm, other_hbm, matrix_hbm, value_ref, error_ref, cell_ref, ab_hbm, c_hbm,
    ab_ref, c_ref,    volume, matrix, wide, anomalies, surprises, weights, lhs0, lhs1, rhs0, rhs1, total, offsets, sems, out_sems,
):
    mem = lax.axis_index("mem")
    chunks = sems.shape[0]
    radar_blocks = matrix.shape[0]
    held = volume_hbm.shape[0]
    tiles = count_ref.shape[1]
    chunk = radar_blocks // chunks
    steps = radar_blocks * SUB // STEP
    per_step = STEP // SUB

    def fetch(index):
        part = pl.ds(index * chunk, chunk)
        return (
            pltpu.make_async_copy(volume_hbm.at[:, part], volume.at[pl.ds(mem * held, held), part], sems.at[index, 0]),
            pltpu.make_async_copy(
                other_hbm.at[:, part], volume.at[pl.ds((1 - mem) * held, held), part], sems.at[index, 1]
            ),
            pltpu.make_async_copy(matrix_hbm.at[part], matrix.at[part], sems.at[index, 2]),
        )

    for index in range(chunks):
        for copy in fetch(index):
            copy.start()

    offsets[0] = 0
    running = jnp.int32(0)
    for tile in range(tiles):
        running = running + count_ref[0, tile]
        offsets[tile + 1] = running
    for extra in range(12):
        offsets[tiles + 1 + extra] = running
    total[...] = jnp.zeros_like(total)
    centre_y = lax.broadcasted_iota(jnp.int32, (16, STEP), 0).astype(jnp.float32) * B + (B - 1) / 2

    def project(index, carry):
        for copy in fetch(index):
            copy.wait()
        part = pl.ds(pl.multiple_of(index * chunk, chunk), chunk)
        for member in range(2 * held):
            wide[member * chunk:member * chunk + chunk, :] = volume[member, part].astype(jnp.float32)
        for inner in range(chunk // per_step):
            step = index * (chunk // per_step) + inner
            here = pl.ds(pl.multiple_of(step * STEP, STEP), STEP)
            cells = cell_ref[:, here]
            pos_x = (cells >> 7).astype(jnp.float32)
            pos_y = (cells & 127).astype(jnp.float32)
            inverse = (1.0 / error_ref[:, here]).astype(jnp.bfloat16).astype(jnp.float32)
            near_y = jnp.exp((pos_y - centre_y) ** 2 * (-0.5 / LOC**2)) * inverse
            for i in range(2):
                near_x = jnp.exp((pos_x - (i * B + (B - 1) / 2)) ** 2 * (-0.5 / LOC**2))
                weights[step, i * 16:i * 16 + 16, :] = (near_x * near_y).astype(jnp.bfloat16)
            values = value_ref[:, here].astype(jnp.float32)
            for sub in range(per_step):
                local = inner * per_step + sub
                block = index * chunk + local
                gates = wide[pl.ds(local, 2 * held, stride=chunk), :].astype(jnp.bfloat16)
                obs = jnp.dot(gates, matrix[block], preferred_element_type=jnp.float32)
                obs = obs.astype(jnp.bfloat16).astype(jnp.float32)
                mean = jnp.sum(obs, axis=0, keepdims=True) * (1.0 / 40)
                anomalies[block] = obs - mean
                surprises[block] = jnp.broadcast_to(values[:, sub * SUB:(sub + 1) * SUB] - mean, (8, SUB))
        return carry

    lax.fori_loop(0, chunks, project, 0)

    lane = lax.broadcasted_iota(jnp.int32, (8, STEP), 1)

    def build(item, lhs, rhs, products):
        step, group = item
        step = jnp.minimum(step, steps - 1)
        for sub in range(per_step):
            block = step * per_step + sub
            lanes = slice(sub * SUB, (sub + 1) * SUB)
            part = [
                anomalies[block, 8 * i:8 * i + 8, :].astype(jnp.bfloat16).astype(jnp.float32) for i in range(5)
            ]
            made = {}

            def operand(kind, entry):
                low, high, turn = entry
                if kind == 0:
                    return part[low]
                if high < 0:
                    return surprises[block]
                if (high, turn) not in made:
                    made[high, turn] = part[high] if turn == 0 else pltpu.roll(part[high], turn, 0)
                return made[high, turn]

            packed = {}

            def pack(kind, both):
                key = tuple((kind, entry[0]) if kind == 0 else (kind, entry[1:]) for entry in both)
                if key not in packed:
                    packed[key] = jnp.concatenate([operand(kind, entry) for entry in both], axis=0).astype(jnp.bfloat16)
                return packed[key]

            for index, both in enumerate(products):
                if both[0] is None:
                    continue
                lhs[index * 16:index * 16 + 16, lanes] = pack(0, both) * pack(1, both)
        slot = lane + step * STEP
        reached = [jnp.where(slot >= offsets[group * 4 + i], 1.0, 0.0) for i in range(9)]
        weight = weights[step]
        for i in range(8):
            inside = reached[i] - reached[i + 1]
            inside = jnp.concatenate([inside, inside], axis=0).astype(jnp.bfloat16)
            for half in range(2):
                rhs[i * 32 + half * 16:i * 32 + half * 16 + 16, :] = weight[half * 16:half * 16 + 16] * inside

    def use(group, lhs, rhs):
        added = lax.dot_general(
            lhs[...], rhs[...], (((1,), (1,)), ((), ())), preferred_element_type=jnp.float32
        )
        total[group] += added[:, :128]
        total[group + 1] += added[:, 128:]

    def follow(item):
        step, group = item
        end = (step + 1) * STEP
        again = (group + 2 < tiles // 4) & (offsets[group * 4 + 8] < end)
        ahead = (offsets[group * 4 + 4] <= end).astype(jnp.int32) + (offsets[group * 4 + 8] <= end).astype(jnp.int32)
        next_step = jnp.where(again, step, step + 1)
        next_group = jnp.where(again, group + 2, group + ahead)
        return next_step, jnp.where(next_step >= steps, tiles // 4, next_group)

    for core, products in enumerate(core_products()):

        @pl.when(mem == core)
        def _():
            if products[-1][0] is None:
                lhs0[len(products) * 16 - 16:, :] = jnp.zeros((16, STEP), jnp.bfloat16)
                lhs1[len(products) * 16 - 16:, :] = jnp.zeros((16, STEP), jnp.bfloat16)
            start = (jnp.int32(0), jnp.int32(0))
            build(start, lhs0, rhs0, products)

            def body(turns, item):
                for turn in range(turns):
                    lhs, rhs = (lhs0, rhs0) if turn % 2 == 0 else (lhs1, rhs1)
                    other_lhs, other_rhs = (lhs1, rhs1) if turn % 2 == 0 else (lhs0, rhs0)
                    following = follow(item)
                    use(item[1], lhs, rhs)
                    build(following, other_lhs, other_rhs, products)
                    item = following
                return item

            item = lax.while_loop(
                lambda item: item[0] <= steps - UNROLL, functools.partial(body, UNROLL), start
            )
            lax.while_loop(lambda item: item[0] < steps, functools.partial(body, 2), item)

    results = []
    for x in range(4):
        for y in range(4):
            ab_ref[x, y] = total[x * 4 + y, :PART_A + PART_B].astype(jnp.bfloat16)
        for z, value in enumerate(block_swap([total[x * 4 + y, PART_A + PART_B:] for y in range(4)])):
            c_ref[z, x] = value.astype(jnp.bfloat16)
        results.append(pltpu.make_async_copy(ab_ref.at[x], ab_hbm.at[x], out_sems.at[2 * x]))
        results.append(pltpu.make_async_copy(c_ref.at[:, x], c_hbm.at[:, x], out_sems.at[2 * x + 1]))
        for copy in results[-2:]:
            copy.start()
    for copy in results:
        copy.wait()


def gram(counts, volume, other, matrix, values, errors, cells):
    blocks = matrix.shape[0]
    tiles = counts.shape[1]
    members = 2 * volume.shape[0]
    rows = PART_A + PART_B + PART_C
    steps = blocks * SUB // STEP
    vmem = pl.BlockSpec(memory_space=pltpu.VMEM)
    hbm = pl.BlockSpec(memory_space=pl.ANY)
    return pl.pallas_call(
        gram_kernel,
        out_shape=(
            jax.ShapeDtypeStruct((4, 4, PART_A + PART_B, 128), jnp.bfloat16),
            jax.ShapeDtypeStruct((4, 4, PART_C, 128), jnp.bfloat16),
        ),
        in_specs=[pl.BlockSpec(memory_space=pltpu.SMEM), hbm, hbm, hbm, vmem, vmem, vmem],
        out_specs=(hbm, hbm),
        scratch_shapes=[
            pltpu.VMEM((4, 4, PART_A + PART_B, 128), jnp.bfloat16),
            pltpu.VMEM((4, 4, PART_C, 128), jnp.bfloat16),
            pltpu.VMEM((members, blocks, 128), jnp.bfloat16),
            pltpu.VMEM((blocks, 128, 128), jnp.bfloat16),
            pltpu.VMEM((members * (blocks // CHUNKS) + 512, 128), jnp.float32),
            pltpu.VMEM((blocks, members, 128), jnp.float32),
            pltpu.VMEM((blocks, 8, 128), jnp.float32),
            pltpu.VMEM((steps, 32, STEP), jnp.bfloat16),
            pltpu.VMEM((rows, STEP), jnp.bfloat16),
            pltpu.VMEM((rows, STEP), jnp.bfloat16),
            pltpu.VMEM((256, STEP), jnp.bfloat16),
            pltpu.VMEM((256, STEP), jnp.bfloat16),
            pltpu.VMEM((tiles // 4 + 2, rows, 128), jnp.float32),
            pltpu.SMEM((tiles + 13,), jnp.int32),
            pltpu.SemaphoreType.DMA((CHUNKS, 3)),
            pltpu.SemaphoreType.DMA((8,)),
        ],
        compiler_params=pltpu.CompilerParams(vmem_limit_bytes=60 * 1024 * 1024),
        name="gram",
    )(counts, volume, other, matrix, values, errors, cells)


def apply_kernel(points_ref, tent_x_ref, tent_y_ref, state_hbm, other_hbm, out_hbm, states, out_ref, fine, flat, result, sems, out_sems):
    levels, width_x, width_y = state_hbm.shape[1:]
    own = out_ref.shape[0]
    members = 2 * own
    mem, tx, ty = lax.axis_index("mem"), lax.axis_index("tx"), lax.axis_index("ty")
    copies = []
    for index, source in enumerate((state_hbm, other_hbm)):
        copies.append(pltpu.make_async_copy(source, states.at[index], sems.at[index]))
        copies[index].start()
    kind_x = jnp.where(tx == 0, 0, jnp.where(tx == lax.axis_size("tx") - 1, 2, 1))
    kind_y = jnp.where(ty == 0, 0, jnp.where(ty == lax.axis_size("ty") - 1, 2, 1))
    tent_x, tent_y = tent_x_ref[kind_x], tent_y_ref[kind_y]
    points = points_ref[...].astype(jnp.float32)
    points = jnp.concatenate([points, jnp.zeros((48, points.shape[1]), jnp.float32)], axis=0).T
    points = points[:, :80].astype(jnp.bfloat16)

    for x in range(0, width_x, 2):
        tent = jnp.concatenate(
            [tent_x[:, x + i:x + i + 1] * tent_y for i in range(2)], axis=1
        ).astype(jnp.bfloat16)
        made = jnp.dot(points, tent, preferred_element_type=jnp.float32)
        fine[x, :made.shape[0], :] = made[:, :128]
        fine[x + 1, :made.shape[0], :] = made[:, 128:]

    for copy in copies:
        copy.wait()

    def widen(member, carry):
        for index, first in enumerate((mem * own, (1 - mem) * own)):
            start = pl.multiple_of((first + member) * levels * width_x, 8)
            flat[pl.ds(start, levels * width_x), :] = (
                states[index, member].astype(jnp.float32).reshape(levels * width_x, width_y)
            )
        return carry

    lax.fori_loop(0, own, widen, 0)

    def column(x, carry):
        def add(step, sums):
            sums = list(sums)
            for inner in range(20):
                k = step * 20 + inner
                field = flat[pl.ds(k * (levels * width_x) + x, levels, stride=width_x), :]
                place = sum(
                    jnp.where(step == turn, (it // 6) * 128 + (it % 6) * 20, 0)
                    for turn, it in enumerate(range(inner, members, 20))
                )
                for j in range(own):
                    row = fine[x, pl.ds(place + j, 8, stride=0), :]
                    sums[j] = sums[j] + row * field
            return tuple(sums)

        zero = jnp.zeros((levels, width_y), jnp.float32)
        sums = lax.fori_loop(0, members // 20, add, (zero,) * own)
        for j in range(own):
            result[pl.ds(j * (levels * width_x) + x, levels, stride=width_x), :] = sums[j]
        return carry

    lax.fori_loop(0, width_x, column, 0)

    def narrow(j, carry):
        start = pl.multiple_of(j * levels * width_x, 8)
        out_ref[j] = (
            result[pl.ds(start, levels * width_x), :]
            .reshape(levels, width_x, width_y)
            .astype(jnp.bfloat16)
        )
        return carry

    parts = out_sems.shape[0]
    share = own // parts
    leaving = []
    for index in range(parts):
        lax.fori_loop(index * share, (index + 1) * share, narrow, 0)
        part = pl.ds(index * share, share)
        leaving.append(pltpu.make_async_copy(out_ref.at[part], out_hbm.at[part], out_sems.at[index]))
        leaving[index].start()
    for copy in leaving:
        copy.wait()


def apply(points, tent_x, tent_y, state, other):
    own, levels, width_x, width_y = state.shape
    members = 2 * own
    return pl.pallas_call(
        apply_kernel,
        out_shape=jax.ShapeDtypeStruct((own, levels, width_x, width_y), jnp.bfloat16),
        in_specs=[pl.BlockSpec(memory_space=pltpu.VMEM)] * 3 + [pl.BlockSpec(memory_space=pl.ANY)] * 2,
        out_specs=pl.BlockSpec(memory_space=pl.ANY),
        scratch_shapes=[
            pltpu.VMEM((2,) + state.shape, state.dtype),
            pltpu.VMEM(state.shape, state.dtype),
            pltpu.VMEM((width_x, points.shape[1] + 16, width_y), jnp.float32),
            pltpu.VMEM((members * levels * width_x + 256, width_y), jnp.float32),
            pltpu.VMEM((own * levels * width_x + 256, width_y), jnp.float32),
            pltpu.SemaphoreType.DMA((2,)),
            pltpu.SemaphoreType.DMA((4,)),
        ],
        compiler_params=pltpu.CompilerParams(vmem_limit_bytes=60 * 1024 * 1024),
        name="apply",
    )(points, tent_x, tent_y, state, other)


def swap_kernel(volume_ref, other_ref, send, recv):
    mate = (lax.axis_index("tx"), lax.axis_index("ty"), 1 - lax.axis_index("mem"))
    barrier = pltpu.get_barrier_semaphore()
    pl.semaphore_signal(barrier, inc=1, device_id=mate, device_id_type=MESH)
    pl.semaphore_wait(barrier, 1)
    copy = pltpu.make_async_remote_copy(
        src_ref=volume_ref, dst_ref=other_ref, send_sem=send, recv_sem=recv, device_id=mate, device_id_type=MESH
    )
    copy.start()
    copy.wait()


def swap(volume):
    return pl.pallas_call(
        swap_kernel,
        out_shape=jax.ShapeDtypeStruct(volume.shape, volume.dtype),
        in_specs=[pl.BlockSpec(memory_space=pl.ANY)],
        out_specs=pl.BlockSpec(memory_space=pl.ANY),
        scratch_shapes=[pltpu.SemaphoreType.DMA, pltpu.SemaphoreType.DMA],
        compiler_params=pltpu.CompilerParams(
            collective_id=0, has_side_effects=True, vmem_limit_bytes=60 * 1024 * 1024
        ),
        name="swap",
    )(volume)


def coarse_kernel(
    ab_ref, c_ref, pick_ref, eighth_ref, lane_hbm, state_ref, points_ref, other_ref,
    whole_ab, whole_c, pass_a, pass_b, pass_c, via_a, via_b, via_c, got_a, got_b, got_c,
    next_a, next_b, next_c, got_a2, got_b2, got_c2, last_a, last_b, last_c, got_a3, got_b3, got_c3,
    folded, summed, pick, eighth, lane_ref, picked, spread_rows, rows, edges, columns, halo, corners,
    send, recv, local,
):
    x, ty, mem = lax.axis_index("tx"), lax.axis_index("ty"), lax.axis_index("mem")
    y, z = ty // 4, ty % 4
    spot = (x, y, z)

    def along(axis, turn, core=None):
        core = mem if core is None else core
        if axis == 0:
            return ((x + turn) % 4, ty, core)
        if axis == 1:
            return (x, ((y + turn) % 4) * 4 + z, core)
        return (x, y * 4 + (z + turn) % 4, core)

    mate = (x, ty, 1 - mem)
    ahead = 2 * mem - 1
    around = []
    for step in (1, 15):
        for core in range(2):
            around.append(((x, (ty + step) % 16, core), (((x + ahead) + 4) % 4, (ty + step) % 16, core)))
    peers = [along(axis, turn, core) for axis in range(3) for turn in range(1, 4) for core in (mem, 1 - mem)]
    peers += [mate] + [device for pair in around for device in pair]
    peers += [(((x - ahead) + 4) % 4, (ty + step) % 16, mem) for step in (1, 15)]
    barrier = pltpu.get_barrier_semaphore()
    for device in peers:
        pl.semaphore_signal(barrier, inc=1, device_id=device, device_id_type=MESH)

    parts = (
        (0, lambda place, blocks, first, size: whole_ab.at[place, blocks, pl.ds(first, size)], PART_A),
        (1, lambda place, blocks, first, size: whole_ab.at[blocks, place, pl.ds(PART_A + first, size)], PART_B),
        (2, lambda place, blocks, first, size: whole_c.at[place, blocks, pl.ds(first, size)], PART_C),
    )
    passes, vias, gots = (pass_a, pass_b, pass_c), (via_a, via_b, via_c), (got_a, got_b, got_c)
    fetched = [
        pltpu.make_async_copy(ab_ref, whole_ab, local.at[0]),
        pltpu.make_async_copy(c_ref, whole_c, local.at[1]),
    ]
    for copy in fetched:
        copy.start()
    tables = [
        pltpu.make_async_copy(pick_ref, pick, local.at[2]),
        pltpu.make_async_copy(eighth_ref, eighth, local.at[3]),
        pltpu.make_async_copy(lane_hbm, lane_ref, local.at[4]),
    ]
    for copy in tables:
        copy.start()
    for index in (0, 5, 6, 11):
        corners[index * 16:index * 16 + 16, :] = jnp.zeros((16, 128), jnp.float32)
    corners[192:256, :] = jnp.zeros((64, 128), jnp.float32)
    for core in range(2):
        rows[core, 640:, :] = jnp.zeros((rows.shape[1] - 640, 128), jnp.float32)
    for copy in fetched:
        copy.wait()
    pl.semaphore_wait(barrier, len(peers))

    def link(source, target, sent, landed, device):
        pltpu.make_async_remote_copy(
            src_ref=source, dst_ref=target, send_sem=send.at[sent], recv_sem=recv.at[landed],
            device_id=device, device_id_type=MESH,
        ).start()

    def whole(ref, sent, landed):
        return pltpu.make_async_remote_copy(
            src_ref=ref, dst_ref=ref, send_sem=send.at[sent], recv_sem=recv.at[landed],
            device_id=mate, device_id_type=MESH,
        )

    def wait_landed(ref, landed):
        whole(ref, 0, landed).wait_recv()

    def wait_sent(ref, sent):
        whole(ref, sent, 0).wait_send()

    every, halves = pl.ds(0, 4), (pl.ds(0, 2), pl.ds(2, 2))
    for turn, blocks in enumerate(halves):
        for index, (axis, piece, size) in enumerate(parts):
            half = size // 2
            opposite = (spot[axis] + 2) % 4
            for way in range(2):
                link(
                    piece(opposite, blocks, way * half, half), vias[index].at[way, blocks],
                    index, 2 * index + turn, along(axis, 1 + 2 * way),
                )
    for index, (axis, piece, size) in enumerate(parts):
        half = size // 2
        up, down = (spot[axis] + 1) % 4, (spot[axis] + 3) % 4
        link(piece(up, every, half, half), gots[index].at[0, :, pl.ds(half, half)], index, 6 + index, along(axis, 1))
        link(piece(down, every, 0, half), gots[index].at[1, :, pl.ds(0, half)], index, 6 + index, along(axis, 3))
    link(state_ref, other_ref, 14, 17, mate)
    for turn, blocks in enumerate(halves):
        for index, (axis, piece, size) in enumerate(parts):
            half = size // 2
            wait_landed(vias[index].at[:, blocks], 2 * index + turn)
            for way in range(2):
                own = piece((spot[axis] + 1 + 2 * way) % 4, every, way * half, half)
                for block in (2 * turn, 2 * turn + 1):
                    passes[index][way, block] = (
                        own[block].astype(jnp.float32) + vias[index][way, block].astype(jnp.float32)
                    ).astype(jnp.bfloat16)
                link(
                    passes[index].at[way, blocks], gots[index].at[way, blocks, pl.ds(way * half, half)],
                    3 + index, 6 + index, along(axis, 1 + 2 * way),
                )

    def arrive(index):
        wait_landed(gots[index], 6 + index)

    def add_up(index, block):
        axis, piece, size = parts[index]
        value = piece(spot[axis], every, 0, size)[block].astype(jnp.float32)
        for way in range(2):
            value = value + gots[index][way, block].astype(jnp.float32)
        return value

    def stage(index, axis, source, target):
        for turn in (2, 1, 3):
            place = (spot[axis] + turn) % 4
            link(source.at[place], target.at[turn - 1], 6 + index, 9 + index, along(axis, turn))

    def add_last(own, got):
        value = own.astype(jnp.float32)
        for turn in range(3):
            value = value + got[turn].astype(jnp.float32)
        return value

    arrive(0)
    for block in range(4):
        next_a[block] = add_up(0, block).astype(jnp.bfloat16)
    stage(0, 1, next_a, got_a2)
    arrive(1)
    for block, value in enumerate(block_swap([add_up(1, block) for block in range(4)])):
        next_b[block] = value.astype(jnp.bfloat16)
    stage(1, 2, next_b, got_b2)
    arrive(2)
    for block in range(4):
        next_c[block] = add_up(2, block).astype(jnp.bfloat16)
    stage(2, 0, next_c, got_c2)

    def fold(value, target):
        size = value.shape[0] // 8
        folded[0:value.shape[0], :] = value
        pieces = [folded[i * size:(i + 1) * size, :] for i in range(8)]
        for index, part in enumerate(block_swap(pieces)):
            target[index] = part

    def third(index, axis, source, target):
        for turn in (2, 1, 3, 0):
            place = (spot[axis] + turn) % 4
            for core in (1 - mem,) if turn == 0 else (mem, 1 - mem):
                link(
                    source.at[place * 2 + core], target.at[mem * 4 + turn], 9 + index, 12 + index,
                    along(axis, turn, core),
                )
        target[mem * 4] = source[spot[axis] * 2 + mem]

    def sum_third(index, source, target, row):
        wait_landed(target.at[pl.ds(0, 7)], 12 + index)
        size = source.shape[1]
        for core in range(2):
            value = target[core * 4]
            for turn in range(1, 4):
                value = value + target[core * 4 + turn]
            summed[core * 56 + row:core * 56 + row + size, :] = value

    wait_landed(got_a2, 9)
    fold(add_last(next_a[y], got_a2), last_a)
    third(0, 2, last_a, got_a3)
    wait_landed(got_b2, 10)
    fold(add_last(next_b[z], got_b2), last_b)
    third(1, 0, last_b, got_b3)
    wait_landed(got_c2, 11)
    fold(add_last(next_c[x], got_c2), last_c)
    third(2, 1, last_c, got_c3)
    sum_third(0, last_a, got_a3, 0)
    sum_third(1, last_b, got_b3, 20)
    sum_third(2, last_c, got_c3, 40)

    for copy in tables:
        copy.wait()
    coarse_points(summed[...], pick, eighth, lane_ref, picked, spread_rows, rows)

    after = sixths((16, 128))
    for core in range(2):
        for side in range(2):
            point = 15 * (1 - side)
            value = rows[core, pl.ds(point * 40, 16, stride=6), :]
            for p in range(1, 6):
                value = jnp.where(after[p], rows[core, pl.ds(point * 40 + p, 16, stride=6), :], value)
            columns[core, side] = value
    outer = jnp.where(mem == 1, 0, 2)
    for index, (straight, slanted) in enumerate(around):
        side, core = index // 2, index % 2
        for device, turn in ((straight, 1), (slanted, outer)):
            slot = (side * 3 + turn) * 2 + mem
            link(columns.at[core, side], corners.at[pl.ds(slot * 16, 16)], 12, 15, device)
    for core in range(2):
        edges[core] = gather_members(rows.at[core]).astype(jnp.bfloat16)
    link(edges.at[1 - mem], halo.at[mem], 13, 16, mate)
    for other in range(2):
        core = 1 - mem if other else mem
        link(edges.at[core], halo.at[3 - mem], 13, 16, ((x + ahead + 4) % 4, ty, core))
    points_ref[pl.ds(pl.multiple_of(mem * 16, 16), 16), :] = edges[mem]

    wait_landed(corners.at[pl.ds(0, 128)], 15)
    for q in range(7):
        points_ref[64:80, q * 128:q * 128 + 128] = corners[pl.ds(q, 16, stride=16), :].astype(jnp.bfloat16)
    wait_landed(halo.at[pl.ds(0, 3)], 16)
    points_ref[pl.ds(pl.multiple_of((1 - mem) * 16, 16), 16), :] = halo[1 - mem]
    for slot in (2, 3):
        points_ref[slot * 16:slot * 16 + 16, :] = halo[slot]
    for index in range(3):
        wait_sent(gots[index], index)
        wait_sent(passes[index], 3 + index)
        wait_sent((got_a2, got_b2, got_c2)[index], 6 + index)
        wait_sent((got_a3, got_b3, got_c3)[index].at[pl.ds(0, 7)], 9 + index)
    wait_sent(corners.at[pl.ds(0, 128)], 12)
    wait_sent(halo.at[pl.ds(0, 3)], 13)
    whole(other_ref, 14, 17).wait()


def coarse(partial_ab, partial_c, state):
    pick, eighth = pick_tables()
    bf16, f32 = jnp.bfloat16, jnp.float32
    sizes = (PART_A, PART_B, PART_C)
    hbm, vmem = pl.BlockSpec(memory_space=pl.ANY), pl.BlockSpec(memory_space=pltpu.VMEM)
    return pl.pallas_call(
        coarse_kernel,
        out_shape=(
            jax.ShapeDtypeStruct((80, LINK_LANES), bf16),
            jax.ShapeDtypeStruct(state.shape, state.dtype),
        ),
        in_specs=[hbm] * 6,
        out_specs=(vmem, hbm),
        scratch_shapes=[pltpu.VMEM((4, 4, PART_A + PART_B, 128), bf16), pltpu.VMEM((4, 4, PART_C, 128), bf16)]
        + [pltpu.VMEM((2, 4, size // 2, 128), bf16) for size in sizes]
        + [pltpu.VMEM((2, 4, size // 2, 128), bf16) for size in sizes]
        + [pltpu.VMEM((2, 4, size, 128), bf16) for size in sizes]
        + [pltpu.VMEM((4, size, 128), bf16) for size in sizes]
        + [pltpu.VMEM((3, size, 128), bf16) for size in sizes]
        + [pltpu.VMEM((8, size // 8, 128), f32) for size in sizes]
        + [pltpu.VMEM((8, size // 8, 128), f32) for size in sizes]
        + [
            pltpu.VMEM((PART_A, 128), f32),
            pltpu.VMEM((112, 128), f32),
            pltpu.VMEM((1648, 128), bf16),
            pltpu.VMEM((1648, 128), bf16),
            pltpu.VMEM((8, WIDE), jnp.int32),
            pltpu.VMEM((1648, WIDE), bf16),
            pltpu.VMEM((1648, WIDE), f32),
            pltpu.VMEM((2, 1024, 128), f32),
            pltpu.VMEM((2, 16, LINK_LANES), bf16),
            pltpu.VMEM((2, 2, 16, 128), f32),
            pltpu.VMEM((4, 16, LINK_LANES), bf16),
            pltpu.VMEM((512, 128), f32),
            pltpu.SemaphoreType.DMA((15,)),
            pltpu.SemaphoreType.DMA((18,)),
            pltpu.SemaphoreType.DMA((5,)),
        ],
        compiler_params=pltpu.CompilerParams(
            collective_id=1, has_side_effects=True, vmem_limit_bytes=60 * 1024 * 1024
        ),
        name="coarse",
    )(partial_ab, partial_c, jnp.asarray(pick), jnp.asarray(eighth), jnp.asarray(lane_table()), state)


def tent(length, nodes):
    position = np.arange(length, dtype=np.float32)[:, None]
    centre = (np.arange(nodes, dtype=np.float32)[None, :] - 1.0) * B + (B - 1) * 0.5
    return np.maximum(0.0, 1.0 - np.abs(position - centre) / B)


def tent_tables():
    place_x, place_y = np.full(80, -1), np.full(80, -1)
    for i in range(2):
        for j in range(16):
            place_x[i * 16 + j], place_y[i * 16 + j] = i + 1, j + 1
            place_x[32 + i * 16 + j], place_y[32 + i * 16 + j] = 3 * i, j + 1
    for side in range(2):
        for turn in range(3):
            for i in range(2):
                row = 64 + (side * 3 + turn) * 2 + i
                place_y[row] = 17 * side
                place_x[row] = {1: i + 1, 0: 0 if i == 1 else -1, 2: 3 if i == 0 else -1}[turn]
    tables = []
    for length, nodes, place in ((16, 4, place_x), (128, 18, place_y)):
        table = np.zeros((3, 80, length), np.float32)
        for kind in range(3):
            weights = tent(length, nodes)
            if kind == 0:
                weights[:, 1] += weights[:, 0]
                weights[:, 0] = 0
            if kind == 2:
                weights[:, -2] += weights[:, -1]
                weights[:, -1] = 0
            for row in range(80):
                if place[row] >= 0:
                    table[kind, row] = weights[:, place[row]]
        tables.append(table)
    return tables


def per_device(volume, super_matrix, observed, error_var, obs_cells, counts, state):
    other_volume = swap(volume[0])
    partial_ab, partial_c = gram(counts, volume[0], other_volume, super_matrix[0], observed, error_var, obs_cells)
    points, other_state = coarse(partial_ab, partial_c, state)
    tent_x, tent_y = tent_tables()
    return apply(points, jnp.asarray(tent_x), jnp.asarray(tent_y), state, other_state)


def solution(mesh):
    placed = (
        P(("tx", "ty"), "mem", None, None),
        P(("tx", "ty"), None, None, None),
        P(("tx", "ty"), None),
        P(("tx", "ty"), None),
        P(("tx", "ty"), None),
        P(("tx", "ty"), None),
        P("mem", None, "tx", "ty"),
    )
    return jax.shard_map(
        per_device,
        mesh=mesh,
        in_specs=placed,
        out_specs=P("mem", None, "tx", "ty"),
        check_vma=False,
    )
```
